32 devices in a mesh: tensor: 4 (over z), inner: 4 (over x, core), outer: 2 (over y).
Axes of the slice: x: 2, y: 2, z: 4, core: 2. Of those that a mesh axis runs over, the one named last changes fastest.
Arguments:
- tokens: bfloat16 [64, 261, 768], P(('inner', 'outer')), may hold values from -6 to 6
- patch_mask: int32 [64, 256], P(('inner', 'outer')), may hold values from 0 to 1, as said below
- cotangent: bfloat16 [64, 261, 768], P(('inner', 'outer')), may hold values from -6 to 6
- mask_token: float32 [768], replicated, may hold values from -5 to 5
- pos_embed: float32 [261, 768], replicated, may hold values from -2.5 to 2.5
- pre_attn_gain: float32 [768], replicated, may hold values from 0.25 to 1.75
- pre_attn_bias: float32 [768], replicated, may hold values from -1.5 to 1.5
- qkv_weight: bfloat16 [768, 3, 768], P(None, None, 'tensor'), may hold values from -0.21875 to 0.21875
- qv_bias: float32 [2, 768], P(None, 'tensor'), may hold values from -2.5 to 2.5
- proj_weight: bfloat16 [768, 768], P('tensor'), may hold values from -0.875 to 0.875
- proj_bias: float32 [768], replicated, may hold values from -1.5 to 1.5
- attn_scale: float32 [768], replicated, may hold values from 0.5 to 1.5
- pre_mlp_gain: float32 [768], replicated, may hold values from 0.25 to 1.75
- pre_mlp_bias: float32 [768], replicated, may hold values from -1.5 to 1.5
- fc1_weight: bfloat16 [768, 3072], P(None, 'tensor'), may hold values from -0.21875 to 0.21875
- fc1_bias: float32 [3072], P('tensor'), may hold values from -2.5 to 2.5
- fc2_weight: bfloat16 [3072, 768], P('tensor'), may hold values from -0.21875 to 0.21875
- fc2_bias: float32 [768], replicated, may hold values from -1.5 to 1.5
- mlp_scale: float32 [768], replicated, may hold values from 0.5 to 1.5
Outputs:
- result: bfloat16 [64, 261, 768], P(('inner', 'outer'))
- grad_tokens: float32 [64, 261, 768], P(('inner', 'outer'))
- grad_mask_token: float32 [768], P('inner')
- grad_pos_embed: float32 [261, 768], P(None, 'inner')
- grad_pre_attn_gain: float32 [768], P('inner')
- grad_pre_attn_bias: float32 [768], P('inner')
- grad_qkv_weight: float32 [768, 3, 768], P('inner', None, 'tensor')
- grad_qv_bias: float32 [2, 768], P(None, ('tensor', 'inner'))
- grad_proj_weight: float32 [768, 768], P('tensor', 'inner')
- grad_proj_bias: float32 [768], P('inner')
- grad_attn_scale: float32 [768], P('inner')
- grad_pre_mlp_gain: float32 [768], P('inner')
- grad_pre_mlp_bias: float32 [768], P('inner')
- grad_fc1_weight: float32 [768, 3072], P('inner', 'tensor')
- grad_fc1_bias: float32 [3072], P(('tensor', 'inner'))
- grad_fc2_weight: float32 [3072, 768], P('tensor', 'inner')
- grad_fc2_bias: float32 [768], P('inner')
- grad_mlp_scale: float32 [768], P('inner')
The draws below stay inside these ranges and needn't reach their ends.
Inputs may be any that keep to these rules, and one draw needn't show every extreme that they name: `patch_mask`: in each crop the ones form one axis-aligned rectangle of the row-major 16 x 16 patch grid, covering at most half of its patches.
All inputs are finite; a program needn't handle non-finite values.
Results may differ from the reference program's by a relative error of at most 0.012.
The reference program's roundings to bfloat16 on the way count: a program that leaves them out, or rounds other values in their place, can miss the bound.
Values sent between devices are 32-bit elements; how exact they have to be, the bound alone decides.
No kernel may reach another device: no remote copies, remote signals or barrier semaphores. Data moves between devices by JAX's collectives and lax.ppermute only.
A program may use at most 192 MiB of HBM per device.

```python
import jax
import jax.numpy as jnp
from jax import lax

D = 768
HEADS = 12
HEAD_DIM = 64
FF = 3072
GRID = 16
PREFIX = 5
CROPS_DEV = 8
SEQ = 261
CROPS = 64


def draw_patch_mask(key, part):
    key = jax.random.fold_in(key, 7)
    key_high, key_wide, key_row, key_col = jax.random.split(key, 4)
    height = jax.random.randint(key_high, (CROPS,), GRID // 4, GRID // 2 + 1)
    breadth = jax.random.randint(key_wide, (CROPS,), (7 * GRID + 15) // 16, GRID + 1)
    top_row = jax.random.randint(key_row, (CROPS,), 0, GRID - height + 1)
    left_col = jax.random.randint(key_col, (CROPS,), 0, GRID - breadth + 1)
    places = jnp.arange(GRID)
    inside_rows = (places[None, :] >= top_row[:, None]) & (places[None, :] < (top_row + height)[:, None])
    inside_cols = (places[None, :] >= left_col[:, None]) & (places[None, :] < (left_col + breadth)[:, None])
    cells = inside_rows[:, :, None] & inside_cols[:, None, :]
    return cells.reshape(CROPS, GRID * GRID).astype(jnp.int32)


def raised(drawn, own_key, source, target, shards_of, factor):
    owner, partner = [(jnp.arange(drawn.shape[position]) // (drawn.shape[position] // shards_of)).reshape([-1 if axis == position else 1 for axis in range(drawn.ndim)]) for position in (source, target)]
    chosen = jax.random.permutation(own_key, shards_of)[partner]
    strong = (owner == chosen) | (owner == (partner + shards_of // 2) % shards_of)
    return jnp.where(strong, factor * drawn, drawn)


def levels(rng, extent, shards, least, largest):
    def one(dim, parts):
        heights = jax.random.uniform(jax.random.fold_in(jax.random.fold_in(rng, 6), dim), (parts,), jnp.float32, least / len(shards), largest / len(shards))
        return jnp.repeat(jnp.exp(heights), extent[dim] // parts).reshape((-1,) + (1,) * (len(extent) - dim - 1))

    loudness = one(*shards[0])
    for cut in shards[1:]:
        loudness = loudness * one(*cut)
    return loudness


def bell_draw(rng, dims, scale, limit, cuts=(), held_as=jnp.bfloat16):
    values = scale * jax.random.normal(rng, dims, jnp.float32)
    if cuts:
        values = values * levels(rng, dims, cuts, -0.22, 0.18)
    return jnp.clip(values, -limit, limit).astype(held_as)


def gaussian_with(own_key, shape, scale, most, cuts, heavy, held_as=jnp.bfloat16):
    result = scale * jax.random.normal(own_key, shape, jnp.float32)
    if cuts:
        result = result * levels(own_key, shape, cuts, -0.22, 0.18)
    return jnp.clip(raised(result, jax.random.fold_in(own_key, 3), *heavy), -most, most).astype(held_as)


def setup_inputs(seed: int = 0) -> dict:
    key_list = jax.random.split(jax.random.key(seed), 20)
    return {
        "tokens": bell_draw(key_list[0], (CROPS, SEQ, D), 1.0, 6.0, ((0, 8),)),
        "patch_mask": draw_patch_mask(jax.random.fold_in(key_list[19], 71), 0),
        "cotangent": gaussian_with(key_list[2], (CROPS, SEQ, D), 1.0, 6.0, ((0, 8),), (0, 2, 8, 2.0)),
        "mask_token": bell_draw(key_list[3], (D,), 1.0, 5.0, (), jnp.float32),
        "pos_embed": bell_draw(key_list[4], (SEQ, D), 0.5, 2.5, (), jnp.float32),
        "pre_attn_gain": jnp.clip(1.0 + 0.15 * jax.random.normal(key_list[5], (D,), jnp.float32), 0.25, 1.75),
        "pre_attn_bias": bell_draw(key_list[6], (D,), 0.3, 1.5, (), jnp.float32),
        "qkv_weight": bell_draw(key_list[7], (D, 3, D), D ** -0.5, 0.21875, ((2, 4),)),
        "qv_bias": bell_draw(key_list[8], (2, D), 0.5, 2.5, ((1, 4),), jnp.float32),
        "proj_weight": bell_draw(key_list[9], (D, D), (D // 16) ** -0.5, 0.875, ((0, 4),)),
        "proj_bias": bell_draw(key_list[10], (D,), 0.3, 1.5, (), jnp.float32),
        "attn_scale": jnp.clip(jax.random.uniform(key_list[11], (D,), jnp.float32, 0.5, 1.5), 0.5, 1.5),
        "pre_mlp_gain": jnp.clip(1.0 + 0.15 * jax.random.normal(key_list[12], (D,), jnp.float32), 0.25, 1.75),
        "pre_mlp_bias": bell_draw(key_list[13], (D,), 0.3, 1.5, (), jnp.float32),
        "fc1_weight": bell_draw(key_list[14], (D, FF), D ** -0.5, 0.21875, ((1, 4),)),
        "fc1_bias": bell_draw(key_list[15], (FF,), 0.5, 2.5, ((0, 4),), jnp.float32),
        "fc2_weight": bell_draw(key_list[16], (FF, D), (FF // 4) ** -0.5, 0.21875, ((0, 4),)),
        "fc2_bias": bell_draw(key_list[17], (D,), 0.3, 1.5, (), jnp.float32),
        "mlp_scale": jnp.clip(jax.random.uniform(key_list[18], (D,), jnp.float32, 0.5, 1.5), 0.5, 1.5),
    }


@jax.custom_vjp
def low(v):
    return lax.optimization_barrier(v.astype(jnp.bfloat16)).astype(jnp.float32)

@jax.custom_vjp
def low_back(v):
    return v

def low_keep(v):
    return (low(v), None)

def low_pass(kept, grad):
    return (grad,)

def back_keep(v):
    return (v, None)

def back_low(kept, grad):
    return (low(grad),)
low.defvjp(low_keep, low_pass)
low_back.defvjp(back_keep, back_low)
EPS = 1e-06
HIGH = lax.Precision.HIGHEST

def layer_norm(field, gain_vec, bias_vec):
    center = field - lax.optimization_barrier(jnp.mean(field, -1, keepdims=True))
    spread = lax.optimization_barrier(jnp.mean(center * center, -1, keepdims=True))
    return center * lax.rsqrt(spread + EPS) * gain_vec + bias_vec

def forward(params, tokens_in, flagged):
    mask_token, pos_embed, pre_attn_gain, pre_attn_bias, qkv_weight, qv_bias, proj_weight, proj_bias, attn_scale, pre_mlp_gain, pre_mlp_bias, fc1_weight, fc1_bias, fc2_weight, fc2_bias, mlp_scale = params
    crop_count = tokens_in.shape[0]
    begin = jnp.where(flagged, mask_token, tokens_in) + pos_embed
    normed = low(layer_norm(begin, pre_attn_gain, pre_attn_bias))
    bias_rows = jnp.stack([qv_bias[0], jnp.zeros_like(qv_bias[0]), qv_bias[1]])
    mixed = low(low_back(jnp.einsum('csd,dtj->cstj', normed, qkv_weight, precision=HIGH)) + bias_rows)
    split_heads = mixed.reshape(crop_count, SEQ, 3, HEADS, HEAD_DIM)
    factor = HEAD_DIM ** (-0.5)
    scores = low_back(jnp.einsum('cqhe,ckhe->chqk', split_heads[:, :, 0], split_heads[:, :, 1], precision=HIGH) * factor)
    shifted = jnp.exp(scores - lax.optimization_barrier(jnp.max(scores, -1, keepdims=True)))
    weights = low(shifted / lax.optimization_barrier(jnp.sum(shifted, -1, keepdims=True)))
    attended = jnp.einsum('chqk,ckhe->cqhe', weights, split_heads[:, :, 2], precision=HIGH).reshape(crop_count, SEQ, D)
    attended = low(low_back(attended))
    branch = low_back(jnp.einsum('csj,jd->csd', attended, proj_weight, precision=HIGH)) + proj_bias
    middle = begin + attn_scale * branch
    normed_mlp = low(layer_norm(middle, pre_mlp_gain, pre_mlp_bias))
    hidden = low_back(jnp.einsum('csd,df->csf', normed_mlp, fc1_weight, precision=HIGH)) + fc1_bias
    activated = low(jax.nn.gelu(hidden, approximate=False))
    output = low_back(jnp.einsum('csf,fd->csd', activated, fc2_weight, precision=HIGH)) + fc2_bias
    return middle + mlp_scale * output

def reference(tokens, patch_mask, cotangent, mask_token, pos_embed, pre_attn_gain, pre_attn_bias, qkv_weight, qv_bias, proj_weight, proj_bias, attn_scale, pre_mlp_gain, pre_mlp_bias, fc1_weight, fc1_bias, fc2_weight, fc2_bias, mlp_scale):
    params = tuple((entry.astype(jnp.float32) for entry in (mask_token, pos_embed, pre_attn_gain, pre_attn_bias, qkv_weight, qv_bias, proj_weight, proj_bias, attn_scale, pre_mlp_gain, pre_mlp_bias, fc1_weight, fc1_bias, fc2_weight, fc2_bias, mlp_scale)))
    groups = CROPS // CROPS_DEV
    flag_all = (jnp.concatenate([jnp.zeros((CROPS, PREFIX), jnp.int32), patch_mask], 1) == 1)[:, :, None]
    flag_groups = flag_all.reshape(groups, CROPS_DEV, SEQ, 1)
    token_groups = tokens.astype(jnp.float32).reshape(groups, CROPS_DEV, SEQ, D)
    cot_groups = cotangent.astype(jnp.float32).reshape(groups, CROPS_DEV, SEQ, D)

    def one_group(totals, pieces):
        token_piece, flag_piece, cot_piece = pieces
        outcome, pullback = jax.vjp(lambda weights_in, inputs_in: forward(weights_in, inputs_in, flag_piece), params, token_piece)
        grad_params, grad_inputs = pullback(cot_piece)
        totals = jax.tree.map(lambda accum, fresh: accum + fresh, totals, grad_params)
        return (totals, (outcome.astype(jnp.bfloat16), grad_inputs))
    zeros = jax.tree.map(jnp.zeros_like, params)
    totals, (outcomes, grad_inputs) = lax.scan(one_group, zeros, (token_groups, flag_groups, cot_groups))
    return (outcomes.reshape(CROPS, SEQ, D), grad_inputs.reshape(CROPS, SEQ, D), totals[0], totals[1], totals[2], totals[3], totals[4], totals[5], totals[6], totals[7], totals[8], totals[9], totals[10], totals[11], totals[12], totals[13], totals[14], totals[15])
```

```python
import functools

import jax
import jax.numpy as jnp
from jax import lax
from jax.experimental import pallas as pl
from jax.experimental.pallas import tpu as pltpu
from jax.sharding import PartitionSpec as P

HEAD_DIM = 64
EPS = 1e-06
F32 = jnp.float32
BF16 = jnp.bfloat16
NEG = -1e30
LANES = 128
WIDE = 256
MAIN = 256
VMEM_LIMIT = 56 * 1024 * 1024
PLANE = ("inner", "outer")


def mm_nt(a, b):
    return lax.dot_general(a, b, (((1,), (1,)), ((), ())), preferred_element_type=F32)


def mm_nn(a, b):
    return lax.dot_general(a, b, (((1,), (0,)), ((), ())), preferred_element_type=F32)


def mm_tn(a, b):
    return lax.dot_general(a, b, (((0,), (0,)), ((), ())), preferred_element_type=F32)


def params():
    return pltpu.CompilerParams(vmem_limit_bytes=VMEM_LIMIT)


def block(shape):
    return pl.BlockSpec((1,) + tuple(shape[1:]), lambda c: (c,) + (0,) * (len(shape) - 1))


def whole(shape):
    return pl.BlockSpec(tuple(shape), lambda c: (0,) * len(shape))


def row_sum(x):
    return jnp.sum(x, 0, keepdims=True)


def norm_parts(v):
    center = v - jnp.mean(v, -1, keepdims=True)
    rstd = lax.rsqrt(jnp.mean(center * center, -1, keepdims=True) + EPS)
    return center * rstd, rstd


def norm_back(xhat, rstd, u, gain):
    gu = u * gain
    return (
        gu - jnp.mean(gu, -1, keepdims=True) - xhat * jnp.mean(gu * xhat, -1, keepdims=True)
    ) * rstd


def put_columns(ref, rows, x):
    for j in range(ref.shape[0]):
        ref[j, rows, :] = x[:, j * LANES : (j + 1) * LANES]


def get_columns(ref, rows):
    return jnp.concatenate([ref[j, rows, :] for j in range(ref.shape[0])], 1)


def enter_kernel(tok_ref, cot_ref, flag_ref, vec_ref, pos_ref, begin_ref, n1_ref, up_ref, tok_s, cot_s):
    seq, crops, _ = tok_ref.shape
    rows = pos_ref.shape[0]
    step = 29 if seq % 29 == 0 else 1

    @pl.when(pl.program_id(0) == 0)
    def _():
        def move(i, carry):
            part = pl.ds(i * step, step)
            dst = pl.ds(pl.multiple_of(i * (step * crops), crops), step * crops)
            for src, out in ((tok_ref, tok_s), (cot_ref, cot_s)):
                put_columns(out, dst, src[part].astype(F32).reshape(step * crops, -1))
            return carry

        lax.fori_loop(0, seq // step, move, 0)
        for out in (tok_s, cot_s):
            out[:, seq * crops :, :] = jnp.zeros_like(out[:, seq * crops :, :])

    mine = pl.ds(pl.program_id(0), rows, stride=crops)
    flagged = flag_ref[0][:, 0:1] > 0.5
    begin = jnp.where(flagged, vec_ref[0:1, :], get_columns(tok_s, mine)) + pos_ref[...]
    begin_ref[0] = begin
    xhat, _ = norm_parts(begin)
    n1_ref[0] = (xhat * vec_ref[1:2, :] + vec_ref[2:3, :]).astype(BF16)
    up_ref[0] = get_columns(cot_s, mine).astype(BF16)


def enter(tok, cot, flags, vecs, pos):
    seq, crops, width = tok.shape
    rows = pos.shape[0]
    shape = (crops, rows, width)
    return pl.pallas_call(
        enter_kernel,
        grid=(crops,),
        in_specs=[whole(tok.shape), whole(cot.shape), block(flags.shape), whole(vecs.shape), whole(pos.shape)],
        out_specs=[block(shape)] * 3,
        out_shape=[
            jax.ShapeDtypeStruct(shape, F32),
            jax.ShapeDtypeStruct(shape, BF16),
            jax.ShapeDtypeStruct(shape, BF16),
        ],
        scratch_shapes=[pltpu.VMEM((width // LANES, rows * crops, LANES), F32)] * 2,
        compiler_params=params(),
        name="enter",
    )(tok, cot, flags, vecs, pos)


def head_masks(heads):
    lane = lax.broadcasted_iota(jnp.int32, (1, WIDE), 1)
    return [((lane // HEAD_DIM) == h).astype(F32) for h in range(heads)], lane


def per_head_rows(x, masks):
    parts = [x * m for m in masks]
    parts.append(jnp.zeros((LANES - 8 * len(masks), x.shape[1]), F32))
    return jnp.concatenate(parts, 0).astype(BF16)


def pick(index, parts):
    out = parts[-1]
    for h in range(len(parts) - 2, -1, -1):
        out = jnp.where(index == h, parts[h], out)
    return out


def attention_forward(n1, w_ref, bias, heads, tail_valid):
    masks, lane = head_masks(heads)
    low = [m.astype(BF16) for m in masks]
    head_width = heads * HEAD_DIM
    mixed = (mm_nt(n1, w_ref[0 : 3 * WIDE, :]) + bias).astype(BF16)
    q = mixed[:, 0:WIDE] * jnp.asarray(HEAD_DIM**-0.5, BF16)
    k, v = mixed[:, WIDE : 2 * WIDE], mixed[:, 2 * WIDE : 3 * WIDE]
    mixed = jnp.concatenate([q, k, v], 1)
    k_main, v_main = k[0:MAIN], v[0:MAIN]
    v_masks = [m + (lane == head_width + h).astype(F32) for h, m in enumerate(masks)]
    k_tail = per_head_rows(k[MAIN : MAIN + 8].astype(F32), masks)
    v_tail = per_head_rows(v[MAIN : MAIN + 8].astype(F32), v_masks)
    col = lax.broadcasted_iota(jnp.int32, (1, LANES), 1)
    valid = (col < 8 * heads) & ((col % 8) < tail_valid)
    s_tail = jnp.where(valid, mm_nt(q, k_tail), NEG)
    tops, total = [], None
    for h in range(heads):
        s = mm_nt(q * low[h], k_main)
        top = jnp.where((col // 8) == h, s_tail, NEG)
        for i in range(MAIN // LANES):
            top = jnp.maximum(top, s[:, i * LANES : (i + 1) * LANES])
        top = jnp.max(top, -1, keepdims=True)
        tops.append(top)
        part = mm_nn(jnp.exp(s - top).astype(BF16), v_main * v_masks[h].astype(BF16))
        total = part if total is None else total + part
    e_tail = jnp.exp(s_tail - pick(col // 8, tops)).astype(BF16)
    total = total + mm_nn(e_tail, v_tail)
    sums = [total[:, head_width + h : head_width + h + 1] for h in range(heads)]
    scale = pick(lane // HEAD_DIM, [1.0 / s for s in sums])
    attended = (total * scale).astype(BF16)
    log_total = pick(col, [t + jnp.log(s) for t, s in zip(tops, sums)])
    branch = mm_nn(attended, w_ref[3 * WIDE : 4 * WIDE, :])
    return mixed, log_total, attended, branch


def place_pieces(info_ref, pieces, out_ref, base, first):
    p, core = info_ref[0], info_ref[1]
    own, along, far, peer_a, peer_b = pieces
    q = p ^ 2
    a_bit = jnp.where(core == 0, 4, 1)
    b_bit = 5 - a_bit
    spots = (
        (own, None, p),
        (along, None, p ^ a_bit),
        (far, 0, p ^ b_bit),
        (far, 1, p ^ 5),
        (peer_a, 0, q),
        (peer_a, 1, q ^ b_bit),
        (peer_b, 0, q ^ a_bit),
        (peer_b, 1, q ^ 5),
    )
    size = out_ref.shape[0]
    for ref, slot, ident in spots:
        view = ref if slot is None else ref.at[slot]
        rows = 96
        dst = pl.multiple_of(first(ident), 32)
        out_ref[pl.ds(dst, rows), :] = view[base : base + rows, :].astype(BF16)


def attn_kernel(*refs, heads, tail_valid, gathered, accs, finish):
    it = iter(refs)
    if gathered:
        info = next(it)
    n1_ref, bias_ref = next(it), next(it)
    if gathered:
        pieces = [next(it) for _ in range(5)]
    else:
        w_ref = next(it)
    acc_refs = [next(it) for _ in range(accs)]
    if finish:
        begin_ref, vec_ref = next(it), next(it)
    br_ref, mix_ref, lse_ref = next(it), next(it), next(it)
    if gathered:
        w_ref = next(it)

        @pl.when(pl.program_id(0) == 0)
        def _():
            for i in range(4):
                w_ref[i * WIDE + 192 : (i + 1) * WIDE, :] = jnp.zeros((WIDE - 192, w_ref.shape[1]), BF16)
            place_pieces(info, pieces, w_ref, 0, lambda i: (i >> 1) * WIDE + (i & 1) * 96)

    if not gathered:
        att_ref = next(it)
    mixed, log_total, attended, branch = attention_forward(
        n1_ref[0], w_ref, bias_ref[...], heads, tail_valid
    )
    mix_ref[0] = mixed
    lse_ref[0] = log_total
    if not gathered:
        att_ref[0] = attended
    for ref in acc_refs:
        branch = branch + ref[0]
    br_ref[0] = branch
    if finish:
        n2_ref = next(it)
        middle = begin_ref[0] + vec_ref[0:1, :] * (branch + vec_ref[1:2, :])
        xhat, _ = norm_parts(middle)
        n2_ref[0] = (xhat * vec_ref[2:3, :] + vec_ref[3:4, :]).astype(BF16)


def attn(n1, bias, weights, info, accs, heads, tail_valid, finish=None):
    crops, rows, width = n1.shape
    gathered = info is not None
    args, specs = [], []

    def add(x, spec):
        args.append(x)
        specs.append(spec)

    if gathered:
        add(info, pl.BlockSpec(memory_space=pltpu.SMEM))
    add(n1, block(n1.shape))
    add(bias, whole(bias.shape))
    for w in weights:
        add(w, whole(w.shape))
    for a in accs:
        add(a, block(a.shape))
    if finish is not None:
        add(finish[0], block(finish[0].shape))
        add(finish[1], whole(finish[1].shape))
    outs = [
        ((crops, rows, width), F32, block),
        ((crops, rows, 3 * WIDE), BF16, block),
        ((crops, rows, LANES), F32, block),
    ]
    if gathered:
        outs.append(((4 * WIDE, width), BF16, whole))
    else:
        outs.append(((crops, rows, WIDE), BF16, block))
    if finish is not None:
        outs.append(((crops, rows, width), BF16, block))
    return pl.pallas_call(
        functools.partial(
            attn_kernel,
            heads=heads,
            tail_valid=tail_valid,
            gathered=gathered,
            accs=len(accs),
            finish=finish is not None,
        ),
        grid=(crops,),
        in_specs=specs,
        out_specs=[kind(shape) for shape, _, kind in outs],
        out_shape=[jax.ShapeDtypeStruct(shape, dtype) for shape, dtype, _ in outs],
        compiler_params=params(),
        name="attention",
    )(*args)


def attention_backward(gb, w_ref, mix_ref, lse_ref, heads, tail_valid):
    masks, lane = head_masks(heads)
    low = [m.astype(BF16) for m in masks]
    da = mm_nt(gb, w_ref[3 * WIDE : 4 * WIDE, :]).astype(BF16)
    q, k, v = (mix_ref[0, :, i * WIDE : (i + 1) * WIDE] for i in range(3))
    k_main, v_main = k[0:MAIN], v[0:MAIN]
    k_tail = per_head_rows(k[MAIN : MAIN + 8].astype(F32), masks)
    v_tail = per_head_rows(v[MAIN : MAIN + 8].astype(F32), masks)
    col = lax.broadcasted_iota(jnp.int32, (1, LANES), 1)
    valid = (col < 8 * heads) & ((col % 8) < tail_valid)
    lse = [lse_ref[0, :, h : h + 1] for h in range(heads)]
    p_tail = jnp.where(valid, jnp.exp(mm_nt(q, k_tail) - pick(col // 8, lse)), 0.0)
    dp_tail = mm_nt(da, v_tail)
    x_tail = p_tail * dp_tail
    dq = dk = dv = None
    deltas = []
    for h in range(heads):
        qh, dah = q * low[h], da * low[h]
        p = jnp.exp(mm_nt(qh, k_main) - lse[h])
        dp = mm_nt(dah, v_main)
        x = p * dp
        delta = jnp.where((col // 8) == h, x_tail, 0.0)
        for i in range(MAIN // LANES):
            delta = delta + x[:, i * LANES : (i + 1) * LANES]
        delta = jnp.sum(delta, -1, keepdims=True)
        deltas.append(delta)
        ds = (p * (dp - delta)).astype(BF16)
        one = mm_nn(ds, k_main * low[h])
        two = mm_tn(ds, qh)
        three = mm_tn(p.astype(BF16), dah)
        dq = one if dq is None else dq + one
        dk = two if dk is None else dk + two
        dv = three if dv is None else dv + three
    ds_tail = (p_tail * (dp_tail - pick(col // 8, deltas))).astype(BF16)
    dq = (dq + mm_nn(ds_tail, k_tail)) * (HEAD_DIM**-0.5)
    dk_tail = mm_tn(ds_tail, q)
    dv_tail = mm_tn(p_tail.astype(BF16), da)
    dk_tail = sum(dk_tail[8 * h : 8 * h + 8] * masks[h] for h in range(heads))
    dv_tail = sum(dv_tail[8 * h : 8 * h + 8] * masks[h] for h in range(heads))
    rest = jnp.zeros((gb.shape[0] - MAIN - 8, WIDE), F32)
    dk = jnp.concatenate([dk, dk_tail, rest], 0)
    dv = jnp.concatenate([dv, dv_tail, rest], 0)
    return dq, dk, dv


def attn_back_kernel(*refs, heads, tail_valid, own, accs, finish):
    it = iter(refs)
    gb_ref, w_ref, mix_ref, lse_ref = (next(it) for _ in range(4))
    acc_refs = [next(it) for _ in range(accs)]
    if finish:
        begin_ref, gmid_ref, flag_ref, vec_ref = (next(it) for _ in range(4))
    else:
        gn_ref = next(it)
    first = pl.program_id(0) == 0
    dq, dk, dv = attention_backward(gb_ref[0], w_ref, mix_ref, lse_ref, heads, tail_valid)
    gm = jnp.concatenate([dq, dk, dv], 1).astype(BF16)
    if own:
        gm_ref, sum_ref = next(it), next(it)
        gm_ref[0] = gm
        sums = jnp.concatenate([row_sum(dq), row_sum(dv), jnp.zeros((6, WIDE), F32)], 0)
        sum_ref[...] = jnp.where(first, sums, sum_ref[...] + sums)
    gn = mm_nn(gm, w_ref[0 : 3 * WIDE, :])
    for ref in acc_refs:
        gn = gn + ref[0]
    if not finish:
        gn_ref[0] = gn
        return
    gtok_ref, gpos_ref, sum_ref, gtok_s = (next(it) for _ in range(4))
    xhat, rstd = norm_parts(begin_ref[0])
    grad_begin = gmid_ref[0] + norm_back(xhat, rstd, gn, vec_ref[0:1, :])
    flagged = flag_ref[0][:, 0:1] > 0.5
    cleared = jnp.where(flagged, 0.0, grad_begin)
    seq = gtok_ref.shape[0] // 8
    put_columns(gtok_s, pl.ds(pl.program_id(0), cleared.shape[0], stride=8), cleared)
    sums = jnp.concatenate(
        [
            row_sum(gn * xhat),
            row_sum(gn),
            row_sum(grad_begin - cleared),
            jnp.zeros((5, gn.shape[1]), F32),
        ],
        0,
    )

    @pl.when(first)
    def _():
        sum_ref[...] = sums
        gpos_ref[...] = grad_begin

    @pl.when(jnp.logical_not(first))
    def _():
        sum_ref[...] += sums
        gpos_ref[...] += grad_begin

    @pl.when(pl.program_id(0) == pl.num_programs(0) - 1)
    def _():
        for j in range(gtok_s.shape[0]):
            gtok_ref[:, j * LANES : (j + 1) * LANES] = gtok_s[j, 0 : seq * 8, :]


def attn_back(gb, w, mixed, lse, accs, heads, tail_valid, own=False, finish=None, seq=None):
    crops, rows, width = gb.shape
    args = [gb, w, mixed, lse, *accs]
    specs = [block(gb.shape), whole(w.shape), block(mixed.shape), block(lse.shape)]
    specs += [block(a.shape) for a in accs]
    outs, scratch = [], []
    if finish is not None:
        begin, gmid, flags, vecs = finish
        args += [begin, gmid, flags, vecs]
        specs += [block(begin.shape), block(gmid.shape), block(flags.shape), whole(vecs.shape)]
        scratch.append(pltpu.VMEM((width // LANES, rows * crops, LANES), F32))
    else:
        outs.append(((crops, rows, width), F32, block))
    if own:
        outs += [((crops, rows, 3 * WIDE), BF16, block), ((8, WIDE), F32, whole)]
    if finish is not None:
        outs += [
            ((seq * crops, width), F32, whole),
            ((rows, width), F32, whole),
            ((8, width), F32, whole),
        ]
    return pl.pallas_call(
        functools.partial(
            attn_back_kernel,
            heads=heads,
            tail_valid=tail_valid,
            own=own,
            accs=len(accs),
            finish=finish is not None,
        ),
        grid=(crops,),
        in_specs=specs,
        out_specs=[kind(shape) for shape, _, kind in outs],
        out_shape=[jax.ShapeDtypeStruct(shape, dtype) for shape, dtype, _ in outs],
        scratch_shapes=scratch,
        compiler_params=params(),
        name="attention_back",
    )(*args)


def gelu_and_slope(h):
    phi = 0.5 * (1.0 + lax.erf(h * (2.0**-0.5)))
    bell = jnp.exp(-0.5 * h * h) * 0.3989422804014327
    return h * phi, phi + h * bell


def mlp_kernel(*refs, gathered, accs, own, finish):
    it = iter(refs)
    if gathered:
        info = next(it)
    n2_ref, up_ref, vec_ref, bias_ref = (next(it) for _ in range(4))
    if gathered:
        pieces = [next(it) for _ in range(5)]
    else:
        w1_ref, w2_ref = next(it), next(it)
    acc_refs = [(next(it), next(it)) for _ in range(accs)]
    if finish:
        begin_ref, br_ref = next(it), next(it)
        res_ref, gmid_ref, gb_ref, sum_ref = (next(it) for _ in range(4))
    else:
        out_ref, gn_ref = next(it), next(it)
    if own:
        a_ref, gh_ref, go_ref, hsum_ref = (next(it) for _ in range(4))
    first = pl.program_id(0) == 0
    if finish:
        res_s = next(it)
    if gathered:
        w1_ref, w2_ref = next(it), next(it)

        @pl.when(first)
        def _():
            place_pieces(info, pieces, w1_ref, 0, lambda i: i * 96)
            place_pieces(info, pieces, w2_ref, 96, lambda i: i * 96)

    up = up_ref[0].astype(F32)
    grad_output = up * vec_ref[0:1, :]
    go = grad_output.astype(BF16)
    n2 = n2_ref[0]
    a, slope = gelu_and_slope(mm_nt(n2, w1_ref[...]) + bias_ref[...])
    a = a.astype(BF16)
    gh = mm_nt(go, w2_ref[...]) * slope
    if own:
        a_ref[0] = a
        go_ref[0] = go
        sums = jnp.concatenate([row_sum(gh), jnp.zeros((7, gh.shape[1]), F32)], 0)
        hsum_ref[...] = jnp.where(first, sums, hsum_ref[...] + sums)
    gh = gh.astype(BF16)
    if own:
        gh_ref[0] = gh
    out = mm_nn(a, w2_ref[...])
    gn = mm_nn(gh, w1_ref[...])
    for o_ref, g_ref in acc_refs:
        out = out + o_ref[0]
        gn = gn + g_ref[0]
    if not finish:
        out_ref[0] = out
        gn_ref[0] = gn
        return
    mlp_scale, fc2_bias, attn_scale, proj_bias, gain = (vec_ref[i : i + 1, :] for i in range(5))
    out = out + fc2_bias
    branch = br_ref[0] + proj_bias
    middle = begin_ref[0] + attn_scale * branch
    result = middle + mlp_scale * out
    rows = result.shape[0]
    crops = 8
    put_columns(res_s, pl.ds(pl.program_id(0), rows, stride=crops), result)
    xhat, rstd = norm_parts(middle)
    gmid = up + norm_back(xhat, rstd, gn, gain)
    gmid_ref[0] = gmid
    gbr = gmid * attn_scale
    gb_ref[0] = gbr.astype(BF16)
    sums = jnp.concatenate(
        [
            row_sum(up * out),
            row_sum(grad_output),
            row_sum(gn * xhat),
            row_sum(gn),
            row_sum(gmid * branch),
            row_sum(gbr),
            jnp.zeros((2, gn.shape[1]), F32),
        ],
        0,
    )
    sum_ref[...] = jnp.where(first, sums, sum_ref[...] + sums)

    @pl.when(pl.program_id(0) == pl.num_programs(0) - 1)
    def _():
        seq = res_ref.shape[0]
        step = 29 if seq % 29 == 0 else 1

        def move(i, carry):
            src = pl.ds(pl.multiple_of(i * (step * crops), crops), step * crops)
            res_ref[pl.ds(i * step, step)] = get_columns(res_s, src).reshape(step, crops, -1).astype(BF16)
            return carry

        lax.fori_loop(0, seq // step, move, 0)


def mlp(n2, up, vecs, bias, weights, info, accs, own=False, finish=None, seq=None):
    crops, rows, width = n2.shape
    hidden = bias.shape[1]
    gathered = info is not None
    args, specs = [], []

    def add(x, spec):
        args.append(x)
        specs.append(spec)

    if gathered:
        add(info, pl.BlockSpec(memory_space=pltpu.SMEM))
    add(n2, block(n2.shape))
    add(up, block(up.shape))
    add(vecs, whole(vecs.shape))
    add(bias, whole(bias.shape))
    for w in weights:
        add(w, whole(w.shape))
    for pair in accs:
        for a in pair:
            add(a, block(a.shape))
    full = (crops, rows, width)
    scratch = []
    if finish is not None:
        add(finish[0], block(finish[0].shape))
        add(finish[1], block(finish[1].shape))
        outs = [
            ((seq, crops, width), BF16, whole),
            (full, F32, block),
            (full, BF16, block),
            ((8, width), F32, whole),
        ]
        scratch.append(pltpu.VMEM((width // LANES, rows * crops, LANES), F32))
    else:
        outs = [(full, F32, block), (full, F32, block)]
    if own:
        outs += [((crops, rows, hidden), BF16, block)] * 2 + [(full, BF16, block), ((8, hidden), F32, whole)]
    if gathered:
        scratch += [pltpu.VMEM((hidden, width), BF16)] * 2
    return pl.pallas_call(
        functools.partial(mlp_kernel, gathered=gathered, accs=len(accs), own=own, finish=finish is not None),
        grid=(crops,),
        in_specs=specs,
        out_specs=[kind(shape) for shape, _, kind in outs],
        out_shape=[jax.ShapeDtypeStruct(shape, dtype) for shape, dtype, _ in outs],
        scratch_shapes=scratch,
        compiler_params=params(),
        name="mlp",
    )(*args)


def weight_grad_kernel(x1_ref, y1_ref, x2_ref, y2_ref, o1_ref, o2_ref):
    o1_ref[...] = mm_tn(x1_ref[...], y1_ref[...])
    o2_ref[...] = mm_tn(x2_ref[...], y2_ref[...])


def weight_grads(x1, y1, x2, y2):
    rows, width = x1.shape
    col = pl.BlockSpec((rows, WIDE), lambda i: (0, i))

    def out(y):
        return pl.BlockSpec((WIDE, y.shape[1]), lambda i: (i, 0))

    return pl.pallas_call(
        weight_grad_kernel,
        grid=(width // WIDE,),
        in_specs=[col, whole(y1.shape), col, whole(y2.shape)],
        out_specs=[out(y1), out(y2)],
        out_shape=[jax.ShapeDtypeStruct((width, y.shape[1]), F32) for y in (y1, y2)],
        compiler_params=params(),
        name="weight_grads",
    )(x1, y1, x2, y2)


def plane_perm(inner, outer, move):
    pairs = []
    for i in range(inner):
        for o in range(outer):
            j, r = move(i, o)
            pairs.append((i * outer + o, j * outer + r))
    return pairs


def spread(piece, perms):
    one, two, three = perms
    along = lax.ppermute(piece, PLANE, one)
    both = jnp.stack([piece, along])
    far = lax.ppermute(both, PLANE, two)
    peer_a = lax.ppermute(both, PLANE, three)
    peer_b = lax.ppermute(far, PLANE, three)
    return [piece, along, far, peer_a, peer_b]


def reduce_inner(x):
    return lax.psum(lax.psum_scatter(x, "inner", scatter_dimension=0, tiled=True), "outer")


def per_device(
    sizes,
    tokens,
    patch_mask,
    cotangent,
    mask_token,
    pos_embed,
    pre_attn_gain,
    pre_attn_bias,
    qkv_weight,
    qv_bias,
    proj_weight,
    proj_bias,
    attn_scale,
    pre_mlp_gain,
    pre_mlp_bias,
    fc1_weight,
    fc1_bias,
    fc2_weight,
    fc2_bias,
    mlp_scale,
):
    tensor_n, inner_n, outer_n = sizes
    crops, seq, width = tokens.shape
    head_width = qkv_weight.shape[2]
    heads = head_width // HEAD_DIM
    hidden = fc1_weight.shape[1]
    rows = -(-seq // 16) * 16
    tail_valid = seq - MAIN
    t = lax.axis_index("tensor")
    inner = lax.axis_index("inner")
    outer = lax.axis_index("outer")
    place = inner * 2 + outer % 2
    info = jnp.stack([place, inner % 2]).astype(jnp.int32)

    qkv_rows = qkv_weight.transpose(1, 2, 0).reshape(3 * head_width, width)
    own_attn = jnp.concatenate([qkv_rows, proj_weight], 0)
    own_fc1 = fc1_weight.T
    part = width // 8

    def eighth(x):
        return lax.dynamic_slice_in_dim(x, place * part, part, 0).astype(F32)

    attn_piece = eighth(own_attn)
    mlp_piece = jnp.concatenate([eighth(own_fc1), eighth(fc2_weight)], 0)
    perms = (
        plane_perm(inner_n, outer_n, lambda i, o: (i, o ^ 1) if i % 2 else (i ^ 2, o)),
        plane_perm(inner_n, outer_n, lambda i, o: (i ^ 2, o) if i % 2 else (i, o ^ 1)),
        plane_perm(inner_n, outer_n, lambda i, o: (i ^ 1, o)),
    )
    hops = [[(i, i ^ k) for i in range(tensor_n)] for k in range(1, tensor_n)]
    attn_parts = [spread(lax.ppermute(attn_piece, "tensor", hop), perms) for hop in hops]
    mlp_parts = [spread(lax.ppermute(mlp_piece, "tensor", hop), perms) for hop in hops]
    all_biases = lax.all_gather(jnp.concatenate([qv_bias.reshape(-1), fc1_bias]), "tensor")

    def biases_of(k):
        one = lax.dynamic_index_in_dim(all_biases, t ^ k, 0, keepdims=False)
        q_bias, v_bias = one[0:head_width], one[head_width : 2 * head_width]
        ones = jnp.ones((heads,), F32)
        gap = jnp.zeros((WIDE - head_width - heads,), F32)
        zeros = jnp.zeros((WIDE,), F32)
        row = jnp.concatenate([q_bias, zeros[head_width:], zeros, v_bias, ones, gap])
        return row[None, :], one[2 * head_width :][None, :]

    biases = [biases_of(k) for k in range(tensor_n)]

    flag = jnp.concatenate(
        [
            jnp.zeros((crops, seq - patch_mask.shape[1]), F32),
            (patch_mask == 1).astype(F32),
            jnp.zeros((crops, rows - seq), F32),
        ],
        1,
    )
    flags = jnp.broadcast_to(flag[:, :, None], (crops, rows, LANES))
    pos = jnp.pad(pos_embed, ((0, rows - seq), (0, 0)))
    begin, n1, up = enter(
        tokens.transpose(1, 0, 2),
        cotangent.transpose(1, 0, 2),
        flags,
        jnp.stack([mask_token, pre_attn_gain, pre_attn_bias]),
        pos,
    )

    gap_rows = jnp.zeros((WIDE - head_width, width), BF16)
    own_w = jnp.concatenate(
        sum(
            ([own_attn[i * head_width : (i + 1) * head_width], gap_rows] for i in range(4)),
            [],
        ),
        0,
    )
    attn_vecs = jnp.stack([attn_scale, proj_bias, pre_mlp_gain, pre_mlp_bias])
    run = functools.partial(attn, heads=heads, tail_valid=tail_valid)
    br0, mix0, lse0, att0 = run(n1, biases[0][0], [own_w], None, [])
    br1, mix1, lse1, w_1 = run(n1, biases[1][0], attn_parts[0], info, [br0])
    br2, mix2, lse2, w_2 = run(n1, biases[2][0], attn_parts[1], info, [])
    br, mix3, lse3, w_3, n2 = run(
        n1, biases[3][0], attn_parts[2], info, [br2, br1], finish=(begin, attn_vecs)
    )

    mlp_vecs = jnp.stack([mlp_scale, fc2_bias, attn_scale, proj_bias, pre_mlp_gain])
    out0, gn0, a0, gh0, go0, hsum = mlp(
        n2, up, mlp_vecs, biases[0][1], [own_fc1, fc2_weight], None, [], own=True
    )
    flat = lambda x: x.reshape(crops * rows, -1)
    grad_fc1, grad_fc2 = weight_grads(flat(n2), flat(gh0), flat(go0), flat(a0))
    shares_mlp = reduce_inner(jnp.concatenate([grad_fc1, grad_fc2], 1))
    acc1 = mlp(n2, up, mlp_vecs, biases[1][1], mlp_parts[0], info, [(out0, gn0)])
    acc2 = mlp(n2, up, mlp_vecs, biases[2][1], mlp_parts[1], info, [])
    result, gmid, gb, mid_sums = mlp(
        n2, up, mlp_vecs, biases[3][1], mlp_parts[2], info, [acc2, acc1], finish=(begin, br), seq=seq
    )

    back = functools.partial(attn_back, heads=heads, tail_valid=tail_valid)
    gn0, gm0, qv_sums = back(gb, own_w, mix0, lse0, [], own=True)
    grad_qkv, grad_proj = weight_grads(flat(n1), flat(gm0), flat(gb), flat(att0))
    pieces = [grad_qkv[:, i * WIDE : i * WIDE + head_width] for i in range(3)]
    shares_attn = reduce_inner(jnp.concatenate(pieces + [grad_proj[:, :head_width]], 1))
    (gn1,) = back(gb, w_1, mix1, lse1, [gn0])
    (gn2,) = back(gb, w_2, mix2, lse2, [])
    gtok, gpos, last_sums = back(
        gb, w_3, mix3, lse3, [gn2, gn1], finish=(begin, gmid, flags, pre_attn_gain[None, :]), seq=seq
    )

    quarter = width // inner_n
    small = head_width // inner_n

    def spaced(x):
        return jnp.pad(x.reshape(inner_n, small), ((0, 0), (0, quarter - small))).reshape(1, width)

    pack = jnp.concatenate(
        [
            gpos[:seq],
            mid_sums[0:6],
            last_sums[0:3],
            hsum[0:1],
            spaced(qv_sums[0, :head_width]),
            spaced(qv_sums[1, :head_width]),
        ],
        0,
    )
    pack = pack.reshape(-1, inner_n, quarter).transpose(1, 0, 2).reshape(-1, quarter)
    small_sums = reduce_inner(pack)
    vec = lambda i: small_sums[seq + i]
    grad_qkv = shares_attn[:, : 3 * head_width].reshape(-1, 3, head_width)
    return (
        result.transpose(1, 0, 2),
        gtok.reshape(seq, crops, width).transpose(1, 0, 2),
        vec(8),
        small_sums[:seq],
        vec(6),
        vec(7),
        grad_qkv,
        jnp.stack([vec(10)[:small], vec(11)[:small]]),
        shares_attn[:, 3 * head_width :].T,
        vec(5),
        vec(4),
        vec(2),
        vec(3),
        shares_mlp[:, :hidden],
        vec(9),
        shares_mlp[:, hidden:].T,
        vec(1),
        vec(0),
    )


def solution(mesh):
    in_specs = (
        P(("inner", "outer"), None, None),
        P(("inner", "outer"), None),
        P(("inner", "outer"), None, None),
        P(),
        P(),
        P(),
        P(),
        P(None, None, "tensor"),
        P(None, "tensor"),
        P("tensor", None),
        P(),
        P(),
        P(),
        P(),
        P(None, "tensor"),
        P("tensor"),
        P("tensor", None),
        P(),
        P(),
    )
    out_specs = (
        P(("inner", "outer"), None, None),
        P(("inner", "outer"), None, None),
        P("inner"),
        P(None, "inner"),
        P("inner"),
        P("inner"),
        P("inner", None, "tensor"),
        P(None, ("tensor", "inner")),
        P("tensor", "inner"),
        P("inner"),
        P("inner"),
        P("inner"),
        P("inner"),
        P("inner", "tensor"),
        P(("tensor", "inner")),
        P("tensor", "inner"),
        P("inner"),
        P("inner"),
    )
    sizes = tuple(mesh.shape[name] for name in ("tensor", "inner", "outer"))
    return jax.shard_map(
        functools.partial(per_device, sizes),
        mesh=mesh,
        in_specs=in_specs,
        out_specs=out_specs,
        check_vma=False,
    )
```

```python
import functools

import jax
import jax.numpy as jnp
from jax import lax
from jax.experimental import pallas as pl
from jax.experimental.pallas import tpu as pltpu
from jax.sharding import PartitionSpec as P

HEAD_DIM = 64
EPS = 1e-06
F32 = jnp.float32
BF16 = jnp.bfloat16
NEG = -1e30
LANES = 128
WIDE = 256
MAIN = 256
VMEM_LIMIT = 56 * 1024 * 1024
PLANE = ("inner", "outer")
PART = 96


def mm_nt(a, b):
    return lax.dot_general(a, b, (((1,), (1,)), ((), ())), preferred_element_type=F32)


def mm_nn(a, b):
    return lax.dot_general(a, b, (((1,), (0,)), ((), ())), preferred_element_type=F32)


def mm_tn(a, b):
    return lax.dot_general(a, b, (((0,), (0,)), ((), ())), preferred_element_type=F32)


SHARE = 1.0


def cost(us):
    return pl.CostEstimate(flops=int(us * SHARE * 1.15e9), bytes_accessed=1 << 20, transcendentals=0)


(
    MASK_TOKEN,
    PRE_ATTN_GAIN,
    PRE_ATTN_BIAS,
    PROJ_BIAS,
    ATTN_SCALE,
    PRE_MLP_GAIN,
    PRE_MLP_BIAS,
    FC2_BIAS,
    MLP_SCALE,
) = range(9)


def row(ref, i):
    return ref[i : i + 1, :]


def params():
    return pltpu.CompilerParams(vmem_limit_bytes=VMEM_LIMIT)


def block(shape):
    return pl.BlockSpec((1,) + tuple(shape[1:]), lambda c: (c,) + (0,) * (len(shape) - 1))


def whole(shape):
    return pl.BlockSpec(tuple(shape), lambda c: (0,) * len(shape))


def row_sum(x):
    return jnp.sum(x, 0, keepdims=True)


def norm_parts(v):
    center = v - jnp.mean(v, -1, keepdims=True)
    rstd = lax.rsqrt(jnp.mean(center * center, -1, keepdims=True) + EPS)
    return center * rstd, rstd


def norm_back(xhat, rstd, u, gain):
    gu = u * gain
    return (
        gu - jnp.mean(gu, -1, keepdims=True) - xhat * jnp.mean(gu * xhat, -1, keepdims=True)
    ) * rstd


def put_columns(ref, rows, x):
    for j in range(ref.shape[0]):
        ref[j, rows, :] = x[:, j * LANES : (j + 1) * LANES]


def get_columns(ref, rows):
    return jnp.concatenate([ref[j, rows, :] for j in range(ref.shape[0])], 1)


def flag_lanes(mask_ref, rows, prefix):
    crop_mask = mask_ref[pl.ds(pl.program_id(0), 1), :]
    patches = crop_mask.shape[1]
    ones = jnp.broadcast_to((crop_mask == 1).astype(F32), (LANES, patches)).astype(BF16)
    token = lax.broadcasted_iota(jnp.int32, (rows, patches), 0)
    patch = lax.broadcasted_iota(jnp.int32, (rows, patches), 1)
    return mm_nt((token == patch + prefix).astype(F32).astype(BF16), ones)


def flag_wide(mask_ref, rows, prefix, width):
    return jnp.concatenate([flag_lanes(mask_ref, rows, prefix)] * (width // LANES), 1) > 0.5


def by_crop(src_ref, scratch):
    seq, crops, _ = src_ref.shape
    step = 29 if seq % 29 == 0 else 1

    @pl.when(pl.program_id(0) == 0)
    def _():
        def move(i, carry):
            dst = pl.ds(pl.multiple_of(i * (step * crops), crops), step * crops)
            put_columns(scratch, dst, src_ref[pl.ds(i * step, step)].astype(F32).reshape(step * crops, -1))
            return carry

        lax.fori_loop(0, seq // step, move, 0)
        scratch[:, seq * crops :, :] = jnp.zeros_like(scratch[:, seq * crops :, :])

    return get_columns(scratch, pl.ds(pl.program_id(0), scratch.shape[1] // crops, stride=crops))


def enter_kernel(tok_ref, mask_ref, vec_ref, pos_ref, begin_ref, n1_ref, scratch):
    tok = by_crop(tok_ref, scratch)
    rows = tok.shape[0]
    near = pos_ref.shape[0] // 8 * 8
    rest = pos_ref.shape[0] - near
    pos = [pos_ref[0:near, :]]
    if rest:
        pos.append(jnp.concatenate([pos_ref[near:, :], jnp.zeros((8 - rest, tok.shape[1]), F32)], 0))
    pos.append(jnp.zeros((rows - near - 8 * (rest > 0), tok.shape[1]), F32))
    pos = jnp.concatenate(pos, 0)
    prefix = tok_ref.shape[0] - mask_ref.shape[1]
    flagged = flag_wide(mask_ref, rows, prefix, tok.shape[1])
    begin = jnp.where(flagged, row(vec_ref, MASK_TOKEN), tok) + pos
    begin_ref[0] = begin
    xhat, _ = norm_parts(begin)
    n1_ref[0] = (xhat * row(vec_ref, PRE_ATTN_GAIN) + row(vec_ref, PRE_ATTN_BIAS)).astype(BF16)


def enter(tok, mask, vecs, pos, rows):
    seq, crops, width = tok.shape
    shape = (crops, rows, width)
    return pl.pallas_call(
        enter_kernel,
        grid=(crops,),
        in_specs=[whole(tok.shape), whole(mask.shape), whole(vecs.shape), whole(pos.shape)],
        out_specs=[block(shape)] * 2,
        out_shape=[jax.ShapeDtypeStruct(shape, F32), jax.ShapeDtypeStruct(shape, BF16)],
        scratch_shapes=[pltpu.VMEM((width // LANES, rows * crops, LANES), F32)],
        compiler_params=params(),
        cost_estimate=cost(7),
        name="enter",
    )(tok, mask, vecs, pos)


def upstream_kernel(cot_ref, up_ref, scratch):
    up_ref[0] = by_crop(cot_ref, scratch).astype(BF16)


def upstream(cot, rows):
    seq, crops, width = cot.shape
    shape = (crops, rows, width)
    return pl.pallas_call(
        upstream_kernel,
        grid=(crops,),
        in_specs=[whole(cot.shape)],
        out_specs=block(shape),
        out_shape=jax.ShapeDtypeStruct(shape, BF16),
        scratch_shapes=[pltpu.VMEM((width // LANES, rows * crops, LANES), F32)],
        compiler_params=params(),
        cost_estimate=cost(6),
        name="upstream",
    )(cot)


def head_masks(heads):
    lane = lax.broadcasted_iota(jnp.int32, (1, WIDE), 1)
    return [((lane // HEAD_DIM) == h).astype(F32) for h in range(heads)], lane


def per_head_rows(x, masks):
    parts = [x * m for m in masks]
    parts.append(jnp.zeros((LANES - 8 * len(masks), x.shape[1]), F32))
    return jnp.concatenate(parts, 0).astype(BF16)


def pick(index, parts):
    out = parts[-1]
    for h in range(len(parts) - 2, -1, -1):
        out = jnp.where(index == h, parts[h], out)
    return out


def attention_forward(n1, w_ref, bias, heads, tail_valid):
    masks, lane = head_masks(heads)
    low = [m.astype(BF16) for m in masks]
    head_width = heads * HEAD_DIM
    mixed = (mm_nt(n1, w_ref[0 : 3 * WIDE, :]) + bias).astype(BF16)
    q = mixed[:, 0:WIDE] * jnp.asarray(HEAD_DIM**-0.5, BF16)
    k, v = mixed[:, WIDE : 2 * WIDE], mixed[:, 2 * WIDE : 3 * WIDE]
    mixed = jnp.concatenate([q, k, v], 1)
    k_main, v_main = k[0:MAIN], v[0:MAIN]
    v_masks = [m + (lane == head_width + h).astype(F32) for h, m in enumerate(masks)]
    k_tail = per_head_rows(k[MAIN : MAIN + 8].astype(F32), masks)
    v_tail = per_head_rows(v[MAIN : MAIN + 8].astype(F32), v_masks)
    col = lax.broadcasted_iota(jnp.int32, (1, LANES), 1)
    valid = (col < 8 * heads) & ((col % 8) < tail_valid)
    s_tail = jnp.where(valid, mm_nt(q, k_tail), NEG)
    tops, total = [], None
    for h in range(heads):
        s = mm_nt(q * low[h], k_main)
        top = jnp.where((col // 8) == h, s_tail, NEG)
        for i in range(MAIN // LANES):
            top = jnp.maximum(top, s[:, i * LANES : (i + 1) * LANES])
        top = jnp.max(top, -1, keepdims=True)
        tops.append(top)
        part = mm_nn(jnp.exp(s - top).astype(BF16), v_main * v_masks[h].astype(BF16))
        total = part if total is None else total + part
    e_tail = jnp.exp(s_tail - pick(col // 8, tops)).astype(BF16)
    total = total + mm_nn(e_tail, v_tail)
    sums = [total[:, head_width + h : head_width + h + 1] for h in range(heads)]
    scale = pick(lane // HEAD_DIM, [1.0 / s for s in sums])
    attended = (total * scale).astype(BF16)
    log_total = pick(col, [t + jnp.log(s) for t, s in zip(tops, sums)])
    branch = mm_nn(attended, w_ref[3 * WIDE : 4 * WIDE, :])
    return mixed, log_total, attended, branch


def take_pieces(it, count):
    return [(ref, i) for ref in (next(it) for _ in range(count)) for i in range(ref.shape[0])]


def place_pieces(info_ref, pieces, out_ref, base, first):
    p, core = info_ref[0], info_ref[1]
    q = p ^ 2
    a_bit = jnp.where(core == 0, 4, 1)
    b_bit = 5 - a_bit
    idents = (p, p ^ a_bit, p ^ b_bit, p ^ 5, q, q ^ b_bit, q ^ a_bit, q ^ 5)
    for (ref, slot), ident in zip(pieces, idents, strict=True):
        dst = pl.multiple_of(first(ident), 32)
        out_ref[pl.ds(dst, PART), :] = ref[slot, base : base + PART, :].astype(BF16)


def attn_kernel(*refs, heads, tail_valid, own, into, accs, finish, gathers):
    it = iter(refs)
    if own:
        n1_ref, bias_ref, qkv_ref, proj_ref = (next(it) for _ in range(4))
        bias = bias_ref[...]
    else:
        info, n1_ref = next(it), next(it)
        pieces = take_pieces(it, gathers)
        bias = pieces[0][0][0, PART : PART + 1, :]
    acc_refs = [next(it) for _ in range(accs)]
    if finish:
        begin_ref, vec_ref = next(it), next(it)
    for _ in range(into):
        next(it)
    br_ref, mix_ref, lse_ref, w_ref = (next(it) for _ in range(4))

    @pl.when(pl.program_id(0) == 0)
    def _():
        width = heads * HEAD_DIM
        for i in range(4):
            w_ref[i * WIDE + width : (i + 1) * WIDE, :] = jnp.zeros((WIDE - width, w_ref.shape[1]), BF16)
        if own:
            for i in range(3):
                w_ref[i * WIDE : i * WIDE + width, :] = qkv_ref[i * width : (i + 1) * width, :]
            w_ref[3 * WIDE : 3 * WIDE + width, :] = proj_ref[...]
        else:
            place_pieces(info, pieces, w_ref, 0, lambda i: (i >> 1) * WIDE + (i & 1) * PART)

    mixed, log_total, attended, branch = attention_forward(n1_ref[0], w_ref, bias, heads, tail_valid)
    mix_ref[0] = mixed
    lse_ref[0] = log_total
    if own:
        next(it)[0] = attended
    for ref in acc_refs:
        branch = branch + ref[0]
    br_ref[0] = branch
    if finish:
        n2_ref = next(it)
        middle = begin_ref[0] + row(vec_ref, ATTN_SCALE) * (branch + row(vec_ref, PROJ_BIAS))
        xhat, _ = norm_parts(middle)
        n2_ref[0] = (xhat * row(vec_ref, PRE_MLP_GAIN) + row(vec_ref, PRE_MLP_BIAS)).astype(BF16)


def attn(n1, weights, info, accs, heads, tail_valid, finish=None, span=None, into=()):
    crops, rows, width = n1.shape
    own = info is None
    lo, hi = span or (0, crops)
    args, specs = [], []

    def crop(shape):
        return pl.BlockSpec((1,) + tuple(shape[1:]), lambda c: (c + lo,) + (0,) * (len(shape) - 1))

    def add(x, spec):
        args.append(x)
        specs.append(spec)

    if not own:
        add(info, pl.BlockSpec(memory_space=pltpu.SMEM))
    add(n1, crop(n1.shape))
    for w in weights:
        add(w, whole(w.shape))
    for a in accs:
        add(a, crop(a.shape))
    if finish is not None:
        add(finish[0], crop(finish[0].shape))
        add(finish[1], whole(finish[1].shape))
    outs = [
        ((crops, rows, width), F32, crop),
        ((crops, rows, 3 * WIDE), BF16, crop),
        ((crops, rows, LANES), F32, crop),
        ((4 * WIDE, width), BF16, whole),
    ]
    if own:
        outs.append(((crops, rows, WIDE), BF16, crop))
    if finish is not None:
        outs.append(((crops, rows, width), BF16, crop))
    aliases = {}
    for i, x in enumerate(into):
        if outs[i][2] is crop:
            aliases[len(args)] = i
            add(x, pl.BlockSpec(memory_space=pl.ANY))
    return pl.pallas_call(
        functools.partial(
            attn_kernel,
            heads=heads,
            tail_valid=tail_valid,
            own=own,
            gathers=len(weights),
            into=len(aliases),
            accs=len(accs),
            finish=finish is not None,
        ),
        grid=(hi - lo,),
        in_specs=specs,
        out_specs=[kind(shape) for shape, _, kind in outs],
        out_shape=[jax.ShapeDtypeStruct(shape, dtype) for shape, dtype, _ in outs],
        input_output_aliases=aliases,
        compiler_params=params(),
        cost_estimate=cost((21 if finish is not None else 16) * (hi - lo) / crops),
        name="attention",
    )(*args)


def attention_backward(gb, w_ref, mix_ref, lse_ref, heads, tail_valid):
    masks, lane = head_masks(heads)
    low = [m.astype(BF16) for m in masks]
    da = mm_nt(gb, w_ref[3 * WIDE : 4 * WIDE, :]).astype(BF16)
    q, k, v = (mix_ref[0, :, i * WIDE : (i + 1) * WIDE] for i in range(3))
    k_main, v_main = k[0:MAIN], v[0:MAIN]
    k_tail = per_head_rows(k[MAIN : MAIN + 8].astype(F32), masks)
    v_tail = per_head_rows(v[MAIN : MAIN + 8].astype(F32), masks)
    col = lax.broadcasted_iota(jnp.int32, (1, LANES), 1)
    valid = (col < 8 * heads) & ((col % 8) < tail_valid)
    lse = [lse_ref[0, :, h : h + 1] for h in range(heads)]
    p_tail = jnp.where(valid, jnp.exp(mm_nt(q, k_tail) - pick(col // 8, lse)), 0.0)
    dp_tail = mm_nt(da, v_tail)
    x_tail = p_tail * dp_tail
    dq = dk = dv = None
    deltas = []
    for h in range(heads):
        qh, dah = q * low[h], da * low[h]
        p = jnp.exp(mm_nt(qh, k_main) - lse[h])
        dp = mm_nt(dah, v_main)
        x = p * dp
        delta = jnp.where((col // 8) == h, x_tail, 0.0)
        for i in range(MAIN // LANES):
            delta = delta + x[:, i * LANES : (i + 1) * LANES]
        delta = jnp.sum(delta, -1, keepdims=True)
        deltas.append(delta)
        ds = (p * (dp - delta)).astype(BF16)
        one = mm_nn(ds, k_main * low[h])
        two = mm_tn(ds, qh)
        three = mm_tn(p.astype(BF16), dah)
        dq = one if dq is None else dq + one
        dk = two if dk is None else dk + two
        dv = three if dv is None else dv + three
    ds_tail = (p_tail * (dp_tail - pick(col // 8, deltas))).astype(BF16)
    dq = (dq + mm_nn(ds_tail, k_tail)) * (HEAD_DIM**-0.5)
    dk_tail = mm_tn(ds_tail, q)
    dv_tail = mm_tn(p_tail.astype(BF16), da)
    dk_tail = sum(dk_tail[8 * h : 8 * h + 8] * masks[h] for h in range(heads))
    dv_tail = sum(dv_tail[8 * h : 8 * h + 8] * masks[h] for h in range(heads))
    rest = jnp.zeros((gb.shape[0] - MAIN - 8, WIDE), F32)
    dk = jnp.concatenate([dk, dk_tail, rest], 0)
    dv = jnp.concatenate([dv, dv_tail, rest], 0)
    return dq, dk, dv


def attn_back_kernel(*refs, heads, tail_valid, own, accs, finish):
    it = iter(refs)
    gb_ref, w_ref, mix_ref, lse_ref = (next(it) for _ in range(4))
    acc_refs = [next(it) for _ in range(accs)]
    if finish:
        info, begin_ref, gmid_ref, mask_ref, vec_ref = (next(it) for _ in range(5))
        mid_ref, hsum_ref, qsum_ref = (next(it) for _ in range(3))
    else:
        gn_ref = next(it)
    first = pl.program_id(0) == 0
    dq, dk, dv = attention_backward(gb_ref[0], w_ref, mix_ref, lse_ref, heads, tail_valid)
    gm = jnp.concatenate([dq, dk, dv], 1).astype(BF16)
    if own:
        gm_ref, sum_ref = next(it), next(it)
        gm_ref[0] = gm
        sums = jnp.concatenate([row_sum(dq), row_sum(dv), jnp.zeros((6, WIDE), F32)], 0)
        sum_ref[...] = jnp.where(first, sums, sum_ref[...] + sums)
    gn = mm_nn(gm, w_ref[0 : 3 * WIDE, :])
    for ref in acc_refs:
        gn = gn + ref[0]
    if not finish:
        gn_ref[0] = gn
        return
    gtok_ref, keep_ref, give_ref, gtok_s, pack = (next(it) for _ in range(5))
    xhat, rstd = norm_parts(begin_ref[0])
    grad_begin = gmid_ref[0] + norm_back(xhat, rstd, gn, row(vec_ref, PRE_ATTN_GAIN))
    rows, width = grad_begin.shape
    seq = gtok_ref.shape[0] // 8
    flagged = flag_wide(mask_ref, rows, seq - mask_ref.shape[1], width)
    cleared = jnp.where(flagged, 0.0, grad_begin)
    put_columns(gtok_s, pl.ds(pl.program_id(0), rows, stride=8), cleared)
    last = rows + 8
    sums = jnp.concatenate([row_sum(gn * xhat), row_sum(gn), row_sum(grad_begin - cleared)], 0)

    @pl.when(first)
    def _():
        pack[0:rows, :] = grad_begin
        pack[last : last + 3, :] = sums

    @pl.when(jnp.logical_not(first))
    def _():
        pack[0:rows, :] += grad_begin
        pack[last : last + 3, :] += sums

    @pl.when(pl.program_id(0) == pl.num_programs(0) - 1)
    def _():
        for j in range(gtok_s.shape[0]):
            gtok_ref[:, j * LANES : (j + 1) * LANES] = gtok_s[j, 0 : seq * 8, :]
        pack[rows:last, :] = mid_ref[...]
        pack[last + 3 : last + 4, :] = hsum_ref[0:1, :]
        quarter = keep_ref.shape[2]
        small = heads * HEAD_DIM // 4
        for i in range(4):
            part = pack[:, i * quarter : (i + 1) * quarter]

            def put(ref):
                ref[i // 2] = part
                for t in range(2):
                    ref[i // 2, last + 4 + t : last + 5 + t, 0:small] = qsum_ref[
                        t : t + 1, i * small : (i + 1) * small
                    ]

            pl.when(info[1] == i % 2)(functools.partial(put, keep_ref))
            pl.when(info[1] != i % 2)(functools.partial(put, give_ref))


def attn_back(gb, w, mixed, lse, accs, heads, tail_valid, own=False, finish=None, seq=None):
    crops, rows, width = gb.shape
    args = [gb, w, mixed, lse, *accs]
    specs = [block(gb.shape), whole(w.shape), block(mixed.shape), block(lse.shape)]
    specs += [block(a.shape) for a in accs]
    outs, scratch = [], []
    if finish is not None:
        info, begin, gmid, *tables = finish
        args += [info, begin, gmid, *tables]
        specs += [pl.BlockSpec(memory_space=pltpu.SMEM), block(begin.shape), block(gmid.shape)]
        specs += [whole(x.shape) for x in tables]
        scratch.append(pltpu.VMEM((width // LANES, rows * crops, LANES), F32))
        scratch.append(pltpu.VMEM((rows + 16, width), F32))
    else:
        outs.append(((crops, rows, width), F32, block))
    if own:
        outs += [((crops, rows, 3 * WIDE), BF16, block), ((8, WIDE), F32, whole)]
    if finish is not None:
        outs += [
            ((seq * crops, width), F32, whole),
            ((2, rows + 16, width // 4), F32, whole),
            ((2, rows + 16, width // 4), F32, whole),
        ]
    return pl.pallas_call(
        functools.partial(
            attn_back_kernel,
            heads=heads,
            tail_valid=tail_valid,
            own=own,
            accs=len(accs),
            finish=finish is not None,
        ),
        grid=(crops,),
        in_specs=specs,
        out_specs=[kind(shape) for shape, _, kind in outs],
        out_shape=[jax.ShapeDtypeStruct(shape, dtype) for shape, dtype, _ in outs],
        scratch_shapes=scratch,
        compiler_params=params(),
        cost_estimate=cost(31 if finish is not None else 22),
        name="attention_back",
    )(*args)


def gelu_and_slope(h):
    phi = 0.5 * (1.0 + lax.erf(h * (2.0**-0.5)))
    bell = jnp.exp(-0.5 * h * h) * 0.3989422804014327
    return h * phi, phi + h * bell


def mlp_kernel(*refs, gathered, accs, own, finish):
    it = iter(refs)
    if gathered:
        info = next(it)
    n2_ref, up_ref, vec_ref = (next(it) for _ in range(3))
    if gathered:
        pieces = take_pieces(it, 4)
        bias = pieces[0][0][0, PART : PART + 1, :]
    else:
        bias_ref, w1_ref, w2_ref = (next(it) for _ in range(3))
        bias = bias_ref[...]
    acc_refs = [(next(it), next(it)) for _ in range(accs)]
    if finish:
        begin_ref, br_ref = next(it), next(it)
        res_ref, gmid_ref, gb_ref, sum_ref = (next(it) for _ in range(4))
    else:
        out_ref, gn_ref = next(it), next(it)
    if own:
        a_ref, gh_ref, go_ref, hsum_ref = (next(it) for _ in range(4))
    first = pl.program_id(0) == 0
    if finish:
        res_s = next(it)
    if gathered:
        w1_ref, w2_ref = next(it), next(it)

        @pl.when(first)
        def _():
            place_pieces(info, pieces, w1_ref, 0, lambda i: i * PART)
            place_pieces(info, pieces, w2_ref, PART + 8, lambda i: i * PART)

    up = up_ref[0].astype(F32)
    grad_output = up * row(vec_ref, MLP_SCALE)
    go = grad_output.astype(BF16)
    n2 = n2_ref[0]
    a, slope = gelu_and_slope(mm_nt(n2, w1_ref[...]) + bias)
    a = a.astype(BF16)
    gh = mm_nt(go, w2_ref[...]) * slope
    if own:
        a_ref[0] = a
        go_ref[0] = go
        sums = jnp.concatenate([row_sum(gh), jnp.zeros((7, gh.shape[1]), F32)], 0)
        hsum_ref[...] = jnp.where(first, sums, hsum_ref[...] + sums)
    gh = gh.astype(BF16)
    if own:
        gh_ref[0] = gh
    out = mm_nn(a, w2_ref[...])
    gn = mm_nn(gh, w1_ref[...])
    for o_ref, g_ref in acc_refs:
        out = out + o_ref[0]
        gn = gn + g_ref[0]
    if not finish:
        out_ref[0] = out
        gn_ref[0] = gn
        return
    out = out + row(vec_ref, FC2_BIAS)
    branch = br_ref[0] + row(vec_ref, PROJ_BIAS)
    attn_scale = row(vec_ref, ATTN_SCALE)
    middle = begin_ref[0] + attn_scale * branch
    result = middle + row(vec_ref, MLP_SCALE) * out
    rows = result.shape[0]
    crops = 8
    put_columns(res_s, pl.ds(pl.program_id(0), rows, stride=crops), result)
    xhat, rstd = norm_parts(middle)
    gmid = up + norm_back(xhat, rstd, gn, row(vec_ref, PRE_MLP_GAIN))
    gmid_ref[0] = gmid
    gbr = gmid * attn_scale
    gb_ref[0] = gbr.astype(BF16)
    sums = jnp.concatenate(
        [
            row_sum(up * out),
            row_sum(grad_output),
            row_sum(gn * xhat),
            row_sum(gn),
            row_sum(gmid * branch),
            row_sum(gbr),
            jnp.zeros((2, gn.shape[1]), F32),
        ],
        0,
    )
    sum_ref[...] = jnp.where(first, sums, sum_ref[...] + sums)

    @pl.when(pl.program_id(0) == pl.num_programs(0) - 1)
    def _():
        seq = res_ref.shape[0]
        step = 29 if seq % 29 == 0 else 1

        def move(i, carry):
            src = pl.ds(pl.multiple_of(i * (step * crops), crops), step * crops)
            res_ref[pl.ds(i * step, step)] = get_columns(res_s, src).reshape(step, crops, -1).astype(BF16)
            return carry

        lax.fori_loop(0, seq // step, move, 0)


def mlp(n2, up, vecs, weights, info, accs, hidden, own=False, finish=None, seq=None):
    crops, rows, width = n2.shape
    gathered = info is not None
    args, specs = [], []

    def add(x, spec):
        args.append(x)
        specs.append(spec)

    if gathered:
        add(info, pl.BlockSpec(memory_space=pltpu.SMEM))
    add(n2, block(n2.shape))
    add(up, block(up.shape))
    add(vecs, whole(vecs.shape))
    for w in weights:
        add(w, whole(w.shape))
    for pair in accs:
        for a in pair:
            add(a, block(a.shape))
    full = (crops, rows, width)
    scratch = []
    if finish is not None:
        add(finish[0], block(finish[0].shape))
        add(finish[1], block(finish[1].shape))
        outs = [
            ((seq, crops, width), BF16, whole),
            (full, F32, block),
            (full, BF16, block),
            ((8, width), F32, whole),
        ]
        scratch.append(pltpu.VMEM((width // LANES, rows * crops, LANES), F32))
    else:
        outs = [(full, F32, block), (full, F32, block)]
    if own:
        outs += [((crops, rows, hidden), BF16, block)] * 2 + [(full, BF16, block), ((8, hidden), F32, whole)]
    if gathered:
        scratch += [pltpu.VMEM((hidden, width), BF16)] * 2
    return pl.pallas_call(
        functools.partial(mlp_kernel, gathered=gathered, accs=len(accs), own=own, finish=finish is not None),
        grid=(crops,),
        in_specs=specs,
        out_specs=[kind(shape) for shape, _, kind in outs],
        out_shape=[jax.ShapeDtypeStruct(shape, dtype) for shape, dtype, _ in outs],
        scratch_shapes=scratch,
        compiler_params=params(),
        cost_estimate=cost(28 if finish is not None else 17),
        name="mlp",
    )(*args)


def weight_grad_kernel(x1_ref, y1_ref, x2_ref, y2_ref, out_ref, *, parts):
    first, second = mm_tn(x1_ref[...], y1_ref[...]), mm_tn(x2_ref[...], y2_ref[...])
    out_ref[...] = jnp.concatenate([(first, second)[i][:, lo:hi] for i, lo, hi in parts], 1)


def weight_grads(x1, y1, x2, y2, parts):
    rows, width = x1.shape
    col = pl.BlockSpec((rows, WIDE), lambda i: (0, i))
    wide = sum(hi - lo for _, lo, hi in parts)
    return pl.pallas_call(
        functools.partial(weight_grad_kernel, parts=parts),
        grid=(width // WIDE,),
        in_specs=[col, whole(y1.shape), col, whole(y2.shape)],
        out_specs=pl.BlockSpec((WIDE, wide), lambda i: (i, 0)),
        out_shape=jax.ShapeDtypeStruct((width, wide), F32),
        compiler_params=params(),
        cost_estimate=cost(10),
        name="weight_grads",
    )(x1, y1, x2, y2)


def plane_perm(inner, outer, move):
    pairs = []
    for i in range(inner):
        for o in range(outer):
            j, r = move(i, o)
            pairs.append((i * outer + o, j * outer + r))
    return pairs


def after(x, *others):
    return lax.optimization_barrier((x, *others))[0] if others else x


def fence(new, *done):
    return lax.optimization_barrier((*new, *done))[: len(new)]


class PlaneSum:
    def __init__(self, sizes, inner, keep, give):
        _, self.inner_n, self.outer_n = sizes
        self.side = inner // 2
        self.keep, self.give = keep, give

    def cores(self, *others):
        self.one = lax.ppermute(
            after(self.give, *others), "inner", [(i, i ^ 1) for i in range(self.inner_n)]
        )
        return self.one

    def pick(self, side):
        return sum(lax.dynamic_index_in_dim(x, side, 0, keepdims=False) for x in (self.keep, self.one))

    def sides(self, *others):
        give = after(self.pick(1 - self.side), *others)
        self.two = lax.ppermute(give, "inner", [(i, i ^ 2) for i in range(self.inner_n)])
        return self.two

    def groups(self, *others):
        total = self.pick(self.side) + after(self.two, *others)
        k = 1
        while k < self.outer_n:
            total = total + lax.ppermute(total, "outer", [(o, o ^ k) for o in range(self.outer_n)])
            k *= 2
        return total


def per_device(
    sizes,
    tokens,
    patch_mask,
    cotangent,
    mask_token,
    pos_embed,
    pre_attn_gain,
    pre_attn_bias,
    qkv_weight,
    qv_bias,
    proj_weight,
    proj_bias,
    attn_scale,
    pre_mlp_gain,
    pre_mlp_bias,
    fc1_weight,
    fc1_bias,
    fc2_weight,
    fc2_bias,
    mlp_scale,
):
    tensor_n, inner_n, outer_n = sizes
    crops, seq, width = tokens.shape
    head_width = qkv_weight.shape[2]
    heads = head_width // HEAD_DIM
    hidden = fc1_weight.shape[1]
    rows = -(-seq // 16) * 16
    tail_valid = seq - MAIN
    t = lax.axis_index("tensor")
    inner = lax.axis_index("inner")
    outer = lax.axis_index("outer")
    place = inner * 2 + outer % 2
    info = jnp.stack([place, inner % 2]).astype(jnp.int32)

    qkv_rows = qkv_weight.transpose(1, 2, 0).reshape(3 * head_width, width)
    own_fc1 = fc1_weight.T

    def eighth(x):
        return lax.dynamic_slice_in_dim(x, place * PART, PART, 0).astype(F32)

    ones = jnp.ones((heads,), F32)
    zeros = jnp.zeros((WIDE,), F32)
    attn_bias = jnp.concatenate(
        [qv_bias[0], zeros[head_width:], zeros, qv_bias[1], ones, zeros[head_width + heads :]]
    )[None, :]
    mlp_bias = fc1_bias[None, :]
    below = jnp.zeros((7, width), F32)
    attn_piece = jnp.concatenate(
        [eighth(jnp.concatenate([qkv_rows, proj_weight], 0)), attn_bias, below], 0
    )
    fc1_piece = jnp.concatenate([eighth(own_fc1), mlp_bias, below], 0)
    fc2_piece = eighth(fc2_weight)
    perms = (
        plane_perm(inner_n, outer_n, lambda i, o: (i, o ^ 1) if i % 2 else (i ^ 2, o)),
        plane_perm(inner_n, outer_n, lambda i, o: (i ^ 2, o) if i % 2 else (i, o ^ 1)),
        plane_perm(inner_n, outer_n, lambda i, o: (i ^ 1, o)),
    )
    def over_z(x, k):
        return lax.ppermute(x, "tensor", [(i, i ^ k) for i in range(tensor_n)])

    along, far, peer = (functools.partial(lax.ppermute, axis_name=PLANE, perm=p) for p in perms)

    vecs = jnp.stack(
        [
            mask_token,
            pre_attn_gain,
            pre_attn_bias,
            proj_bias,
            attn_scale,
            pre_mlp_gain,
            pre_mlp_bias,
            fc2_bias,
            mlp_scale,
        ]
    )
    run = functools.partial(attn, heads=heads, tail_valid=tail_valid)
    layer = functools.partial(mlp, hidden=hidden)

    quarter = width // inner_n

    def plane_sum(x):
        x = x.reshape(2, 2, quarter, -1)
        take = lambda core: lax.dynamic_index_in_dim(x, core, 1, keepdims=False)
        return PlaneSum(sizes, inner, take(inner % 2), take(1 - inner % 2))

    def pair(first, second):
        return jnp.stack([first, second])

    cut = 56
    attn_hi, attn_lo = attn_piece[:cut], attn_piece[cut:]

    a1, a2 = over_z(attn_piece, 1), over_z(attn_piece, 2)
    begin, n1 = enter(tokens.transpose(1, 0, 2), patch_mask, vecs, pos_embed, rows)

    n1, a1, a2, attn_hi, fc1_piece = fence((n1, a1, a2, attn_hi, fc1_piece))
    b1, b2 = along(a1), along(a2)
    a3_hi, m1_hi = over_z(attn_hi, 3), over_z(fc1_piece, 1)
    half = crops // 2
    own_w = [attn_bias, qkv_rows, proj_weight]
    early = run(n1, own_w, None, [], span=(0, half))

    both1 = pair(a1, b1)
    cot, both1, attn_lo = fence(
        (cotangent.transpose(1, 0, 2), both1, attn_lo), early[0], b1, b2, a3_hi, m1_hi
    )
    c1, d1 = far(both1), peer(both1)
    a3_lo = over_z(attn_lo, 3)
    up = upstream(cot, rows)

    both2, a3 = pair(a2, b2), jnp.concatenate([a3_hi, a3_lo], 0)
    n1, c1, both2, a3 = fence((n1, c1, both2, a3), up, d1)
    e1 = peer(c1)
    c2, d2 = far(both2), peer(both2)
    b3 = along(a3)
    br0, mix0, lse0, w_0, att0 = run(n1, own_w, None, [], span=(half, crops), into=early)

    both3 = pair(a3, b3)
    n1, c2, both3, fc1_piece, fc2_piece = fence(
        (n1, c2, both3, fc1_piece, fc2_piece), br0, e1, d2
    )
    e2 = peer(c2)
    c3 = far(both3)
    m1_lo = over_z(fc2_piece, 1)
    m2_hi = over_z(fc1_piece, 2)
    br1, mix1, lse1, w_1 = run(n1, [both1, c1, d1, e1], info, [br0])

    four3, m1 = jnp.concatenate([both3, c3], 0), jnp.concatenate([m1_hi, m1_lo], 0)
    n1, four3, m1, fc2_piece = fence((n1, four3, m1, fc2_piece), br1, e2, m2_hi)
    de3 = peer(four3)
    f1 = along(m1)
    m2_lo = over_z(fc2_piece, 2)
    br2, mix2, lse2, w_2 = run(n1, [both2, c2, d2, e2], info, [])

    two1, m2 = pair(m1, f1), jnp.concatenate([m2_hi, m2_lo], 0)
    n1, two1, m2, fc1_piece = fence((n1, two1, m2, fc1_piece), br2, de3)
    g1, h1 = far(two1), peer(two1)
    f2 = along(m2)
    m3_hi = over_z(fc1_piece, 3)
    br, mix3, lse3, w_3, n2 = run(n1, [four3, de3], info, [br2, br1], finish=(begin, vecs))

    two2 = pair(m2, f2)
    n2, g1, two2, fc2_piece = fence((n2, g1, two2, fc2_piece), h1, m3_hi)
    i1 = peer(g1)
    g2, h2 = far(two2), peer(two2)
    m3_lo = over_z(fc2_piece, 3)
    out0, gn0, a0, gh0, go0, hsum = layer(
        n2, up, vecs, [mlp_bias, own_fc1, fc2_weight], None, [], own=True
    )

    flat = lambda x: x.reshape(crops * rows, -1)
    m3 = jnp.concatenate([m3_hi, m3_lo], 0)
    n2, g2, m3 = fence((n2, g2, m3), out0, i1, h2)
    i2 = peer(g2)
    f3 = along(m3)
    mlp_grads = weight_grads(
        flat(n2), flat(gh0), flat(go0), flat(a0), ((0, 0, hidden), (1, 0, hidden))
    )

    two3 = pair(m3, f3)
    n2, two3, mlp_grads = fence((n2, two3, mlp_grads), i2)
    mlp_sum = plane_sum(mlp_grads)
    s1 = mlp_sum.cores()
    g3, h3 = far(two3), peer(two3)
    acc1 = layer(n2, up, vecs, [two1, g1, h1, i1], info, [(out0, gn0)])

    n2, g3 = fence((n2, g3), acc1[0], h3, s1)
    s2 = mlp_sum.sides(acc1[0])
    i3 = peer(g3)
    acc2 = layer(n2, up, vecs, [two2, g2, h2, i2], info, [])

    n2 = after(n2, i3)
    result, gmid, gb, mid_sums = layer(
        n2, up, vecs, [two3, g3, h3, i3], info, [acc2, acc1], finish=(begin, br), seq=seq
    )

    back = functools.partial(attn_back, heads=heads, tail_valid=tail_valid)
    s3 = mlp_sum.groups(gb)
    gb = after(gb, s2)
    gn0, gm0, qv_sums = back(gb, w_0, mix0, lse0, [], own=True)
    attn_grads = weight_grads(
        flat(n1),
        flat(gm0),
        flat(gb),
        flat(att0),
        tuple((0, i * WIDE, i * WIDE + head_width) for i in range(3)) + ((1, 0, head_width),),
    )

    gb = after(gb, attn_grads, s3)
    attn_sum = plane_sum(attn_grads)
    s1 = attn_sum.cores()
    (gn1,) = back(gb, w_1, mix1, lse1, [gn0])
    gb = after(gb, s1, gn1)
    s2 = attn_sum.sides(gn1)
    (gn2,) = back(gb, w_2, mix2, lse2, [])
    gb = after(gb, s2, gn2)
    shares_attn = attn_sum.groups(gn2)
    gtok, keep, give = back(
        gb,
        w_3,
        mix3,
        lse3,
        [gn2, gn1],
        finish=(info, begin, gmid, patch_mask, vecs, mid_sums, hsum, qv_sums),
        seq=seq,
    )
    shares_mlp = s3

    small = head_width // inner_n
    small_sum = PlaneSum(sizes, inner, keep, after(give, shares_attn))
    small_sum.cores()
    small_sum.sides()
    small_sums = small_sum.groups()
    mid = lambda i: small_sums[rows + i]
    vec = lambda i: small_sums[rows + 8 + i]
    grad_qkv = shares_attn[:, : 3 * head_width].reshape(-1, 3, head_width)
    return (
        result.transpose(1, 0, 2),
        gtok.reshape(seq, crops, width).transpose(1, 0, 2),
        vec(2),
        small_sums[:seq],
        vec(0),
        vec(1),
        grad_qkv,
        jnp.stack([vec(4)[:small], vec(5)[:small]]),
        shares_attn[:, 3 * head_width :].T,
        mid(5),
        mid(4),
        mid(2),
        mid(3),
        shares_mlp[:, :hidden],
        vec(3),
        shares_mlp[:, hidden:].T,
        mid(1),
        mid(0),
    )


def solution(mesh):
    in_specs = (
        P(("inner", "outer"), None, None),
        P(("inner", "outer"), None),
        P(("inner", "outer"), None, None),
        P(),
        P(),
        P(),
        P(),
        P(None, None, "tensor"),
        P(None, "tensor"),
        P("tensor", None),
        P(),
        P(),
        P(),
        P(),
        P(None, "tensor"),
        P("tensor"),
        P("tensor", None),
        P(),
        P(),
    )
    out_specs = (
        P(("inner", "outer"), None, None),
        P(("inner", "outer"), None, None),
        P("inner"),
        P(None, "inner"),
        P("inner"),
        P("inner"),
        P("inner", None, "tensor"),
        P(None, ("tensor", "inner")),
        P("tensor", "inner"),
        P("inner"),
        P("inner"),
        P("inner"),
        P("inner"),
        P("inner", "tensor"),
        P(("tensor", "inner")),
        P("tensor", "inner"),
        P("inner"),
        P("inner"),
    )
    sizes = tuple(mesh.shape[name] for name in ("tensor", "inner", "outer"))
    return jax.shard_map(
        functools.partial(per_device, sizes),
        mesh=mesh,
        in_specs=in_specs,
        out_specs=out_specs,
        check_vma=False,
    )
```

```python
import functools

import jax
import jax.numpy as jnp
from jax import lax
from jax.experimental import pallas as pl
from jax.experimental.pallas import tpu as pltpu
from jax.sharding import PartitionSpec as P

HEAD_DIM = 64
EPS = 1e-06
F32 = jnp.float32
BF16 = jnp.bfloat16
NEG = -1e30
LANES = 128
WIDE = 256
MAIN = 256
VMEM_LIMIT = 50 * 1024 * 1024
VMEM_MOST = 60 * 1024 * 1024
PLANE = ("inner", "outer")
PART = 96


def mm_nt(a, b):
    return lax.dot_general(a, b, (((1,), (1,)), ((), ())), preferred_element_type=F32)


def mm_nn(a, b):
    return lax.dot_general(a, b, (((1,), (0,)), ((), ())), preferred_element_type=F32)


def mm_tn(a, b):
    return lax.dot_general(a, b, (((0,), (0,)), ((), ())), preferred_element_type=F32)


ATTN_PER, BACK_PER, MLP_PER = 2, 2, 2


def cost(us):
    return pl.CostEstimate(flops=int(us * 1.15e9), bytes_accessed=1 << 20, transcendentals=0)


(
    MASK_TOKEN,
    PRE_ATTN_GAIN,
    PRE_ATTN_BIAS,
    PROJ_BIAS,
    ATTN_SCALE,
    PRE_MLP_GAIN,
    PRE_MLP_BIAS,
    FC2_BIAS,
    MLP_SCALE,
) = range(9)


def row(ref, i):
    return ref[i : i + 1, :]


def params(limit=VMEM_LIMIT):
    return pltpu.CompilerParams(vmem_limit_bytes=limit)


def block(shape, per=1):
    return pl.BlockSpec((per,) + tuple(shape[1:]), lambda c: (c,) + (0,) * (len(shape) - 1))


def whole(shape):
    return pl.BlockSpec(tuple(shape), lambda c: (0,) * len(shape))


def once(shape):
    return pl.BlockSpec(tuple(shape), lambda c: (0,) * len(shape), pipeline_mode=pl.Buffered(1))


def row_sum(x):
    return jnp.sum(x, 0, keepdims=True)


def norm_parts(v):
    center = v - jnp.mean(v, -1, keepdims=True)
    rstd = lax.rsqrt(jnp.mean(center * center, -1, keepdims=True) + EPS)
    return center * rstd, rstd


def norm_back(xhat, rstd, u, gain):
    gu = u * gain
    return (
        gu - jnp.mean(gu, -1, keepdims=True) - xhat * jnp.mean(gu * xhat, -1, keepdims=True)
    ) * rstd


def put_columns(ref, rows, x):
    for j in range(ref.shape[0]):
        ref[j, rows, :] = x[:, j * LANES : (j + 1) * LANES]


def get_columns(ref, rows):
    return jnp.concatenate([ref[j, rows, :] for j in range(ref.shape[0])], 1)


def flag_lanes(mask_ref, crop, rows, prefix):
    crop_mask = mask_ref[pl.ds(crop, 1), :]
    patches = crop_mask.shape[1]
    ones = jnp.broadcast_to((crop_mask == 1).astype(F32), (LANES, patches)).astype(BF16)
    token = lax.broadcasted_iota(jnp.int32, (rows, patches), 0)
    patch = lax.broadcasted_iota(jnp.int32, (rows, patches), 1)
    return mm_nt((token == patch + prefix).astype(F32).astype(BF16), ones)


def flag_wide(mask_ref, crop, rows, prefix, width):
    return jnp.concatenate([flag_lanes(mask_ref, crop, rows, prefix)] * (width // LANES), 1) > 0.5


def by_crop(src_ref, scratch):
    seq, crops, _ = src_ref.shape
    step = 29 if seq % 29 == 0 else 1

    @pl.when(pl.program_id(0) == 0)
    def _():
        def move(i, carry):
            dst = pl.ds(pl.multiple_of(i * (step * crops), crops), step * crops)
            put_columns(scratch, dst, src_ref[pl.ds(i * step, step)].astype(F32).reshape(step * crops, -1))
            return carry

        lax.fori_loop(0, seq // step, move, 0)
        scratch[:, seq * crops :, :] = jnp.zeros_like(scratch[:, seq * crops :, :])

    return get_columns(scratch, pl.ds(pl.program_id(0), scratch.shape[1] // crops, stride=crops))


def enter_kernel(tok_ref, mask_ref, vec_ref, pos_ref, begin_ref, n1_ref, scratch):
    tok = by_crop(tok_ref, scratch)
    rows = tok.shape[0]
    near = pos_ref.shape[0] // 8 * 8
    rest = pos_ref.shape[0] - near
    pos = [pos_ref[0:near, :]]
    if rest:
        pos.append(jnp.concatenate([pos_ref[near:, :], jnp.zeros((8 - rest, tok.shape[1]), F32)], 0))
    pos.append(jnp.zeros((rows - near - 8 * (rest > 0), tok.shape[1]), F32))
    pos = jnp.concatenate(pos, 0)
    prefix = tok_ref.shape[0] - mask_ref.shape[1]
    flagged = flag_wide(mask_ref, pl.program_id(0), rows, prefix, tok.shape[1])
    begin = jnp.where(flagged, row(vec_ref, MASK_TOKEN), tok) + pos
    begin_ref[0] = begin
    xhat, _ = norm_parts(begin)
    n1_ref[0] = (xhat * row(vec_ref, PRE_ATTN_GAIN) + row(vec_ref, PRE_ATTN_BIAS)).astype(BF16)


def enter(tok, mask, vecs, pos, rows):
    seq, crops, width = tok.shape
    shape = (crops, rows, width)
    return pl.pallas_call(
        enter_kernel,
        grid=(crops,),
        in_specs=[once(x.shape) for x in (tok, mask, vecs, pos)],
        out_specs=[block(shape)] * 2,
        out_shape=[jax.ShapeDtypeStruct(shape, F32), jax.ShapeDtypeStruct(shape, BF16)],
        scratch_shapes=[pltpu.VMEM((width // LANES, rows * crops, LANES), F32)],
        compiler_params=params(),
        cost_estimate=cost(7),
        name="enter",
    )(tok, mask, vecs, pos)


def upstream_kernel(cot_ref, up_ref, scratch):
    up_ref[0] = by_crop(cot_ref, scratch).astype(BF16)


def upstream(cot, rows):
    seq, crops, width = cot.shape
    shape = (crops, rows, width)
    return pl.pallas_call(
        upstream_kernel,
        grid=(crops,),
        in_specs=[once(cot.shape)],
        out_specs=block(shape),
        out_shape=jax.ShapeDtypeStruct(shape, BF16),
        scratch_shapes=[pltpu.VMEM((width // LANES, rows * crops, LANES), F32)],
        compiler_params=params(),
        cost_estimate=cost(6),
        name="upstream",
    )(cot)


def head_masks(heads):
    lane = lax.broadcasted_iota(jnp.int32, (1, WIDE), 1)
    return [((lane // HEAD_DIM) == h).astype(F32) for h in range(heads)], lane


def per_head_rows(x, masks):
    parts = [x * m for m in masks]
    parts.append(jnp.zeros((LANES - 8 * len(masks), x.shape[1]), F32))
    return jnp.concatenate(parts, 0).astype(BF16)


def pick(index, parts):
    out = parts[-1]
    for h in range(len(parts) - 2, -1, -1):
        out = jnp.where(index == h, parts[h], out)
    return out


def interleave(chains):
    live, waiting = [], list(chains)
    while live or waiting:
        live += waiting[:1]
        del waiting[:1]
        live = [chain for chain in live if next(chain, True) is None]


def attention_forward(n1, w_ref, bias, heads, tail_valid, last):
    masks, lane = head_masks(heads)
    low = [m.astype(BF16) for m in masks]
    head_width = heads * HEAD_DIM
    mixed = (mm_nt(n1, w_ref[0 : 3 * WIDE, :]) + bias).astype(BF16)
    yield
    q = mixed[:, 0:WIDE] * jnp.asarray(HEAD_DIM**-0.5, BF16)
    k, v = mixed[:, WIDE : 2 * WIDE], mixed[:, 2 * WIDE : 3 * WIDE]
    mixed = jnp.concatenate([q, k, v], 1)
    k_main, v_main = k[0:MAIN], v[0:MAIN]
    v_masks = [m + (lane == head_width + h).astype(F32) for h, m in enumerate(masks)]
    k_tail = per_head_rows(k[MAIN : MAIN + 8].astype(F32), masks)
    v_tail = per_head_rows(v[MAIN : MAIN + 8].astype(F32), v_masks)
    col = lax.broadcasted_iota(jnp.int32, (1, LANES), 1)
    valid = (col < 8 * heads) & ((col % 8) < tail_valid)
    s_tail = jnp.where(valid, mm_nt(q, k_tail), NEG)
    scores = [mm_nt(q * low[h], k_main) for h in range(heads)]
    yield
    tops, total = [], None
    for h in range(heads):
        s = scores[h]
        top = jnp.where((col // 8) == h, s_tail, NEG)
        for i in range(MAIN // LANES):
            top = jnp.maximum(top, s[:, i * LANES : (i + 1) * LANES])
        top = jnp.max(top, -1, keepdims=True)
        tops.append(top)
        part = mm_nn(jnp.exp(s - top).astype(BF16), v_main * v_masks[h].astype(BF16))
        total = part if total is None else total + part
    e_tail = jnp.exp(s_tail - pick(col // 8, tops)).astype(BF16)
    total = total + mm_nn(e_tail, v_tail)
    yield
    sums = [total[:, head_width + h : head_width + h + 1] for h in range(heads)]
    scale = pick(lane // HEAD_DIM, [1.0 / s for s in sums])
    attended = (total * scale).astype(BF16)
    log_total = pick(col, [t + jnp.log(s) for t, s in zip(tops, sums)])
    branch = mm_nn(attended, w_ref[3 * WIDE : 4 * WIDE, :])
    yield
    last(mixed, log_total, attended, branch)


def take_pieces(it, count):
    return [(ref, i) for ref in (next(it) for _ in range(count)) for i in range(ref.shape[0])]


def place_pieces(info_ref, pieces, out_ref, base, first):
    p, core = info_ref[0], info_ref[1]
    q = p ^ 2
    a_bit = jnp.where(core == 0, 4, 1)
    b_bit = 5 - a_bit
    idents = (p, p ^ a_bit, p ^ b_bit, p ^ 5, q, q ^ b_bit, q ^ a_bit, q ^ 5)
    for (ref, slot), ident in zip(pieces, idents, strict=True):
        dst = pl.multiple_of(first(ident), 32)
        out_ref[pl.ds(dst, PART), :] = ref[slot, base : base + PART, :].astype(BF16)


def attn_kernel(*refs, heads, tail_valid, own, into, accs, finish, gathers):
    it = iter(refs)
    if own:
        n1_ref, bias_ref, qkv_ref, proj_ref = (next(it) for _ in range(4))
        bias = bias_ref[...]
    else:
        info, n1_ref = next(it), next(it)
        pieces = take_pieces(it, gathers)
        bias = pieces[0][0][0, PART : PART + 1, :]
    acc_refs = [next(it) for _ in range(accs)]
    if finish:
        begin_ref, vec_ref = next(it), next(it)
    for _ in range(into):
        next(it)
    br_ref, mix_ref, lse_ref, w_ref = (next(it) for _ in range(4))

    @pl.when(pl.program_id(0) == 0)
    def _():
        width = heads * HEAD_DIM
        for i in range(4):
            w_ref[i * WIDE + width : (i + 1) * WIDE, :] = jnp.zeros((WIDE - width, w_ref.shape[1]), BF16)
        if own:
            for i in range(3):
                w_ref[i * WIDE : i * WIDE + width, :] = qkv_ref[i * width : (i + 1) * width, :]
            w_ref[3 * WIDE : 3 * WIDE + width, :] = proj_ref[...]
        else:
            place_pieces(info, pieces, w_ref, 0, lambda i: (i >> 1) * WIDE + (i & 1) * PART)

    att_ref = next(it) if own else None
    n2_ref = next(it) if finish else None

    def last(i, mixed, log_total, attended, branch):
        mix_ref[i] = mixed
        lse_ref[i] = log_total
        if own:
            att_ref[i] = attended
        for ref in acc_refs:
            branch = branch + ref[i]
        br_ref[i] = branch
        if finish:
            middle = begin_ref[i] + row(vec_ref, ATTN_SCALE) * (branch + row(vec_ref, PROJ_BIAS))
            xhat, _ = norm_parts(middle)
            n2 = xhat * row(vec_ref, PRE_MLP_GAIN) + row(vec_ref, PRE_MLP_BIAS)
            n2_ref[i] = n2.astype(BF16)

    interleave(
        [
            attention_forward(n1_ref[i], w_ref, bias, heads, tail_valid, functools.partial(last, i))
            for i in range(n1_ref.shape[0])
        ]
    )


def attn(n1, weights, info, accs, heads, tail_valid, finish=None, span=None, into=()):
    crops, rows, width = n1.shape
    own = info is None
    lo, hi = span or (0, crops)
    args, specs = [], []

    per = ATTN_PER

    def crop(shape):
        at = lambda c: (c + lo // per,) + (0,) * (len(shape) - 1)
        return pl.BlockSpec((per,) + tuple(shape[1:]), at)

    def add(x, spec):
        args.append(x)
        specs.append(spec)

    if not own:
        add(info, pl.BlockSpec(memory_space=pltpu.SMEM))
    add(n1, crop(n1.shape))
    for w in weights:
        add(w, once(w.shape))
    for a in accs:
        add(a, crop(a.shape))
    if finish is not None:
        add(finish[0], crop(finish[0].shape))
        add(finish[1], once(finish[1].shape))
    outs = [
        ((crops, rows, width), F32, crop),
        ((crops, rows, 3 * WIDE), BF16, crop),
        ((crops, rows, LANES), F32, crop),
        ((4 * WIDE, width), BF16, whole),
    ]
    if own:
        outs.append(((crops, rows, WIDE), BF16, crop))
    if finish is not None:
        outs.append(((crops, rows, width), BF16, crop))
    aliases = {}
    for i, x in enumerate(into):
        if outs[i][2] is crop:
            aliases[len(args)] = i
            add(x, pl.BlockSpec(memory_space=pl.ANY))
    return pl.pallas_call(
        functools.partial(
            attn_kernel,
            heads=heads,
            tail_valid=tail_valid,
            own=own,
            gathers=len(weights),
            into=len(aliases),
            accs=len(accs),
            finish=finish is not None,
        ),
        grid=((hi - lo) // per,),
        in_specs=specs,
        out_specs=[kind(shape) for shape, _, kind in outs],
        out_shape=[jax.ShapeDtypeStruct(shape, dtype) for shape, dtype, _ in outs],
        input_output_aliases=aliases,
        compiler_params=params(),
        cost_estimate=cost((21 if finish is not None else 16) * (hi - lo) / crops),
        name="attention",
    )(*args)


def attention_backward(gb, w_ref, mix, lse_in, heads, tail_valid, last):
    masks, lane = head_masks(heads)
    low = [m.astype(BF16) for m in masks]
    da = mm_nt(gb, w_ref[3 * WIDE : 4 * WIDE, :]).astype(BF16)
    q, k, v = (mix[:, i * WIDE : (i + 1) * WIDE] for i in range(3))
    k_main, v_main = k[0:MAIN], v[0:MAIN]
    k_tail = per_head_rows(k[MAIN : MAIN + 8].astype(F32), masks)
    v_tail = per_head_rows(v[MAIN : MAIN + 8].astype(F32), masks)
    col = lax.broadcasted_iota(jnp.int32, (1, LANES), 1)
    valid = (col < 8 * heads) & ((col % 8) < tail_valid)
    lse = [lse_in[:, h : h + 1] for h in range(heads)]
    s_tail = mm_nt(q, k_tail)
    qs = [q * m for m in low]
    scores = [mm_nt(x, k_main) for x in qs]
    yield
    p_tail = jnp.where(valid, jnp.exp(s_tail - pick(col // 8, lse)), 0.0)
    dp_tail = mm_nt(da, v_tail)
    x_tail = p_tail * dp_tail
    das = [da * m for m in low]
    dps = [mm_nt(x, v_main) for x in das]
    ps = [jnp.exp(s - t) for s, t in zip(scores, lse)]
    yield
    dq = dk = dv = None
    deltas = []
    for h in range(heads):
        p, dp = ps[h], dps[h]
        x = p * dp
        delta = jnp.where((col // 8) == h, x_tail, 0.0)
        for i in range(MAIN // LANES):
            delta = delta + x[:, i * LANES : (i + 1) * LANES]
        delta = jnp.sum(delta, -1, keepdims=True)
        deltas.append(delta)
        ds = (p * (dp - delta)).astype(BF16)
        one = mm_nn(ds, k_main * low[h])
        two = mm_tn(ds, qs[h])
        three = mm_tn(p.astype(BF16), das[h])
        dq = one if dq is None else dq + one
        dk = two if dk is None else dk + two
        dv = three if dv is None else dv + three
    yield
    ds_tail = (p_tail * (dp_tail - pick(col // 8, deltas))).astype(BF16)
    dq = (dq + mm_nn(ds_tail, k_tail)) * (HEAD_DIM**-0.5)
    dk_tail = mm_tn(ds_tail, q)
    dv_tail = mm_tn(p_tail.astype(BF16), da)
    dk_tail = sum(dk_tail[8 * h : 8 * h + 8] * masks[h] for h in range(heads))
    dv_tail = sum(dv_tail[8 * h : 8 * h + 8] * masks[h] for h in range(heads))
    rest = jnp.zeros((gb.shape[0] - MAIN - 8, WIDE), F32)
    dk = jnp.concatenate([dk, dk_tail, rest], 0)
    dv = jnp.concatenate([dv, dv_tail, rest], 0)
    gm = jnp.concatenate([dq, dk, dv], 1).astype(BF16)
    gn = mm_nn(gm, w_ref[0 : 3 * WIDE, :])
    yield
    last(dq, dv, gm, gn)


def attn_back_kernel(*refs, heads, tail_valid, own, accs, finish):
    it = iter(refs)
    gb_ref, w_ref, mix_ref, lse_ref = (next(it) for _ in range(4))
    acc_refs = [next(it) for _ in range(accs)]
    if finish:
        info, begin_ref, gmid_ref, mask_ref, vec_ref = (next(it) for _ in range(5))
        mid_ref, hsum_ref, qsum_ref = (next(it) for _ in range(3))
    else:
        gn_ref = next(it)
    if own:
        gm_ref, sum_ref = next(it), next(it)
    if finish:
        gtok_ref, keep_ref, give_ref, gtok_s, pack = (next(it) for _ in range(5))
        seq = gtok_ref.shape[0] // 8
    first = pl.program_id(0) == 0
    per, rows, width = gb_ref.shape
    many, positions = [], []

    def last(i, dq, dv, gm, gn):
        if own:
            gm_ref[i] = gm
            many.append(jnp.concatenate([row_sum(dq), row_sum(dv), jnp.zeros((6, WIDE), F32)], 0))
        for ref in acc_refs:
            gn = gn + ref[i]
        if not finish:
            gn_ref[i] = gn
            return
        xhat, rstd = norm_parts(begin_ref[i])
        grad_begin = gmid_ref[i] + norm_back(xhat, rstd, gn, row(vec_ref, PRE_ATTN_GAIN))
        crop = pl.program_id(0) * per + i
        flagged = flag_wide(mask_ref, crop, rows, seq - mask_ref.shape[1], width)
        cleared = jnp.where(flagged, 0.0, grad_begin)
        put_columns(gtok_s, pl.ds(crop, rows, stride=8), cleared)
        many.append(
            jnp.concatenate([row_sum(gn * xhat), row_sum(gn), row_sum(grad_begin - cleared)], 0)
        )
        positions.append(grad_begin)

    interleave(
        [
            attention_backward(
                gb_ref[i], w_ref, mix_ref[i], lse_ref[i], heads, tail_valid, functools.partial(last, i)
            )
            for i in range(per)
        ]
    )
    sums, grad_pos = (sum(x[1:], x[0]) if x else None for x in (many, positions))
    if own:
        sum_ref[...] = jnp.where(first, sums, sum_ref[...] + sums)
    if not finish:
        return
    after_mid = rows + 8

    @pl.when(first)
    def _():
        pack[0:rows, :] = grad_pos
        pack[after_mid : after_mid + 3, :] = sums

    @pl.when(jnp.logical_not(first))
    def _():
        pack[0:rows, :] += grad_pos
        pack[after_mid : after_mid + 3, :] += sums

    @pl.when(pl.program_id(0) == pl.num_programs(0) - 1)
    def _():
        for j in range(gtok_s.shape[0]):
            gtok_ref[:, j * LANES : (j + 1) * LANES] = gtok_s[j, 0 : seq * 8, :]
        pack[rows:after_mid, :] = mid_ref[...]
        pack[after_mid + 3 : after_mid + 4, :] = hsum_ref[0:1, :]
        quarter = keep_ref.shape[2]
        small = heads * HEAD_DIM // 4
        for i in range(4):
            part = pack[:, i * quarter : (i + 1) * quarter]

            def put(ref):
                ref[i // 2] = part
                for t in range(2):
                    ref[i // 2, after_mid + 4 + t : after_mid + 5 + t, 0:small] = qsum_ref[
                        t : t + 1, i * small : (i + 1) * small
                    ]

            pl.when(info[1] == i % 2)(functools.partial(put, keep_ref))
            pl.when(info[1] != i % 2)(functools.partial(put, give_ref))


def attn_back(gb, w, mixed, lse, accs, heads, tail_valid, own=False, finish=None, seq=None):
    crops, rows, width = gb.shape
    per = BACK_PER
    crop = functools.partial(block, per=per)
    args = [gb, w, mixed, lse, *accs]
    specs = [crop(gb.shape), once(w.shape), crop(mixed.shape), crop(lse.shape)]
    specs += [crop(a.shape) for a in accs]
    outs, scratch = [], []
    if finish is not None:
        info, begin, gmid, *tables = finish
        args += [info, begin, gmid, *tables]
        specs += [pl.BlockSpec(memory_space=pltpu.SMEM), crop(begin.shape), crop(gmid.shape)]
        specs += [once(x.shape) for x in tables]
        scratch.append(pltpu.VMEM((width // LANES, rows * crops, LANES), F32))
        scratch.append(pltpu.VMEM((rows + 16, width), F32))
    else:
        outs.append(((crops, rows, width), F32, crop))
    if own:
        outs += [((crops, rows, 3 * WIDE), BF16, crop), ((8, WIDE), F32, whole)]
    if finish is not None:
        outs += [
            ((seq * crops, width), F32, whole),
            ((2, rows + 16, width // 4), F32, whole),
            ((2, rows + 16, width // 4), F32, whole),
        ]
    return pl.pallas_call(
        functools.partial(
            attn_back_kernel,
            heads=heads,
            tail_valid=tail_valid,
            own=own,
            accs=len(accs),
            finish=finish is not None,
        ),
        grid=(crops // per,),
        in_specs=specs,
        out_specs=[kind(shape) for shape, _, kind in outs],
        out_shape=[jax.ShapeDtypeStruct(shape, dtype) for shape, dtype, _ in outs],
        scratch_shapes=scratch,
        compiler_params=params(),
        cost_estimate=cost(31 if finish is not None else 22),
        name="attention_back",
    )(*args)


def gelu_and_slope(h):
    phi = 0.5 * (1.0 + lax.erf(h * (2.0**-0.5)))
    bell = jnp.exp(-0.5 * h * h) * 0.3989422804014327
    return h * phi, phi + h * bell


def mlp_chain(n2, go, shards, accs, last):
    sums = []
    for i, (w1_ref, w2_ref, bias) in enumerate(shards):
        h = mm_nn(n2, w1_ref[...]) + bias[0:1, :]
        ga = mm_nt(go, w2_ref[...])
        yield
        a, slope = gelu_and_slope(h)
        a = a.astype(BF16)
        gh = ga * slope
        gh_low = gh.astype(BF16)
        pair = mm_nn(a, w2_ref[...]), mm_nt(gh_low, w1_ref[...])
        if i == 0:
            for one in accs:
                pair = tuple(x + y() for x, y in zip(pair, one))
        if i < 2:
            sums.append(pair)
        else:
            sums[1] = tuple(x + y for x, y in zip(sums[1], pair))
    yield
    out, gn = sums[0] if len(sums) == 1 else (x + y for x, y in zip(*sums))
    last(out, gn, a, gh, gh_low)


def place_mlp(info, pieces, w1_ref, w2_ref, bias_ref):
    place_pieces(info, pieces, w1_ref, 0, lambda j: j * PART)
    place_pieces(info, pieces, w2_ref, PART + 8, lambda j: j * PART)
    ref, slot = pieces[0]
    bias_ref[...] = ref[slot, PART : PART + 8, :]


def placed_mlp(width, hidden):
    return [((width, hidden), BF16), ((hidden, width), BF16), ((8, hidden), F32)]


def assemble_kernel(*refs):
    it = iter(refs)
    info, pieces = next(it), take_pieces(it, 4)
    place_mlp(info, pieces, *it)


def assemble(pieces, info, width, hidden):
    return pl.pallas_call(
        assemble_kernel,
        grid=(1,),
        in_specs=[pl.BlockSpec(memory_space=pltpu.SMEM)] + [once(x.shape) for x in pieces],
        out_specs=[once(shape) for shape, _ in placed_mlp(width, hidden)],
        out_shape=[jax.ShapeDtypeStruct(*x) for x in placed_mlp(width, hidden)],
        compiler_params=params(16 * 1024 * 1024),
        cost_estimate=cost(4),
        name="assemble",
    )(info, *pieces)


def mlp_kernel(*refs, ready, accs, own, finish):
    it = iter(refs)
    info, n2_ref, up_ref, vec_ref = (next(it) for _ in range(4))
    shards = [tuple(next(it) for _ in range(3)) for _ in range(ready)]
    pieces = take_pieces(it, 4)
    acc_refs = [(next(it), next(it)) for _ in range(accs)]
    if finish:
        begin_ref, br_ref = next(it), next(it)
        res_ref, gmid_ref, gb_ref, sum_ref = (next(it) for _ in range(4))
    else:
        out_ref, gn_ref = next(it), next(it)
    if own:
        a_ref, gh_ref, go_ref, hsum_ref = (next(it) for _ in range(4))
    first = pl.program_id(0) == 0
    placed = tuple(next(it) for _ in range(3))
    if finish:
        res_s = next(it)

    @pl.when(first)
    def _():
        place_mlp(info, pieces, *placed)

    if not own:
        shards.append(placed)
    per, rows, width = n2_ref.shape
    crops = 8
    many = []

    def last(i, up, grad_output, go, out, gn, a, gh, gh_low):
        if own:
            a_ref[i] = a
            go_ref[i] = go
            gh_ref[i] = gh_low
            many.append(jnp.concatenate([row_sum(gh), jnp.zeros((7, gh.shape[1]), F32)], 0))
        if not finish:
            out_ref[i] = out
            gn_ref[i] = gn
            return
        out = out + row(vec_ref, FC2_BIAS)
        branch = br_ref[i] + row(vec_ref, PROJ_BIAS)
        attn_scale = row(vec_ref, ATTN_SCALE)
        middle = begin_ref[i] + attn_scale * branch
        result = middle + row(vec_ref, MLP_SCALE) * out
        put_columns(res_s, pl.ds(pl.program_id(0) * per + i, rows, stride=crops), result)
        xhat, rstd = norm_parts(middle)
        gmid = up + norm_back(xhat, rstd, gn, row(vec_ref, PRE_MLP_GAIN))
        gmid_ref[i] = gmid
        gbr = gmid * attn_scale
        gb_ref[i] = gbr.astype(BF16)
        sums = (up * out, grad_output, gn * xhat, gn, gmid * branch, gbr)
        many.append(
            jnp.concatenate([row_sum(x) for x in sums] + [jnp.zeros((2, gn.shape[1]), F32)], 0)
        )

    chains = []
    for i in range(per):
        up = up_ref[i].astype(F32)
        grad_output = up * row(vec_ref, MLP_SCALE)
        go = grad_output.astype(BF16)
        held = [[lambda ref=ref, i=i: ref[i] for ref in pair] for pair in acc_refs]
        chains.append(
            mlp_chain(n2_ref[i], go, shards, held, functools.partial(last, i, up, grad_output, go))
        )
    interleave(chains)
    if many:
        ref = sum_ref if finish else hsum_ref
        sums = sum(many[1:], many[0])
        ref[...] = jnp.where(first, sums, ref[...] + sums)
    if not finish:
        return

    @pl.when(pl.program_id(0) == pl.num_programs(0) - 1)
    def _():
        seq = res_ref.shape[0]
        step = 29 if seq % 29 == 0 else 1

        def move(i, carry):
            src = pl.ds(pl.multiple_of(i * (step * crops), crops), step * crops)
            res_ref[pl.ds(i * step, step)] = get_columns(res_s, src).reshape(step, crops, -1).astype(BF16)
            return carry

        lax.fori_loop(0, seq // step, move, 0)


def mlp(n2, up, vecs, ready, pieces, info, accs, hidden, own=False, finish=None, seq=None):
    crops, rows, width = n2.shape
    per = MLP_PER
    crop = functools.partial(block, per=per)
    args, specs = [], []

    def add(x, spec):
        args.append(x)
        specs.append(spec)

    add(info, pl.BlockSpec(memory_space=pltpu.SMEM))
    add(n2, crop(n2.shape))
    add(up, crop(up.shape))
    add(vecs, once(vecs.shape))
    for w in sum(ready, ()):
        add(w, once(w.shape))
    for x in pieces:
        add(x, once(x.shape))
    for pair in accs:
        for a in pair:
            add(a, crop(a.shape))
    full = (crops, rows, width)
    scratch = []
    if finish is not None:
        add(finish[0], crop(finish[0].shape))
        add(finish[1], crop(finish[1].shape))
        outs = [
            ((seq, crops, width), BF16, once),
            (full, F32, crop),
            (full, BF16, crop),
            ((8, width), F32, whole),
        ]
        scratch.append(pltpu.VMEM((width // LANES, rows * crops, LANES), F32))
    else:
        outs = [(full, F32, crop), (full, F32, crop)]
    placed = placed_mlp(width, hidden)
    if own:
        outs += [((crops, rows, hidden), BF16, crop)] * 2 + [(full, BF16, crop), ((8, hidden), F32, whole)]
        outs += [(shape, dtype, once) for shape, dtype in placed]
    else:
        scratch = [pltpu.VMEM(shape, dtype) for shape, dtype in placed] + scratch
    return pl.pallas_call(
        functools.partial(mlp_kernel, ready=len(ready), accs=len(accs), own=own, finish=finish is not None),
        grid=(crops // per,),
        in_specs=specs,
        out_specs=[kind(shape) for shape, _, kind in outs],
        out_shape=[jax.ShapeDtypeStruct(shape, dtype) for shape, dtype, _ in outs],
        scratch_shapes=scratch,
        compiler_params=params(VMEM_LIMIT if own else VMEM_MOST),
        cost_estimate=cost(16 if own else 45),
        name="mlp",
    )(*args)


def weight_grad_kernel(*refs, parts, prepare):
    it = iter(refs)
    if prepare:
        info, pieces = next(it), take_pieces(it, 4)
    x1_ref, y1_ref, x2_ref, y2_ref, out_ref = (next(it) for _ in range(5))
    if prepare:

        @pl.when(pl.program_id(0) == 0)
        def _():
            place_mlp(info, pieces, *it)

    first, second = mm_tn(x1_ref[...], y1_ref[...]), mm_tn(x2_ref[...], y2_ref[...])
    out_ref[...] = jnp.concatenate([(first, second)[i][:, lo:hi] for i, lo, hi in parts], 1)


def weight_grads(x1, y1, x2, y2, parts, prepare=None):
    rows, width = x1.shape
    col = pl.BlockSpec((rows, WIDE), lambda i: (0, i))
    wide = sum(hi - lo for _, lo, hi in parts)
    args = [x1, y1, x2, y2]
    specs = [col, once(y1.shape), col, once(y2.shape)]
    outs = [pl.BlockSpec((WIDE, wide), lambda i: (i, 0))]
    shapes = [jax.ShapeDtypeStruct((width, wide), F32)]
    if prepare:
        info, pieces = prepare
        args = [info, *pieces, *args]
        specs = [pl.BlockSpec(memory_space=pltpu.SMEM)] + [once(x.shape) for x in pieces] + specs
        for shape, dtype in placed_mlp(width, y1.shape[1]):
            outs.append(once(shape))
            shapes.append(jax.ShapeDtypeStruct(shape, dtype))
    return pl.pallas_call(
        functools.partial(weight_grad_kernel, parts=parts, prepare=prepare is not None),
        grid=(width // WIDE,),
        in_specs=specs,
        out_specs=outs,
        out_shape=shapes,
        compiler_params=params(),
        cost_estimate=cost(10),
        name="weight_grads",
    )(*args)


def plane_perm(inner, outer, move):
    pairs = []
    for i in range(inner):
        for o in range(outer):
            j, r = move(i, o)
            pairs.append((i * outer + o, j * outer + r))
    return pairs


def after(x, *others):
    return lax.optimization_barrier((x, *others))[0] if others else x


def fence(new, *done):
    return lax.optimization_barrier((*new, *done))[: len(new)]


class PlaneSum:
    def __init__(self, sizes, inner, mine, give):
        _, self.inner_n, self.outer_n = sizes
        self.side = inner // 2
        self.inner = inner
        self.mine, self.give = mine, give

    def cores(self):
        self.one = lax.ppermute(self.give, "inner", [(i, i ^ 1) for i in range(self.inner_n)])
        return self.one

    def pick(self, side):
        at = side if self.mine.shape[0] == 2 else 2 * side + self.inner % 2
        return sum(lax.dynamic_index_in_dim(x, at, 0, keepdims=False) for x in (self.mine, self.one))

    def sides(self):
        self.two = lax.ppermute(
            self.pick(1 - self.side), "inner", [(i, i ^ 2) for i in range(self.inner_n)]
        )
        return self.two

    def total(self):
        return self.pick(self.side) + self.two


def sum_groups(x, outer_n):
    k = 1
    while k < outer_n:
        x = x + lax.ppermute(x, "outer", [(o, o ^ k) for o in range(outer_n)])
        k *= 2
    return x


def leave_kernel(x_ref, qkv_ref, proj_ref):
    side = proj_ref.shape[0]
    for t in range(3):
        qkv_ref[t] = x_ref[:, t * side : (t + 1) * side]
    proj_ref[...] = x_ref[:, 3 * side : 4 * side].T


def leave(x, side):
    rows = x.shape[0]
    return pl.pallas_call(
        leave_kernel,
        out_shape=[
            jax.ShapeDtypeStruct((3, rows, side), F32),
            jax.ShapeDtypeStruct((side, rows), F32),
        ],
        compiler_params=params(16 * 1024 * 1024),
        cost_estimate=cost(2),
        name="leave",
    )(x)


def per_device(
    sizes,
    tokens,
    patch_mask,
    cotangent,
    mask_token,
    pos_embed,
    pre_attn_gain,
    pre_attn_bias,
    qkv_weight,
    qv_bias,
    proj_weight,
    proj_bias,
    attn_scale,
    pre_mlp_gain,
    pre_mlp_bias,
    fc1_weight,
    fc1_bias,
    fc2_weight,
    fc2_bias,
    mlp_scale,
):
    tensor_n, inner_n, outer_n = sizes
    crops, seq, width = tokens.shape
    head_width = qkv_weight.shape[2]
    heads = head_width // HEAD_DIM
    hidden = fc1_weight.shape[1]
    rows = -(-seq // 16) * 16
    tail_valid = seq - MAIN
    t = lax.axis_index("tensor")
    inner = lax.axis_index("inner")
    outer = lax.axis_index("outer")
    place = inner * 2 + outer % 2
    info = jnp.stack([place, inner % 2]).astype(jnp.int32)

    qkv_rows = qkv_weight.transpose(1, 2, 0).reshape(3 * head_width, width)

    def eighth(x):
        return lax.dynamic_slice_in_dim(x, place * PART, PART, 0).astype(F32)

    ones = jnp.ones((heads,), F32)
    zeros = jnp.zeros((WIDE,), F32)
    attn_bias = jnp.concatenate(
        [qv_bias[0], zeros[head_width:], zeros, qv_bias[1], ones, zeros[head_width + heads :]]
    )[None, :]
    mlp_bias = fc1_bias[None, :]
    below = jnp.zeros((7, width), F32)
    attn_piece = jnp.concatenate(
        [eighth(jnp.concatenate([qkv_rows, proj_weight], 0)), attn_bias, below], 0
    )
    mlp_piece = jnp.concatenate([eighth(fc1_weight), mlp_bias, below, eighth(fc2_weight)], 0)
    cut_1, cut_2 = 104, 72
    perms = (
        plane_perm(inner_n, outer_n, lambda i, o: (i, o ^ 1) if i % 2 else (i ^ 2, o)),
        plane_perm(inner_n, outer_n, lambda i, o: (i ^ 2, o) if i % 2 else (i, o ^ 1)),
        plane_perm(inner_n, outer_n, lambda i, o: (i ^ 1, o)),
    )
    def over_z(x, k):
        return lax.ppermute(x, "tensor", [(i, i ^ k) for i in range(tensor_n)])

    along, far, peer = (functools.partial(lax.ppermute, axis_name=PLANE, perm=p) for p in perms)

    vecs = jnp.stack(
        [
            mask_token,
            pre_attn_gain,
            pre_attn_bias,
            proj_bias,
            attn_scale,
            pre_mlp_gain,
            pre_mlp_bias,
            fc2_bias,
            mlp_scale,
        ]
    )
    run = functools.partial(attn, heads=heads, tail_valid=tail_valid)
    layer = functools.partial(mlp, hidden=hidden)

    quarter = width // inner_n

    def plane_sum(x):
        x = x.reshape(inner_n, quarter, -1)
        return PlaneSum(sizes, inner, x, x)

    def pair(first, second):
        return jnp.stack([first, second])

    a1, a2 = over_z(attn_piece, 1), over_z(attn_piece, 2)
    begin, n1 = enter(tokens.transpose(1, 0, 2), patch_mask, vecs, pos_embed, rows)

    n1, a1, a2 = fence((n1, a1, a2))
    b1, b2 = along(a1), along(a2)
    a3 = over_z(a2, 1)
    half = crops // 2
    own_w = [attn_bias, qkv_rows, proj_weight]
    early = run(n1, own_w, None, [], span=(0, half))

    both1 = pair(a1, b1)
    cot, both1, a3, m1_piece = fence(
        (cotangent.transpose(1, 0, 2), both1, a3, mlp_piece[:cut_1]), early[0], b2
    )
    c1, d1 = far(both1), peer(both1)
    m1_hi = over_z(m1_piece, 1)
    up = upstream(cot, rows)

    both2 = pair(a2, b2)
    n1, c1, both2, a3, m1_piece, m2_piece = fence(
        (n1, c1, both2, a3, mlp_piece[cut_1:], mlp_piece[:cut_2]), up, d1, m1_hi
    )
    e1 = peer(c1)
    c2 = far(both2)
    b3 = along(a3)
    m1_lo = over_z(m1_piece, 1)
    m2_hi = over_z(m2_piece, 2)
    br0, mix0, lse0, w_0, att0 = run(n1, own_w, None, [], span=(half, crops), into=early)

    both3, four2 = pair(a3, b3), jnp.concatenate([both2, c2], 0)
    m1 = jnp.concatenate([m1_hi, m1_lo], 0)
    n1, four2, both3, m1, m2_piece = fence(
        (n1, four2, both3, m1, mlp_piece[cut_2:]), br0, e1, m2_hi
    )
    de2 = peer(four2)
    c3 = far(both3)
    f1 = along(m1)
    m2_lo = over_z(m2_piece, 2)
    br1, mix1, lse1, w_1 = run(n1, [both1, c1, d1, e1], info, [br0])

    four3, two1 = jnp.concatenate([both3, c3], 0), pair(m1, f1)
    m2 = jnp.concatenate([m2_hi, m2_lo], 0)
    n1, four3, two1, m2 = fence((n1, four3, two1, m2), br1, de2)
    de3 = peer(four3)
    g1, h1 = far(two1), peer(two1)
    m3 = over_z(m2, 1)
    br2, mix2, lse2, w_2 = run(n1, [four2, de2], info, [])

    n1, g1, m2, m3 = fence((n1, g1, m2, m3), br2, de3, h1)
    i1 = peer(g1)
    f2, f3 = along(m2), along(m3)
    br, mix3, lse3, w_3, n2 = run(n1, [four3, de3], info, [br2, br1], finish=(begin, vecs))

    two2, two3 = pair(m2, f2), pair(m3, f3)
    n2, two2, two3 = fence((n2, two2, two3), i1)
    g2, h2 = far(two2), peer(two2)
    own_mlp = (fc1_weight, fc2_weight, mlp_bias)
    out0, gn0, a0, gh0, go0, hsum, *mlp_1 = layer(
        n2, up, vecs, [own_mlp], [two1, g1, h1, i1], info, [], own=True
    )

    flat = lambda x: x.reshape(crops * rows, -1)
    n2, g2, two3 = fence((n2, g2, two3), out0, h2)
    i2 = peer(g2)
    g3, h3 = far(two3), peer(two3)
    (mlp_grads,) = weight_grads(
        flat(n2), flat(gh0), flat(go0), flat(a0), ((0, 0, hidden), (1, 0, hidden))
    )

    n2, g3, mlp_grads = fence((n2, g3, mlp_grads), i2, h3)
    i3 = peer(g3)
    mlp_2 = assemble([two2, g2, h2, i2], info, width, hidden)
    n2, mlp_grads = fence((n2, mlp_grads), i3, mlp_2[0])

    mlp_sum = plane_sum(mlp_grads)
    s1 = mlp_sum.cores()
    result, gmid, gb, mid_sums = layer(
        n2,
        up,
        vecs,
        [tuple(mlp_1), tuple(mlp_2)],
        [two3, g3, h3, i3],
        info,
        [(out0, gn0)],
        finish=(begin, br),
        seq=seq,
    )

    back = functools.partial(attn_back, heads=heads, tail_valid=tail_valid)
    gb, mlp_sum.one = fence((gb, s1))
    s2 = mlp_sum.sides()
    gn0, gm0, qv_sums = back(gb, w_0, mix0, lse0, [], own=True)
    (attn_grads,) = weight_grads(
        flat(n1),
        flat(gm0),
        flat(gb),
        flat(att0),
        tuple((0, i * WIDE, i * WIDE + head_width) for i in range(3)) + ((1, 0, head_width),),
    )

    gb, attn_grads, mlp_sum.two = fence((gb, attn_grads, s2))
    attn_sum = plane_sum(attn_grads)
    s1 = attn_sum.cores()
    mlp_total = mlp_sum.total()
    grad_fc1 = sum_groups(mlp_total[:, :hidden], outer_n)
    (gn1,) = back(gb, w_1, mix1, lse1, [gn0])

    gb, attn_sum.one, rest = fence((gb, s1, mlp_total[:, hidden:]), gn1, grad_fc1)
    s2 = attn_sum.sides()
    grad_fc2 = sum_groups(rest, outer_n)
    (gn2,) = back(gb, w_2, mix2, lse2, [])

    gb, attn_sum.two = fence((gb, s2), gn2, grad_fc2)
    shares_attn = sum_groups(attn_sum.total(), outer_n)
    gtok, keep, give = back(
        gb,
        w_3,
        mix3,
        lse3,
        [gn2, gn1],
        finish=(info, begin, gmid, patch_mask, vecs, mid_sums, hsum, qv_sums),
        seq=seq,
    )

    small = head_width // inner_n
    small_sum = PlaneSum(sizes, inner, keep, after(give, shares_attn))
    small_sum.cores()
    small_sum.sides()
    small_sums = sum_groups(small_sum.total(), outer_n)
    grad_qkv, grad_proj = leave(shares_attn, head_width)
    mid = lambda i: small_sums[rows + i]
    vec = lambda i: small_sums[rows + 8 + i]
    return (
        result.transpose(1, 0, 2),
        gtok.reshape(seq, crops, width).transpose(1, 0, 2),
        vec(2),
        small_sums[:seq],
        vec(0),
        vec(1),
        grad_qkv.transpose(1, 0, 2),
        jnp.stack([vec(4)[:small], vec(5)[:small]]),
        grad_proj,
        mid(5),
        mid(4),
        mid(2),
        mid(3),
        grad_fc1,
        vec(3),
        grad_fc2.T,
        mid(1),
        mid(0),
    )


def solution(mesh):
    in_specs = (
        P(("inner", "outer"), None, None),
        P(("inner", "outer"), None),
        P(("inner", "outer"), None, None),
        P(),
        P(),
        P(),
        P(),
        P(None, None, "tensor"),
        P(None, "tensor"),
        P("tensor", None),
        P(),
        P(),
        P(),
        P(),
        P(None, "tensor"),
        P("tensor"),
        P("tensor", None),
        P(),
        P(),
    )
    out_specs = (
        P(("inner", "outer"), None, None),
        P(("inner", "outer"), None, None),
        P("inner"),
        P(None, "inner"),
        P("inner"),
        P("inner"),
        P("inner", None, "tensor"),
        P(None, ("tensor", "inner")),
        P("tensor", "inner"),
        P("inner"),
        P("inner"),
        P("inner"),
        P("inner"),
        P("inner", "tensor"),
        P(("tensor", "inner")),
        P("tensor", "inner"),
        P("inner"),
        P("inner"),
    )
    sizes = tuple(mesh.shape[name] for name in ("tensor", "inner", "outer"))
    return jax.shard_map(
        functools.partial(per_device, sizes),
        mesh=mesh,
        in_specs=in_specs,
        out_specs=out_specs,
        check_vma=False,
    )
```

```python
import functools

import jax
import jax.numpy as jnp
from jax import lax
from jax.experimental import pallas as pl
from jax.experimental.pallas import tpu as pltpu
from jax.sharding import PartitionSpec as P

HEAD_DIM = 64
EPS = 1e-06
F32 = jnp.float32
BF16 = jnp.bfloat16
NEG = -1e30
LANES = 128
WIDE = 256
MAIN = 256
MIB = 1024 * 1024
ENTER_MEM, ATTN_MEM, MLP_MEM, GRAD_MEM, BACK_MEM, LAST_MEM = 50, 50, 50, 50, 50, 50
VMEM_MOST = 60
PLANE = ("inner", "outer")
PART = 96


def mm_nt(a, b):
    return lax.dot_general(a, b, (((1,), (1,)), ((), ())), preferred_element_type=F32)


def mm_nn(a, b):
    return lax.dot_general(a, b, (((1,), (0,)), ((), ())), preferred_element_type=F32)


def mm_tn(a, b):
    return lax.dot_general(a, b, (((0,), (0,)), ((), ())), preferred_element_type=F32)


ATTN_PER, BACK_PER, MLP_PER = 2, 2, 2


def cost(us):
    return pl.CostEstimate(flops=int(us * 1.15e9), bytes_accessed=1 << 20, transcendentals=0)


(
    MASK_TOKEN,
    PRE_ATTN_GAIN,
    PRE_ATTN_BIAS,
    PROJ_BIAS,
    ATTN_SCALE,
    PRE_MLP_GAIN,
    PRE_MLP_BIAS,
    FC2_BIAS,
    MLP_SCALE,
) = range(9)


def row(ref, i):
    return ref[i : i + 1, :]


def params(limit):
    return pltpu.CompilerParams(vmem_limit_bytes=limit * MIB)


def block(shape, per=1):
    return pl.BlockSpec((per,) + tuple(shape[1:]), lambda c: (c,) + (0,) * (len(shape) - 1))


def whole(shape):
    return pl.BlockSpec(tuple(shape), lambda c: (0,) * len(shape))


def once(shape):
    return pl.BlockSpec(tuple(shape), lambda c: (0,) * len(shape), pipeline_mode=pl.Buffered(1))


def row_sum(x):
    return jnp.sum(x, 0, keepdims=True)


def norm_parts(v):
    center = v - jnp.mean(v, -1, keepdims=True)
    rstd = lax.rsqrt(jnp.mean(center * center, -1, keepdims=True) + EPS)
    return center * rstd, rstd


def norm_back(xhat, rstd, u, gain):
    gu = u * gain
    return (
        gu - jnp.mean(gu, -1, keepdims=True) - xhat * jnp.mean(gu * xhat, -1, keepdims=True)
    ) * rstd


def put_columns(ref, rows, x):
    for j in range(ref.shape[0]):
        ref[j, rows, :] = x[:, j * LANES : (j + 1) * LANES]


def get_columns(ref, rows):
    return jnp.concatenate([ref[j, rows, :] for j in range(ref.shape[0])], 1)


def flag_lanes(mask_ref, crop, rows, prefix):
    crop_mask = mask_ref[pl.ds(crop, 1), :]
    patches = crop_mask.shape[1]
    ones = jnp.broadcast_to((crop_mask == 1).astype(F32), (LANES, patches)).astype(BF16)
    token = lax.broadcasted_iota(jnp.int32, (rows, patches), 0)
    patch = lax.broadcasted_iota(jnp.int32, (rows, patches), 1)
    return mm_nt((token == patch + prefix).astype(F32).astype(BF16), ones)


def flag_wide(mask_ref, crop, rows, prefix, width):
    return jnp.concatenate([flag_lanes(mask_ref, crop, rows, prefix)] * (width // LANES), 1) > 0.5


def by_crop(src_ref, scratch):
    seq, crops, _ = src_ref.shape
    step = 29 if seq % 29 == 0 else 1

    @pl.when(pl.program_id(0) == 0)
    def _():
        def move(i, carry):
            dst = pl.ds(pl.multiple_of(i * (step * crops), crops), step * crops)
            put_columns(scratch, dst, src_ref[pl.ds(i * step, step)].astype(F32).reshape(step * crops, -1))
            return carry

        lax.fori_loop(0, seq // step, move, 0)
        scratch[:, seq * crops :, :] = jnp.zeros_like(scratch[:, seq * crops :, :])

    return get_columns(scratch, pl.ds(pl.program_id(0), scratch.shape[1] // crops, stride=crops))


def enter_kernel(info, tok_ref, mask_ref, vec_ref, pos_ref, w1_ref, w2_ref, bias_ref, *refs, chunks):
    begin_ref, n1_ref, *chunk_refs, scratch = refs

    @pl.when(pl.program_id(0) == 0)
    def _():
        mine = pl.ds(pl.multiple_of(info[0] * PART, 32), PART)
        hidden = w1_ref.shape[1]
        below = jnp.zeros((7, hidden), F32)
        piece = [w1_ref[mine, :].astype(F32), bias_ref[...], below, w2_ref[mine, :].astype(F32)]
        piece = jnp.concatenate(piece, 0)
        for (lo, hi), ref in zip(chunks, chunk_refs):
            ref[...] = piece[lo:hi]

    tok = by_crop(tok_ref, scratch)
    rows = tok.shape[0]
    near = pos_ref.shape[0] // 8 * 8
    rest = pos_ref.shape[0] - near
    pos = [pos_ref[0:near, :]]
    if rest:
        pos.append(jnp.concatenate([pos_ref[near:, :], jnp.zeros((8 - rest, tok.shape[1]), F32)], 0))
    pos.append(jnp.zeros((rows - near - 8 * (rest > 0), tok.shape[1]), F32))
    pos = jnp.concatenate(pos, 0)
    prefix = tok_ref.shape[0] - mask_ref.shape[1]
    flagged = flag_wide(mask_ref, pl.program_id(0), rows, prefix, tok.shape[1])
    begin = jnp.where(flagged, row(vec_ref, MASK_TOKEN), tok) + pos
    begin_ref[0] = begin
    xhat, _ = norm_parts(begin)
    n1_ref[0] = (xhat * row(vec_ref, PRE_ATTN_GAIN) + row(vec_ref, PRE_ATTN_BIAS)).astype(BF16)


def enter(info, tok, mask, vecs, pos, rows, own_mlp, chunks):
    seq, crops, width = tok.shape
    shape = (crops, rows, width)
    args = (tok, mask, vecs, pos, *own_mlp)
    small = [(hi - lo, width) for lo, hi in chunks]
    return pl.pallas_call(
        functools.partial(enter_kernel, chunks=chunks),
        grid=(crops,),
        in_specs=[pl.BlockSpec(memory_space=pltpu.SMEM)] + [once(x.shape) for x in args],
        out_specs=[block(shape)] * 2 + [once(x) for x in small],
        out_shape=[
            jax.ShapeDtypeStruct(shape, F32),
            jax.ShapeDtypeStruct(shape, BF16),
            *(jax.ShapeDtypeStruct(x, F32) for x in small),
        ],
        scratch_shapes=[pltpu.VMEM((width // LANES, rows * crops, LANES), F32)],
        compiler_params=params(ENTER_MEM),
        cost_estimate=cost(7),
        name="enter",
    )(info, *args)


def upstream_kernel(cot_ref, up_ref, scratch):
    up_ref[0] = by_crop(cot_ref, scratch).astype(BF16)


def upstream(cot, rows):
    seq, crops, width = cot.shape
    shape = (crops, rows, width)
    return pl.pallas_call(
        upstream_kernel,
        grid=(crops,),
        in_specs=[once(cot.shape)],
        out_specs=block(shape),
        out_shape=jax.ShapeDtypeStruct(shape, BF16),
        scratch_shapes=[pltpu.VMEM((width // LANES, rows * crops, LANES), F32)],
        compiler_params=params(ENTER_MEM),
        cost_estimate=cost(6),
        name="upstream",
    )(cot)


def by_token_kernel(*refs):
    arrays = (len(refs) - 1) // 2
    scratch = refs[-1]
    for x_ref, out_ref in zip(refs[:arrays], refs[arrays:-1]):
        crops, step, _ = x_ref.shape
        for c in range(crops):
            put_columns(scratch, pl.ds(c, step, stride=crops), x_ref[c].astype(F32))
        out = get_columns(scratch, slice(None))
        out_ref[...] = out.reshape(out_ref.shape).astype(out_ref.dtype)


def by_token(arrays, seq):
    crops, rows, width = arrays[0].shape
    step = 48
    return pl.pallas_call(
        by_token_kernel,
        grid=(-(-seq // step),),
        in_specs=[pl.BlockSpec((crops, step, width), lambda i: (0, i, 0))] * len(arrays),
        out_specs=[pl.BlockSpec((step, crops, width), lambda i: (i, 0, 0))] * len(arrays),
        out_shape=[jax.ShapeDtypeStruct((seq, crops, width), x.dtype) for x in arrays],
        scratch_shapes=[pltpu.VMEM((width // LANES, step * crops, LANES), F32)],
        compiler_params=params(VMEM_MOST),
        cost_estimate=cost(8),
        name="by_token",
    )(*arrays)


def head_masks(heads):
    lane = lax.broadcasted_iota(jnp.int32, (1, WIDE), 1)
    return [((lane // HEAD_DIM) == h).astype(F32) for h in range(heads)], lane


def per_head_rows(x, masks):
    parts = [x * m for m in masks]
    parts.append(jnp.zeros((LANES - 8 * len(masks), x.shape[1]), F32))
    return jnp.concatenate(parts, 0).astype(BF16)


def pick(index, parts):
    out = parts[-1]
    for h in range(len(parts) - 2, -1, -1):
        out = jnp.where(index == h, parts[h], out)
    return out


def interleave(chains):
    live, waiting = [], list(chains)
    while live or waiting:
        live += waiting[:1]
        del waiting[:1]
        live = [c for c in live[::-1] if next(c, True) is None][::-1]


def by_head(x, heads):
    rows = x.shape[0] // heads
    return [x[h * rows : (h + 1) * rows] for h in range(heads)]


def attention_forward(n1, w_ref, bias, heads, tail_valid, last):
    masks, lane = head_masks(heads)
    low = [m.astype(BF16) for m in masks]
    head_width = heads * HEAD_DIM
    mixed = (mm_nt(n1, w_ref[0 : 3 * WIDE, :]) + bias).astype(BF16)
    yield
    q = mixed[:, 0:WIDE] * jnp.asarray(HEAD_DIM**-0.5, BF16)
    k, v = mixed[:, WIDE : 2 * WIDE], mixed[:, 2 * WIDE : 3 * WIDE]
    mixed = jnp.concatenate([q, k, v], 1)
    k_main, v_main = k[0:MAIN], v[0:MAIN]
    v_masks = [m + (lane == head_width + h).astype(F32) for h, m in enumerate(masks)]
    k_tail = per_head_rows(k[MAIN : MAIN + 8].astype(F32), masks)
    v_tail = per_head_rows(v[MAIN : MAIN + 8].astype(F32), v_masks)
    col = lax.broadcasted_iota(jnp.int32, (1, LANES), 1)
    valid = (col < 8 * heads) & ((col % 8) < tail_valid)
    qs = jnp.concatenate([q * m for m in low], 0)
    vs = jnp.concatenate([v_main * m.astype(BF16) for m in v_masks] + [v_tail], 0)
    yield
    s_tail = mm_nt(q, k_tail)
    scores = by_head(mm_nt(qs, k_main), heads)
    yield
    s_tail = jnp.where(valid, s_tail, NEG)
    tops, exps = [], []
    for h, s in enumerate(scores):
        top = jnp.where((col // 8) == h, s_tail, NEG)
        for i in range(MAIN // LANES):
            top = jnp.maximum(top, s[:, i * LANES : (i + 1) * LANES])
        top = jnp.max(top, -1, keepdims=True)
        tops.append(top)
        exps.append(jnp.exp(s - top).astype(BF16))
    exps.append(jnp.exp(s_tail - pick(col // 8, tops)).astype(BF16))
    yield
    total = mm_nn(jnp.concatenate(exps, 1), vs)
    yield
    sums = [total[:, head_width + h : head_width + h + 1] for h in range(heads)]
    scale = pick(lane // HEAD_DIM, [1.0 / s for s in sums])
    attended = (total * scale).astype(BF16)
    log_total = pick(col, [t + jnp.log(s) for t, s in zip(tops, sums)])
    yield
    branch = mm_nn(attended, w_ref[3 * WIDE : 4 * WIDE, :])
    yield
    last(mixed, log_total, attended, branch)


def take_pieces(it, count):
    return [(ref, i) for ref in (next(it) for _ in range(count)) for i in range(ref.shape[0])]


def place_pieces(info_ref, pieces, out_ref, base, first):
    p, core = info_ref[0], info_ref[1]
    q = p ^ 2
    a_bit = jnp.where(core == 0, 4, 1)
    b_bit = 5 - a_bit
    idents = (p, p ^ a_bit, p ^ b_bit, p ^ 5, q, q ^ b_bit, q ^ a_bit, q ^ 5)
    for (ref, slot), ident in zip(pieces, idents, strict=True):
        dst = pl.multiple_of(first(ident), 32)
        out_ref[pl.ds(dst, PART), :] = ref[slot, base : base + PART, :].astype(BF16)


def attn_kernel(*refs, heads, tail_valid, own, into, accs, finish, gathers):
    it = iter(refs)
    if own:
        n1_ref, bias_ref, qkv_ref, proj_ref = (next(it) for _ in range(4))
        bias = bias_ref[...]
    else:
        info, n1_ref = next(it), next(it)
        pieces = take_pieces(it, gathers)
        bias = pieces[0][0][0, PART : PART + 1, :]
    acc_refs = [next(it) for _ in range(accs)]
    if finish:
        begin_ref, vec_ref = next(it), next(it)
    for _ in range(into):
        next(it)
    br_ref, mix_ref, lse_ref, w_ref = (next(it) for _ in range(4))

    @pl.when(pl.program_id(0) == 0)
    def _():
        width = heads * HEAD_DIM
        for i in range(4):
            w_ref[i * WIDE + width : (i + 1) * WIDE, :] = jnp.zeros((WIDE - width, w_ref.shape[1]), BF16)
        if own:
            for i in range(3):
                w_ref[i * WIDE : i * WIDE + width, :] = qkv_ref[i * width : (i + 1) * width, :]
            w_ref[3 * WIDE : 3 * WIDE + width, :] = proj_ref[...]
        else:
            place_pieces(info, pieces, w_ref, 0, lambda i: (i >> 1) * WIDE + (i & 1) * PART)

    att_ref = next(it) if own else None
    n2_ref = next(it) if finish else None

    def last(i, mixed, log_total, attended, branch):
        mix_ref[i] = mixed
        lse_ref[i] = log_total
        if own:
            att_ref[i] = attended
        for ref in acc_refs:
            branch = branch + ref[i]
        br_ref[i] = branch
        if finish:
            middle = begin_ref[i] + row(vec_ref, ATTN_SCALE) * (branch + row(vec_ref, PROJ_BIAS))
            xhat, _ = norm_parts(middle)
            n2 = xhat * row(vec_ref, PRE_MLP_GAIN) + row(vec_ref, PRE_MLP_BIAS)
            n2_ref[i] = n2.astype(BF16)

    interleave(
        [
            attention_forward(n1_ref[i], w_ref, bias, heads, tail_valid, functools.partial(last, i))
            for i in range(n1_ref.shape[0])
        ]
    )


def attn(n1, weights, info, accs, heads, tail_valid, finish=None, span=None, into=()):
    crops, rows, width = n1.shape
    own = info is None
    lo, hi = span or (0, crops)
    args, specs = [], []

    per = ATTN_PER

    def crop(shape):
        at = lambda c: (c + lo // per,) + (0,) * (len(shape) - 1)
        return pl.BlockSpec((per,) + tuple(shape[1:]), at)

    def add(x, spec):
        args.append(x)
        specs.append(spec)

    if not own:
        add(info, pl.BlockSpec(memory_space=pltpu.SMEM))
    add(n1, crop(n1.shape))
    for w in weights:
        add(w, once(w.shape))
    for a in accs:
        add(a, crop(a.shape))
    if finish is not None:
        add(finish[0], crop(finish[0].shape))
        add(finish[1], once(finish[1].shape))
    outs = [
        ((crops, rows, width), F32, crop),
        ((crops, rows, 3 * WIDE), BF16, crop),
        ((crops, rows, LANES), F32, crop),
        ((4 * WIDE, width), BF16, whole),
    ]
    if own:
        outs.append(((crops, rows, WIDE), BF16, crop))
    if finish is not None:
        outs.append(((crops, rows, width), BF16, crop))
    aliases = {}
    for i, x in enumerate(into):
        if outs[i][2] is crop:
            aliases[len(args)] = i
            add(x, pl.BlockSpec(memory_space=pl.ANY))
    return pl.pallas_call(
        functools.partial(
            attn_kernel,
            heads=heads,
            tail_valid=tail_valid,
            own=own,
            gathers=len(weights),
            into=len(aliases),
            accs=len(accs),
            finish=finish is not None,
        ),
        grid=((hi - lo) // per,),
        in_specs=specs,
        out_specs=[kind(shape) for shape, _, kind in outs],
        out_shape=[jax.ShapeDtypeStruct(shape, dtype) for shape, dtype, _ in outs],
        input_output_aliases=aliases,
        compiler_params=params(ATTN_MEM),
        cost_estimate=cost((21 if finish is not None else 16) * (hi - lo) / crops),
        name="attention",
    )(*args)


def attention_backward(gb, w_ref, mix, lse_in, heads, tail_valid, last):
    masks, lane = head_masks(heads)
    low = [m.astype(BF16) for m in masks]
    da = mm_nt(gb, w_ref[3 * WIDE : 4 * WIDE, :])
    q, k, v = (mix[:, i * WIDE : (i + 1) * WIDE] for i in range(3))
    k_main, v_main = k[0:MAIN], v[0:MAIN]
    k_tail = per_head_rows(k[MAIN : MAIN + 8].astype(F32), masks)
    v_tail = per_head_rows(v[MAIN : MAIN + 8].astype(F32), masks)
    qs = jnp.concatenate([q * m for m in low], 0)
    s_tail = mm_nt(q, k_tail)
    scores = by_head(mm_nt(qs, k_main), heads)
    yield
    da = da.astype(BF16)
    das = jnp.concatenate([da * m for m in low], 0)
    col = lax.broadcasted_iota(jnp.int32, (1, LANES), 1)
    valid = (col < 8 * heads) & ((col % 8) < tail_valid)
    lse = [lse_in[:, h : h + 1] for h in range(heads)]
    p_tail = jnp.where(valid, jnp.exp(s_tail - pick(col // 8, lse)), 0.0)
    ps = [jnp.exp(s - t) for s, t in zip(scores, lse)]
    yield
    dp_tail = mm_nt(da, v_tail)
    dps = by_head(mm_nt(das, v_main), heads)
    yield
    x_tail = p_tail * dp_tail
    deltas, dss = [], []
    for h, (p, dp) in enumerate(zip(ps, dps)):
        x = p * dp
        delta = jnp.where((col // 8) == h, x_tail, 0.0)
        for i in range(MAIN // LANES):
            delta = delta + x[:, i * LANES : (i + 1) * LANES]
        delta = jnp.sum(delta, -1, keepdims=True)
        deltas.append(delta)
        dss.append((p * (dp - delta)).astype(BF16))
    ds_tail = (p_tail * (dp_tail - pick(col // 8, deltas))).astype(BF16)
    pbs = jnp.concatenate([p.astype(BF16) for p in ps], 0)
    pb_tail = p_tail.astype(BF16)
    ks = jnp.concatenate([k_main * m for m in low] + [k_tail], 0)
    yield
    dq = mm_nn(jnp.concatenate(dss + [ds_tail], 1), ks)
    dk, dv = mm_tn(jnp.concatenate(dss, 0), qs), mm_tn(pbs, das)
    dk_tail = mm_tn(ds_tail, q)
    dv_tail = mm_tn(pb_tail, da)
    yield
    dq = dq * (HEAD_DIM**-0.5)
    dk_tail = sum(dk_tail[8 * h : 8 * h + 8] * masks[h] for h in range(heads))
    dv_tail = sum(dv_tail[8 * h : 8 * h + 8] * masks[h] for h in range(heads))
    rest = jnp.zeros((gb.shape[0] - MAIN - 8, WIDE), F32)
    dk = jnp.concatenate([dk, dk_tail, rest], 0)
    dv = jnp.concatenate([dv, dv_tail, rest], 0)
    gm = jnp.concatenate([dq, dk, dv], 1).astype(BF16)
    yield
    gn = mm_nn(gm, w_ref[0 : 3 * WIDE, :])
    yield
    last(dq, dv, gm, gn)


def attn_back_kernel(*refs, heads, tail_valid, own, accs, finish):
    it = iter(refs)
    gb_ref, w_ref, mix_ref, lse_ref = (next(it) for _ in range(4))
    acc_refs = [next(it) for _ in range(accs)]
    if finish:
        info, begin_ref, gmid_ref, mask_ref, vec_ref = (next(it) for _ in range(5))
        mid_ref, hsum_ref, qsum_ref = (next(it) for _ in range(3))
    else:
        gn_ref = next(it)
    if own:
        gm_ref, sum_ref = next(it), next(it)
    if finish:
        gtok_ref, keep_ref, give_ref, pack = (next(it) for _ in range(4))
    first = pl.program_id(0) == 0
    per, rows, width = gb_ref.shape
    many, positions = [], []

    def last(i, dq, dv, gm, gn):
        if own:
            gm_ref[i] = gm
            many.append(jnp.concatenate([row_sum(dq), row_sum(dv), jnp.zeros((6, WIDE), F32)], 0))
        for ref in acc_refs:
            gn = gn + ref[i]
        if not finish:
            gn_ref[i] = gn
            return
        xhat, rstd = norm_parts(begin_ref[i])
        grad_begin = gmid_ref[i] + norm_back(xhat, rstd, gn, row(vec_ref, PRE_ATTN_GAIN))
        crop = pl.program_id(0) * per + i
        flagged = flag_wide(mask_ref, crop, rows, MAIN + tail_valid - mask_ref.shape[1], width)
        cleared = jnp.where(flagged, 0.0, grad_begin)
        gtok_ref[i] = cleared
        many.append(
            jnp.concatenate([row_sum(gn * xhat), row_sum(gn), row_sum(grad_begin - cleared)], 0)
        )
        positions.append(grad_begin)

    interleave(
        [
            attention_backward(
                gb_ref[i], w_ref, mix_ref[i], lse_ref[i], heads, tail_valid, functools.partial(last, i)
            )
            for i in range(per)
        ]
    )
    sums, grad_pos = (sum(x[1:], x[0]) if x else None for x in (many, positions))
    if own:
        sum_ref[...] = jnp.where(first, sums, sum_ref[...] + sums)
    if not finish:
        return
    after_mid = rows + 8

    @pl.when(first)
    def _():
        pack[0:rows, :] = grad_pos
        pack[after_mid : after_mid + 3, :] = sums

    @pl.when(jnp.logical_not(first))
    def _():
        pack[0:rows, :] += grad_pos
        pack[after_mid : after_mid + 3, :] += sums

    @pl.when(pl.program_id(0) == pl.num_programs(0) - 1)
    def _():
        pack[rows:after_mid, :] = mid_ref[...]
        pack[after_mid + 3 : after_mid + 4, :] = hsum_ref[0:1, :]
        quarter = width // 4
        small = heads * HEAD_DIM // 4
        deep = keep_ref.shape[1]
        for i in range(4):
            for t in range(2):
                pack[after_mid + 4 + t : after_mid + 5 + t, i * quarter : i * quarter + small] = qsum_ref[
                    t : t + 1, i * small : (i + 1) * small
                ]
        for i in range(4):

            def put(ref):
                part = pack[:, i * quarter : (i + 1) * quarter]
                ref[i // 2] = jnp.concatenate([part[j * deep : (j + 1) * deep] for j in range(4)], 1)

            pl.when(info[1] == i % 2)(functools.partial(put, keep_ref))
            pl.when(info[1] != i % 2)(functools.partial(put, give_ref))


def attn_back(gb, w, mixed, lse, accs, heads, tail_valid, own=False, finish=None):
    crops, rows, width = gb.shape
    per = BACK_PER
    crop = functools.partial(block, per=per)
    args = [gb, w, mixed, lse, *accs]
    specs = [crop(gb.shape), once(w.shape), crop(mixed.shape), crop(lse.shape)]
    specs += [crop(a.shape) for a in accs]
    outs, scratch = [], []
    if finish is not None:
        info, begin, gmid, *tables = finish
        args += [info, begin, gmid, *tables]
        specs += [pl.BlockSpec(memory_space=pltpu.SMEM), crop(begin.shape), crop(gmid.shape)]
        specs += [once(x.shape) for x in tables]
        scratch.append(pltpu.VMEM((rows + 16, width), F32))
    else:
        outs.append(((crops, rows, width), F32, crop))
    if own:
        outs += [((crops, rows, 3 * WIDE), BF16, crop), ((8, WIDE), F32, whole)]
    if finish is not None:
        outs += [
            ((crops, rows, width), F32, crop),
            ((2, (rows + 16) // 4, width), F32, whole),
            ((2, (rows + 16) // 4, width), F32, whole),
        ]
    return pl.pallas_call(
        functools.partial(
            attn_back_kernel,
            heads=heads,
            tail_valid=tail_valid,
            own=own,
            accs=len(accs),
            finish=finish is not None,
        ),
        grid=(crops // per,),
        in_specs=specs,
        out_specs=[kind(shape) for shape, _, kind in outs],
        out_shape=[jax.ShapeDtypeStruct(shape, dtype) for shape, dtype, _ in outs],
        scratch_shapes=scratch,
        compiler_params=params(LAST_MEM if finish is not None else BACK_MEM),
        cost_estimate=cost(31 if finish is not None else 22),
        name="attention_back",
    )(*args)


def gelu_and_slope(h):
    phi = 0.5 * (1.0 + lax.erf(h * (2.0**-0.5)))
    bell = jnp.exp(-0.5 * h * h) * 0.3989422804014327
    return h * phi, phi + h * bell


def mlp_chain(n2, go, shards, accs, last):
    sums = []
    for i, (w1_ref, w2_ref, bias) in enumerate(shards):
        h = mm_nn(n2, w1_ref[...]) + bias[0:1, :]
        ga = mm_nt(go, w2_ref[...])
        yield
        a, slope = gelu_and_slope(h)
        a = a.astype(BF16)
        gh = ga * slope
        gh_low = gh.astype(BF16)
        yield
        pair = mm_nn(a, w2_ref[...]), mm_nt(gh_low, w1_ref[...])
        if i == 0:
            for one in accs:
                pair = tuple(x + y() for x, y in zip(pair, one))
        if i < 2:
            sums.append(pair)
        else:
            sums[1] = tuple(x + y for x, y in zip(sums[1], pair))
    yield
    out, gn = sums[0] if len(sums) == 1 else (x + y for x, y in zip(*sums))
    last(out, gn, a, gh, gh_low)


def place_mlp(info, pieces, w1_ref, w2_ref, bias_ref):
    place_pieces(info, pieces, w1_ref, 0, lambda j: j * PART)
    place_pieces(info, pieces, w2_ref, PART + 8, lambda j: j * PART)
    ref, slot = pieces[0]
    bias_ref[...] = ref[slot, PART : PART + 8, :]


def placed_mlp(width, hidden):
    return [((width, hidden), BF16), ((hidden, width), BF16), ((8, hidden), F32)]


def mlp_kernel(*refs, ready, gathers, accs, own, finish):
    it = iter(refs)
    info, n2_ref, up_ref, vec_ref = (next(it) for _ in range(4))
    shards = [tuple(next(it) for _ in range(3)) for _ in range(ready)]
    pieces = [take_pieces(it, 4) for _ in range(gathers)]
    acc_refs = [(next(it), next(it)) for _ in range(accs)]
    if finish:
        begin_ref, br_ref = next(it), next(it)
        res_ref, gmid_ref, gb_ref, sum_ref = (next(it) for _ in range(4))
    else:
        out_ref, gn_ref = next(it), next(it)
    if own:
        a_ref, gh_ref, go_ref, hsum_ref = (next(it) for _ in range(4))
    first = pl.program_id(0) == 0
    placed = [tuple(next(it) for _ in range(3)) for _ in range(gathers)]

    @pl.when(first)
    def _():
        for parts, to in zip(pieces, placed):
            place_mlp(info, parts, *to)

    if not own:
        shards += placed
    per = n2_ref.shape[0]
    many = []

    def last(i, up, grad_output, go, out, gn, a, gh, gh_low):
        if own:
            a_ref[i] = a
            go_ref[i] = go
            gh_ref[i] = gh_low
            many.append(jnp.concatenate([row_sum(gh), jnp.zeros((7, gh.shape[1]), F32)], 0))
        if not finish:
            out_ref[i] = out
            gn_ref[i] = gn
            return
        out = out + row(vec_ref, FC2_BIAS)
        branch = br_ref[i] + row(vec_ref, PROJ_BIAS)
        attn_scale = row(vec_ref, ATTN_SCALE)
        middle = begin_ref[i] + attn_scale * branch
        result = middle + row(vec_ref, MLP_SCALE) * out
        res_ref[i] = result.astype(BF16)
        xhat, rstd = norm_parts(middle)
        gmid = up + norm_back(xhat, rstd, gn, row(vec_ref, PRE_MLP_GAIN))
        gmid_ref[i] = gmid
        gbr = gmid * attn_scale
        gb_ref[i] = gbr.astype(BF16)
        sums = (up * out, grad_output, gn * xhat, gn, gmid * branch, gbr)
        many.append(
            jnp.concatenate([row_sum(x) for x in sums] + [jnp.zeros((2, gn.shape[1]), F32)], 0)
        )

    chains = []
    for i in range(per):
        up = up_ref[i].astype(F32)
        grad_output = up * row(vec_ref, MLP_SCALE)
        go = grad_output.astype(BF16)
        held = [[lambda ref=ref, i=i: ref[i] for ref in pair] for pair in acc_refs]
        chains.append(
            mlp_chain(n2_ref[i], go, shards, held, functools.partial(last, i, up, grad_output, go))
        )
    interleave(chains)
    if many:
        ref = sum_ref if finish else hsum_ref
        sums = sum(many[1:], many[0])
        ref[...] = jnp.where(first, sums, ref[...] + sums)


def mlp(n2, up, vecs, ready, pieces, info, accs, hidden, own=False, finish=None):
    crops, rows, width = n2.shape
    per = MLP_PER
    crop = functools.partial(block, per=per)
    args, specs = [], []

    def add(x, spec):
        args.append(x)
        specs.append(spec)

    add(info, pl.BlockSpec(memory_space=pltpu.SMEM))
    add(n2, crop(n2.shape))
    add(up, crop(up.shape))
    add(vecs, once(vecs.shape))
    for w in sum(ready, ()):
        add(w, once(w.shape))
    for x in pieces:
        add(x, once(x.shape))
    for pair in accs:
        for a in pair:
            add(a, crop(a.shape))
    full = (crops, rows, width)
    scratch = []
    if finish is not None:
        add(finish[0], crop(finish[0].shape))
        add(finish[1], crop(finish[1].shape))
        outs = [
            (full, BF16, crop),
            (full, F32, crop),
            (full, BF16, crop),
            ((8, width), F32, whole),
        ]
    else:
        outs = [(full, F32, crop), (full, F32, crop)]
    gathers = len(pieces) // 4
    placed = placed_mlp(width, hidden) * gathers
    if own:
        outs += [((crops, rows, hidden), BF16, crop)] * 2 + [(full, BF16, crop), ((8, hidden), F32, whole)]
        outs += [(shape, dtype, once) for shape, dtype in placed]
    else:
        scratch = [pltpu.VMEM(shape, dtype) for shape, dtype in placed]
    return pl.pallas_call(
        functools.partial(
            mlp_kernel,
            ready=len(ready),
            gathers=gathers,
            accs=len(accs),
            own=own,
            finish=finish is not None,
        ),
        grid=(crops // per,),
        in_specs=specs,
        out_specs=[kind(shape) for shape, _, kind in outs],
        out_shape=[jax.ShapeDtypeStruct(shape, dtype) for shape, dtype, _ in outs],
        scratch_shapes=scratch,
        compiler_params=params(MLP_MEM if own else VMEM_MOST),
        cost_estimate=cost(16 if own else 45),
        name="mlp",
    )(*args)


def weight_grad_kernel(x1_ref, y1_ref, x2_ref, y2_ref, out_ref, *, parts):
    first, second = mm_tn(x1_ref[...], y1_ref[...]), mm_tn(x2_ref[...], y2_ref[...])
    out_ref[...] = jnp.concatenate([(first, second)[i][:, lo:hi] for i, lo, hi in parts], 1)


def weight_grads(x1, y1, x2, y2, parts):
    rows, width = x1.shape
    col = pl.BlockSpec((rows, WIDE), lambda i: (0, i))
    wide = sum(hi - lo for _, lo, hi in parts)
    return pl.pallas_call(
        functools.partial(weight_grad_kernel, parts=parts),
        grid=(width // WIDE,),
        in_specs=[col, once(y1.shape), col, once(y2.shape)],
        out_specs=pl.BlockSpec((WIDE, wide), lambda i: (i, 0)),
        out_shape=jax.ShapeDtypeStruct((width, wide), F32),
        compiler_params=params(GRAD_MEM),
        cost_estimate=cost(10),
        name="weight_grads",
    )(x1, y1, x2, y2)


def plane_perm(inner, outer, move):
    pairs = []
    for i in range(inner):
        for o in range(outer):
            j, r = move(i, o)
            pairs.append((i * outer + o, j * outer + r))
    return pairs


def after(x, *others):
    return lax.optimization_barrier((x, *others))[0] if others else x


def fence(new, *done):
    return lax.optimization_barrier((*new, *done))[: len(new)]


class PlaneSum:
    def __init__(self, sizes, inner, mine, give):
        _, self.inner_n, self.outer_n = sizes
        self.side = inner // 2
        self.inner = inner
        self.mine, self.give = mine, give

    def cores(self):
        self.one = lax.ppermute(self.give, "inner", [(i, i ^ 1) for i in range(self.inner_n)])
        return self.one

    def pick(self, side):
        at = side if self.mine.shape[0] == 2 else 2 * side + self.inner % 2
        return sum(lax.dynamic_index_in_dim(x, at, 0, keepdims=False) for x in (self.mine, self.one))

    def sides(self, lo=0, hi=None):
        give = self.pick(1 - self.side)[:, lo:hi]
        return lax.ppermute(give, "inner", [(i, i ^ 2) for i in range(self.inner_n)])

    def total(self, two, lo=0, hi=None):
        return self.pick(self.side)[:, lo:hi] + two


def sum_groups(x, outer_n):
    k = 1
    while k < outer_n:
        x = x + lax.ppermute(x, "outer", [(o, o ^ k) for o in range(outer_n)])
        k *= 2
    return x


def leave_kernel(x_ref, qkv_ref, proj_ref):
    side = proj_ref.shape[0]
    for t in range(3):
        qkv_ref[t] = x_ref[:, t * side : (t + 1) * side]
    proj_ref[...] = x_ref[:, 3 * side : 4 * side].T


def leave(x, side):
    rows = x.shape[0]
    return pl.pallas_call(
        leave_kernel,
        out_shape=[
            jax.ShapeDtypeStruct((3, rows, side), F32),
            jax.ShapeDtypeStruct((side, rows), F32),
        ],
        compiler_params=params(16),
        cost_estimate=cost(2),
        name="leave",
    )(x)


def per_device(
    sizes,
    tokens,
    patch_mask,
    cotangent,
    mask_token,
    pos_embed,
    pre_attn_gain,
    pre_attn_bias,
    qkv_weight,
    qv_bias,
    proj_weight,
    proj_bias,
    attn_scale,
    pre_mlp_gain,
    pre_mlp_bias,
    fc1_weight,
    fc1_bias,
    fc2_weight,
    fc2_bias,
    mlp_scale,
):
    tensor_n, inner_n, outer_n = sizes
    crops, seq, width = tokens.shape
    head_width = qkv_weight.shape[2]
    heads = head_width // HEAD_DIM
    hidden = fc1_weight.shape[1]
    rows = -(-seq // 16) * 16
    tail_valid = seq - MAIN
    t = lax.axis_index("tensor")
    inner = lax.axis_index("inner")
    outer = lax.axis_index("outer")
    place = inner * 2 + outer % 2
    info = jnp.stack([place, inner % 2]).astype(jnp.int32)

    qkv_rows = qkv_weight.transpose(1, 2, 0).reshape(3 * head_width, width)

    def eighth(x):
        return lax.dynamic_slice_in_dim(x, place * PART, PART, 0).astype(F32)

    ones = jnp.ones((heads,), F32)
    zeros = jnp.zeros((WIDE,), F32)
    attn_bias = jnp.concatenate(
        [qv_bias[0], zeros[head_width:], zeros, qv_bias[1], ones, zeros[head_width + heads :]]
    )[None, :]
    mlp_bias = fc1_bias[None, :]
    below = jnp.zeros((7, width), F32)
    attn_piece = jnp.concatenate(
        [eighth(jnp.concatenate([qkv_rows, proj_weight], 0)), attn_bias, below], 0
    )
    own_mlp = (fc1_weight, fc2_weight, mlp_bias)
    chunks = ((0, 72), (72, 112), (112, 200), (72, 200))
    perms = (
        plane_perm(inner_n, outer_n, lambda i, o: (i, o ^ 1) if i % 2 else (i ^ 2, o)),
        plane_perm(inner_n, outer_n, lambda i, o: (i ^ 2, o) if i % 2 else (i, o ^ 1)),
        plane_perm(inner_n, outer_n, lambda i, o: (i ^ 1, o)),
    )
    def over_z(x, k):
        return lax.ppermute(x, "tensor", [(i, i ^ k) for i in range(tensor_n)])

    along, far, peer = (functools.partial(lax.ppermute, axis_name=PLANE, perm=p) for p in perms)

    vecs = jnp.stack(
        [
            mask_token,
            pre_attn_gain,
            pre_attn_bias,
            proj_bias,
            attn_scale,
            pre_mlp_gain,
            pre_mlp_bias,
            fc2_bias,
            mlp_scale,
        ]
    )
    run = functools.partial(attn, heads=heads, tail_valid=tail_valid)
    layer = functools.partial(mlp, hidden=hidden)

    quarter = width // inner_n

    def plane_sum(x):
        x = x.reshape(inner_n, quarter, -1)
        return PlaneSum(sizes, inner, x, x)

    def pair(first, second):
        return jnp.stack([first, second])

    a1, a2 = over_z(attn_piece, 1), over_z(attn_piece, 2)
    begin, n1, *pieces = enter(
        info, tokens.transpose(1, 0, 2), patch_mask, vecs, pos_embed, rows, own_mlp, chunks
    )
    m1_pieces, m2_pieces = (pieces[0], pieces[3]), pieces[:3]

    n1, a1, a2, m2_piece = fence((n1, a1, a2, m2_pieces[0]))
    b1, b2 = along(a1), along(a2)
    a3 = over_z(a2, 1)
    m2 = [over_z(m2_piece, 2)]
    half = crops // 2
    own_w = [attn_bias, qkv_rows, proj_weight]
    early = run(n1, own_w, None, [], span=(0, half))

    both1 = pair(a1, b1)
    cot, both1, a3, m1_piece = fence(
        (cotangent.transpose(1, 0, 2), both1, a3, m1_pieces[0]), early[0], b2, *m2
    )
    c1, d1 = far(both1), peer(both1)
    m1 = [over_z(m1_piece, 1)]
    up = upstream(cot, rows)

    both2 = pair(a2, b2)
    n1, c1, both2, a3, m1_piece, m2_piece = fence(
        (n1, c1, both2, a3, m1_pieces[1], m2_pieces[1]), up, d1, *m1
    )
    e1 = peer(c1)
    c2 = far(both2)
    b3 = along(a3)
    m1.append(over_z(m1_piece, 1))
    m2.append(over_z(m2_piece, 2))
    br0, mix0, lse0, w_0, att0 = run(n1, own_w, None, [], span=(half, crops), into=early)

    both3, four2 = pair(a3, b3), jnp.concatenate([both2, c2], 0)
    m1 = jnp.concatenate(m1, 0)
    n1, four2, both3, m1, m2_piece = fence(
        (n1, four2, both3, m1, m2_pieces[2]), br0, e1, m2[1]
    )
    de2 = peer(four2)
    c3 = far(both3)
    f1 = along(m1)
    m2.append(over_z(m2_piece, 2))
    br1, mix1, lse1, w_1 = run(n1, [both1, c1, d1, e1], info, [br0])

    four3, two1 = jnp.concatenate([both3, c3], 0), pair(m1, f1)
    m2 = jnp.concatenate(m2, 0)
    n1, four3, two1, m2 = fence((n1, four3, two1, m2), br1, de2)
    de3 = peer(four3)
    g1, h1 = far(two1), peer(two1)
    m3 = over_z(m2, 1)
    br2, mix2, lse2, w_2 = run(n1, [four2, de2], info, [])

    n1, g1, m2, m3 = fence((n1, g1, m2, m3), br2, de3, h1)
    i1 = peer(g1)
    f2, f3 = along(m2), along(m3)
    br, mix3, lse3, w_3, n2 = run(n1, [four3, de3], info, [br2, br1], finish=(begin, vecs))

    two2, two3 = pair(m2, f2), pair(m3, f3)
    n2, two2, two3 = fence((n2, two2, two3), i1)
    g2, h2 = far(two2), peer(two2)
    out0, gn0, a0, gh0, go0, hsum, *mlp_1 = layer(
        n2, up, vecs, [own_mlp], [two1, g1, h1, i1], info, [], own=True
    )

    flat = lambda x: x.reshape(crops * rows, -1)
    n2, g2, two3 = fence((n2, g2, two3), out0, h2)
    i2 = peer(g2)
    g3, h3 = far(two3), peer(two3)
    mlp_grads = weight_grads(
        flat(n2), flat(gh0), flat(go0), flat(a0), ((0, 0, hidden), (1, 0, hidden))
    )

    n2, g3, mlp_grads = fence((n2, g3, mlp_grads), i2, h3)
    i3 = peer(g3)
    n2, mlp_grads = fence((n2, mlp_grads), i3)

    mlp_sum = plane_sum(mlp_grads)
    s1 = mlp_sum.cores()
    result, gmid, gb, mid_sums = layer(
        n2,
        up,
        vecs,
        [tuple(mlp_1)],
        [two2, g2, h2, i2, two3, g3, h3, i3],
        info,
        [(out0, gn0)],
        finish=(begin, br),
    )

    back = functools.partial(attn_back, heads=heads, tail_valid=tail_valid)
    gb, mlp_sum.one = fence((gb, s1))
    s2 = mlp_sum.sides(0, hidden)
    gn0, gm0, qv_sums = back(gb, w_0, mix0, lse0, [], own=True)
    attn_grads = weight_grads(
        flat(n1),
        flat(gm0),
        flat(gb),
        flat(att0),
        tuple((0, i * WIDE, i * WIDE + head_width) for i in range(3)) + ((1, 0, head_width),),
    )

    gb, attn_grads, s2, mlp_sum.one = fence((gb, attn_grads, s2, mlp_sum.one))
    attn_sum = plane_sum(attn_grads)
    s1 = attn_sum.cores()
    grad_fc1 = sum_groups(mlp_sum.total(s2, 0, hidden), outer_n)
    s3 = mlp_sum.sides(hidden)
    (gn1,) = back(gb, w_1, mix1, lse1, [gn0])

    gb, attn_sum.one, s3 = fence((gb, s1, s3), gn1, grad_fc1)
    s2 = attn_sum.sides()
    grad_fc2 = sum_groups(mlp_sum.total(s3, hidden), outer_n)
    (gn2,) = back(gb, w_2, mix2, lse2, [])

    gb, s2 = fence((gb, s2), gn2, grad_fc2)
    shares_attn = sum_groups(attn_sum.total(s2), outer_n)
    gtok, keep, give = back(
        gb,
        w_3,
        mix3,
        lse3,
        [gn2, gn1],
        finish=(info, begin, gmid, patch_mask, vecs, mid_sums, hsum, qv_sums),
    )

    small = head_width // inner_n
    small_sum = PlaneSum(sizes, inner, keep, after(give, shares_attn))
    small_sum.cores()
    give, mine = small_sum.pick(1 - small_sum.side), small_sum.pick(small_sum.side)
    if outer_n == 2:
        corner = plane_perm(inner_n, outer_n, lambda i, o: (i ^ 2, o ^ 1))
        give, mine, result, gtok = fence((give, mine, result, gtok))
        near = lax.ppermute(give, "inner", [(i, i ^ 2) for i in range(inner_n)])
        over = lax.ppermute(mine, "outer", [(0, 1), (1, 0)])
        across = lax.ppermute(give, PLANE, corner)
        small_sums = (mine + near) + (over + across)
    else:
        small_sums = sum_groups(small_sum.total(small_sum.sides()), outer_n)
    result, gtok = by_token([result, gtok], seq)
    small_sums = small_sums.reshape(-1, inner_n, quarter).transpose(1, 0, 2).reshape(-1, quarter)
    grad_qkv, grad_proj = leave(shares_attn, head_width)
    mid = lambda i: small_sums[rows + i]
    vec = lambda i: small_sums[rows + 8 + i]
    return (
        result.transpose(1, 0, 2),
        gtok.transpose(1, 0, 2),
        vec(2),
        small_sums[:seq],
        vec(0),
        vec(1),
        grad_qkv.transpose(1, 0, 2),
        jnp.stack([vec(4)[:small], vec(5)[:small]]),
        grad_proj,
        mid(5),
        mid(4),
        mid(2),
        mid(3),
        grad_fc1,
        vec(3),
        grad_fc2.T,
        mid(1),
        mid(0),
    )


def solution(mesh):
    in_specs = (
        P(("inner", "outer"), None, None),
        P(("inner", "outer"), None),
        P(("inner", "outer"), None, None),
        P(),
        P(),
        P(),
        P(),
        P(None, None, "tensor"),
        P(None, "tensor"),
        P("tensor", None),
        P(),
        P(),
        P(),
        P(),
        P(None, "tensor"),
        P("tensor"),
        P("tensor", None),
        P(),
        P(),
    )
    out_specs = (
        P(("inner", "outer"), None, None),
        P(("inner", "outer"), None, None),
        P("inner"),
        P(None, "inner"),
        P("inner"),
        P("inner"),
        P("inner", None, "tensor"),
        P(None, ("tensor", "inner")),
        P("tensor", "inner"),
        P("inner"),
        P("inner"),
        P("inner"),
        P("inner"),
        P("inner", "tensor"),
        P(("tensor", "inner")),
        P("tensor", "inner"),
        P("inner"),
        P("inner"),
    )
    sizes = tuple(mesh.shape[name] for name in ("tensor", "inner", "outer"))
    return jax.shard_map(
        functools.partial(per_device, sizes),
        mesh=mesh,
        in_specs=in_specs,
        out_specs=out_specs,
        check_vma=False,
    )
```

```python
import functools

import jax
import jax.numpy as jnp
from jax import lax
from jax.experimental import pallas as pl
from jax.experimental.pallas import tpu as pltpu
from jax.sharding import PartitionSpec as P

HEAD_DIM = 64
EPS = 1e-06
F32 = jnp.float32
BF16 = jnp.bfloat16
NEG = -1e30
LANES = 128
WIDE = 256
MAIN = 256
MIB = 1024 * 1024
ENTER_MEM, ATTN_MEM, MLP_MEM, GRAD_MEM, BACK_MEM, LAST_MEM = 50, 50, 50, 50, 50, 50
VMEM_MOST = 60
PLANE = ("inner", "outer")
PART = 96


def mm_nt(a, b):
    return lax.dot_general(a, b, (((1,), (1,)), ((), ())), preferred_element_type=F32)


def mm_nn(a, b):
    return lax.dot_general(a, b, (((1,), (0,)), ((), ())), preferred_element_type=F32)


def mm_tn(a, b):
    return lax.dot_general(a, b, (((0,), (0,)), ((), ())), preferred_element_type=F32)


ATTN_PER, BACK_PER, MLP_PER = 2, 2, 1


def cost(us):
    return pl.CostEstimate(flops=int(us * 1.15e9), bytes_accessed=1 << 20, transcendentals=0)


(
    MASK_TOKEN,
    PRE_ATTN_GAIN,
    PRE_ATTN_BIAS,
    PROJ_BIAS,
    ATTN_SCALE,
    PRE_MLP_GAIN,
    PRE_MLP_BIAS,
    FC2_BIAS,
    MLP_SCALE,
) = range(9)


def row(ref, i):
    return ref[i : i + 1, :]


def params(limit):
    return pltpu.CompilerParams(vmem_limit_bytes=limit * MIB)


def block(shape, per=1):
    return pl.BlockSpec((per,) + tuple(shape[1:]), lambda c: (c,) + (0,) * (len(shape) - 1))


def whole(shape):
    return pl.BlockSpec(tuple(shape), lambda c: (0,) * len(shape))


def once(shape):
    return pl.BlockSpec(tuple(shape), lambda c: (0,) * len(shape), pipeline_mode=pl.Buffered(1))


def row_sum(x):
    return jnp.sum(x, 0, keepdims=True)


def norm_parts(v):
    center = v - jnp.mean(v, -1, keepdims=True)
    rstd = lax.rsqrt(jnp.mean(center * center, -1, keepdims=True) + EPS)
    return center * rstd, rstd


def norm_back(xhat, rstd, u, gain):
    gu = u * gain
    return (
        gu - jnp.mean(gu, -1, keepdims=True) - xhat * jnp.mean(gu * xhat, -1, keepdims=True)
    ) * rstd


def put_columns(ref, rows, x):
    for j in range(ref.shape[0]):
        ref[j, rows, :] = x[:, j * LANES : (j + 1) * LANES]


def get_columns(ref, rows):
    return jnp.concatenate([ref[j, rows, :] for j in range(ref.shape[0])], 1)


def flag_lanes(mask_ref, crop, rows, prefix):
    crop_mask = mask_ref[pl.ds(crop, 1), :]
    patches = crop_mask.shape[1]
    ones = jnp.broadcast_to((crop_mask == 1).astype(F32), (LANES, patches)).astype(BF16)
    token = lax.broadcasted_iota(jnp.int32, (rows, patches), 0)
    patch = lax.broadcasted_iota(jnp.int32, (rows, patches), 1)
    return mm_nt((token == patch + prefix).astype(F32).astype(BF16), ones)


def flag_wide(mask_ref, crop, rows, prefix, width):
    return jnp.concatenate([flag_lanes(mask_ref, crop, rows, prefix)] * (width // LANES), 1) > 0.5


def by_crop(src_ref, scratch):
    seq, crops, _ = src_ref.shape
    step = 29 if seq % 29 == 0 else 1

    @pl.when(pl.program_id(0) == 0)
    def _():
        def move(i, carry):
            dst = pl.ds(pl.multiple_of(i * (step * crops), crops), step * crops)
            put_columns(scratch, dst, src_ref[pl.ds(i * step, step)].astype(F32).reshape(step * crops, -1))
            return carry

        lax.fori_loop(0, seq // step, move, 0)
        scratch[:, seq * crops :, :] = jnp.zeros_like(scratch[:, seq * crops :, :])

    return get_columns(scratch, pl.ds(pl.program_id(0), scratch.shape[1] // crops, stride=crops))


def enter_kernel(info, tok_ref, mask_ref, vec_ref, pos_ref, w1_ref, w2_ref, bias_ref, *refs, chunks):
    begin_ref, n1_ref, *chunk_refs, scratch = refs

    @pl.when(pl.program_id(0) == 0)
    def _():
        mine = pl.ds(pl.multiple_of(info[0] * PART, 32), PART)
        hidden = w1_ref.shape[1]
        below = jnp.zeros((7, hidden), F32)
        piece = [w1_ref[mine, :].astype(F32), bias_ref[...], below, w2_ref[mine, :].astype(F32)]
        piece = jnp.concatenate(piece, 0)
        for (lo, hi), ref in zip(chunks, chunk_refs):
            ref[...] = piece[lo:hi]

    tok = by_crop(tok_ref, scratch)
    rows = tok.shape[0]
    near = pos_ref.shape[0] // 8 * 8
    rest = pos_ref.shape[0] - near
    pos = [pos_ref[0:near, :]]
    if rest:
        pos.append(jnp.concatenate([pos_ref[near:, :], jnp.zeros((8 - rest, tok.shape[1]), F32)], 0))
    pos.append(jnp.zeros((rows - near - 8 * (rest > 0), tok.shape[1]), F32))
    pos = jnp.concatenate(pos, 0)
    prefix = tok_ref.shape[0] - mask_ref.shape[1]
    flagged = flag_wide(mask_ref, pl.program_id(0), rows, prefix, tok.shape[1])
    begin = jnp.where(flagged, row(vec_ref, MASK_TOKEN), tok) + pos
    begin_ref[0] = begin
    xhat, _ = norm_parts(begin)
    n1_ref[0] = (xhat * row(vec_ref, PRE_ATTN_GAIN) + row(vec_ref, PRE_ATTN_BIAS)).astype(BF16)


def enter(info, tok, mask, vecs, pos, rows, own_mlp, chunks):
    seq, crops, width = tok.shape
    shape = (crops, rows, width)
    args = (tok, mask, vecs, pos, *own_mlp)
    small = [(hi - lo, width) for lo, hi in chunks]
    return pl.pallas_call(
        functools.partial(enter_kernel, chunks=chunks),
        grid=(crops,),
        in_specs=[pl.BlockSpec(memory_space=pltpu.SMEM)] + [once(x.shape) for x in args],
        out_specs=[block(shape)] * 2 + [once(x) for x in small],
        out_shape=[
            jax.ShapeDtypeStruct(shape, F32),
            jax.ShapeDtypeStruct(shape, BF16),
            *(jax.ShapeDtypeStruct(x, F32) for x in small),
        ],
        scratch_shapes=[pltpu.VMEM((width // LANES, rows * crops, LANES), F32)],
        compiler_params=params(ENTER_MEM),
        cost_estimate=cost(7),
        name="enter",
    )(info, *args)


def upstream_kernel(cot_ref, up_ref, scratch):
    up_ref[0] = by_crop(cot_ref, scratch).astype(BF16)


def upstream(cot, rows):
    seq, crops, width = cot.shape
    shape = (crops, rows, width)
    return pl.pallas_call(
        upstream_kernel,
        grid=(crops,),
        in_specs=[once(cot.shape)],
        out_specs=block(shape),
        out_shape=jax.ShapeDtypeStruct(shape, BF16),
        scratch_shapes=[pltpu.VMEM((width // LANES, rows * crops, LANES), F32)],
        compiler_params=params(ENTER_MEM),
        cost_estimate=cost(6),
        name="upstream",
    )(cot)


def by_token_kernel(*refs):
    arrays = (len(refs) - 1) // 2
    scratch = refs[-1]
    for x_ref, out_ref in zip(refs[:arrays], refs[arrays:-1]):
        crops, step, _ = x_ref.shape
        for c in range(crops):
            put_columns(scratch, pl.ds(c, step, stride=crops), x_ref[c].astype(F32))
        out = get_columns(scratch, slice(None))
        out_ref[...] = out.reshape(out_ref.shape).astype(out_ref.dtype)


def by_token(arrays, seq):
    crops, rows, width = arrays[0].shape
    step = 48
    return pl.pallas_call(
        by_token_kernel,
        grid=(-(-seq // step),),
        in_specs=[pl.BlockSpec((crops, step, width), lambda i: (0, i, 0))] * len(arrays),
        out_specs=[pl.BlockSpec((step, crops, width), lambda i: (i, 0, 0))] * len(arrays),
        out_shape=[jax.ShapeDtypeStruct((seq, crops, width), x.dtype) for x in arrays],
        scratch_shapes=[pltpu.VMEM((width // LANES, step * crops, LANES), F32)],
        compiler_params=params(14),
        cost_estimate=cost(8),
        name="by_token",
    )(*arrays)


def head_masks(heads):
    lane = lax.broadcasted_iota(jnp.int32, (1, WIDE), 1)
    return [((lane // HEAD_DIM) == h).astype(F32) for h in range(heads)], lane


def per_head_rows(x, masks):
    parts = [x * m for m in masks]
    parts.append(jnp.zeros((LANES - 8 * len(masks), x.shape[1]), F32))
    return jnp.concatenate(parts, 0).astype(BF16)


def pick(index, parts):
    out = parts[-1]
    for h in range(len(parts) - 2, -1, -1):
        out = jnp.where(index == h, parts[h], out)
    return out


def interleave(chains):
    live, waiting = [], list(chains)
    while live or waiting:
        live += waiting[:1]
        del waiting[:1]
        live = [c for c in live[::-1] if next(c, True) is None][::-1]


def by_head(x, heads):
    rows = x.shape[0] // heads
    return [x[h * rows : (h + 1) * rows] for h in range(heads)]


def attention_forward(n1, w_ref, bias, heads, tail_valid, last):
    masks, lane = head_masks(heads)
    low = [m.astype(BF16) for m in masks]
    head_width = heads * HEAD_DIM
    mixed = (mm_nt(n1, w_ref[0 : 3 * WIDE, :]) + bias).astype(BF16)
    yield
    q = mixed[:, 0:WIDE] * jnp.asarray(HEAD_DIM**-0.5, BF16)
    k, v = mixed[:, WIDE : 2 * WIDE], mixed[:, 2 * WIDE : 3 * WIDE]
    mixed = jnp.concatenate([q, k, v], 1)
    k_main, v_main = k[0:MAIN], v[0:MAIN]
    v_masks = [m + (lane == head_width + h).astype(F32) for h, m in enumerate(masks)]
    k_tail = per_head_rows(k[MAIN : MAIN + 8].astype(F32), masks)
    v_tail = per_head_rows(v[MAIN : MAIN + 8].astype(F32), v_masks)
    col = lax.broadcasted_iota(jnp.int32, (1, LANES), 1)
    valid = (col < 8 * heads) & ((col % 8) < tail_valid)
    qs = jnp.concatenate([q * m for m in low], 0)
    vs = jnp.concatenate([v_main * m.astype(BF16) for m in v_masks] + [v_tail], 0)
    yield
    s_tail = mm_nt(q, k_tail)
    scores = by_head(mm_nt(qs, k_main), heads)
    yield
    s_tail = jnp.where(valid, s_tail, NEG)
    tops, exps = [], []
    for h, s in enumerate(scores):
        top = jnp.where((col // 8) == h, s_tail, NEG)
        for i in range(MAIN // LANES):
            top = jnp.maximum(top, s[:, i * LANES : (i + 1) * LANES])
        top = jnp.max(top, -1, keepdims=True)
        tops.append(top)
        exps.append(jnp.exp(s - top).astype(BF16))
    exps.append(jnp.exp(s_tail - pick(col // 8, tops)).astype(BF16))
    yield
    total = mm_nn(jnp.concatenate(exps, 1), vs)
    yield
    sums = [total[:, head_width + h : head_width + h + 1] for h in range(heads)]
    scale = pick(lane // HEAD_DIM, [1.0 / s for s in sums])
    attended = (total * scale).astype(BF16)
    log_total = pick(col, [t + jnp.log(s) for t, s in zip(tops, sums)])
    yield
    branch = mm_nn(attended, w_ref[3 * WIDE : 4 * WIDE, :])
    yield
    last(mixed, log_total, attended, branch)


def take_pieces(it, count):
    found = []
    for ref in (next(it) for _ in range(count)):
        found += [ref] if len(ref.shape) == 2 else [ref.at[i] for i in range(ref.shape[0])]
    return found


def place_pieces(info_ref, pieces, out_ref, base, first):
    p, core = info_ref[0], info_ref[1]
    q = p ^ 2
    a_bit = jnp.where(core == 0, 4, 1)
    b_bit = 5 - a_bit
    idents = (p, p ^ a_bit, p ^ b_bit, p ^ 5, q, q ^ b_bit, q ^ a_bit, q ^ 5)
    for ref, ident in zip(pieces, idents, strict=True):
        dst = pl.multiple_of(first(ident), 32)
        out_ref[pl.ds(dst, PART), :] = ref[base : base + PART, :].astype(BF16)


def attn_kernel(*refs, heads, tail_valid, own, into, accs, finish, gathers):
    it = iter(refs)
    if own:
        n1_ref, bias_ref, qkv_ref, proj_ref = (next(it) for _ in range(4))
        bias = bias_ref[...]
    else:
        info, n1_ref = next(it), next(it)
        pieces = take_pieces(it, gathers)
        bias = pieces[0][PART : PART + 1, :]
    acc_refs = [next(it) for _ in range(accs)]
    if finish:
        begin_ref, vec_ref = next(it), next(it)
    for _ in range(into):
        next(it)
    br_ref, mix_ref, lse_ref, w_ref = (next(it) for _ in range(4))

    @pl.when(pl.program_id(0) == 0)
    def _():
        width = heads * HEAD_DIM
        for i in range(4):
            w_ref[i * WIDE + width : (i + 1) * WIDE, :] = jnp.zeros((WIDE - width, w_ref.shape[1]), BF16)
        if own:
            for i in range(3):
                w_ref[i * WIDE : i * WIDE + width, :] = qkv_ref[i * width : (i + 1) * width, :]
            w_ref[3 * WIDE : 3 * WIDE + width, :] = proj_ref[...]
        else:
            place_pieces(info, pieces, w_ref, 0, lambda i: (i >> 1) * WIDE + (i & 1) * PART)

    att_ref = next(it) if own else None
    n2_ref = next(it) if finish else None

    def last(i, mixed, log_total, attended, branch):
        mix_ref[i] = mixed
        lse_ref[i] = log_total
        if own:
            att_ref[i] = attended
        for ref in acc_refs:
            branch = branch + ref[i]
        br_ref[i] = branch
        if finish:
            middle = begin_ref[i] + row(vec_ref, ATTN_SCALE) * (branch + row(vec_ref, PROJ_BIAS))
            xhat, _ = norm_parts(middle)
            n2 = xhat * row(vec_ref, PRE_MLP_GAIN) + row(vec_ref, PRE_MLP_BIAS)
            n2_ref[i] = n2.astype(BF16)

    interleave(
        [
            attention_forward(n1_ref[i], w_ref, bias, heads, tail_valid, functools.partial(last, i))
            for i in range(n1_ref.shape[0])
        ]
    )


def attn(n1, weights, info, accs, heads, tail_valid, finish=None, span=None, into=()):
    crops, rows, width = n1.shape
    own = info is None
    lo, hi = span or (0, crops)
    args, specs = [], []

    per = ATTN_PER

    def crop(shape):
        at = lambda c: (c + lo // per,) + (0,) * (len(shape) - 1)
        return pl.BlockSpec((per,) + tuple(shape[1:]), at)

    def add(x, spec):
        args.append(x)
        specs.append(spec)

    if not own:
        add(info, pl.BlockSpec(memory_space=pltpu.SMEM))
    add(n1, crop(n1.shape))
    for w in weights:
        add(w, once(w.shape))
    for a in accs:
        add(a, crop(a.shape))
    if finish is not None:
        add(finish[0], crop(finish[0].shape))
        add(finish[1], once(finish[1].shape))
    outs = [
        ((crops, rows, width), F32, crop),
        ((crops, rows, 3 * WIDE), BF16, crop),
        ((crops, rows, LANES), F32, crop),
        ((4 * WIDE, width), BF16, whole),
    ]
    if own:
        outs.append(((crops, rows, WIDE), BF16, crop))
    if finish is not None:
        outs.append(((crops, rows, width), BF16, crop))
    aliases = {}
    for i, x in enumerate(into):
        if outs[i][2] is crop:
            aliases[len(args)] = i
            add(x, pl.BlockSpec(memory_space=pl.ANY))
    return pl.pallas_call(
        functools.partial(
            attn_kernel,
            heads=heads,
            tail_valid=tail_valid,
            own=own,
            gathers=len(weights),
            into=len(aliases),
            accs=len(accs),
            finish=finish is not None,
        ),
        grid=((hi - lo) // per,),
        in_specs=specs,
        out_specs=[kind(shape) for shape, _, kind in outs],
        out_shape=[jax.ShapeDtypeStruct(shape, dtype) for shape, dtype, _ in outs],
        input_output_aliases=aliases,
        compiler_params=params(ATTN_MEM),
        cost_estimate=cost((21 if finish is not None else 16) * (hi - lo) / crops),
        name="attention",
    )(*args)


def attention_backward(gb, w_ref, mix, lse_in, heads, tail_valid, last):
    masks, lane = head_masks(heads)
    low = [m.astype(BF16) for m in masks]
    da = mm_nt(gb, w_ref[3 * WIDE : 4 * WIDE, :])
    q, k, v = (mix[:, i * WIDE : (i + 1) * WIDE] for i in range(3))
    k_main, v_main = k[0:MAIN], v[0:MAIN]
    k_tail = per_head_rows(k[MAIN : MAIN + 8].astype(F32), masks)
    v_tail = per_head_rows(v[MAIN : MAIN + 8].astype(F32), masks)
    qs = jnp.concatenate([q * m for m in low], 0)
    s_tail = mm_nt(q, k_tail)
    scores = by_head(mm_nt(qs, k_main), heads)
    yield
    da = da.astype(BF16)
    das = jnp.concatenate([da * m for m in low], 0)
    col = lax.broadcasted_iota(jnp.int32, (1, LANES), 1)
    valid = (col < 8 * heads) & ((col % 8) < tail_valid)
    lse = [lse_in[:, h : h + 1] for h in range(heads)]
    p_tail = jnp.where(valid, jnp.exp(s_tail - pick(col // 8, lse)), 0.0)
    ps = [jnp.exp(s - t) for s, t in zip(scores, lse)]
    yield
    dp_tail = mm_nt(da, v_tail)
    dps = by_head(mm_nt(das, v_main), heads)
    yield
    x_tail = p_tail * dp_tail
    deltas, dss = [], []
    for h, (p, dp) in enumerate(zip(ps, dps)):
        x = p * dp
        delta = jnp.where((col // 8) == h, x_tail, 0.0)
        for i in range(MAIN // LANES):
            delta = delta + x[:, i * LANES : (i + 1) * LANES]
        delta = jnp.sum(delta, -1, keepdims=True)
        deltas.append(delta)
        dss.append((p * (dp - delta)).astype(BF16))
    ds_tail = (p_tail * (dp_tail - pick(col // 8, deltas))).astype(BF16)
    pbs = jnp.concatenate([p.astype(BF16) for p in ps], 0)
    pb_tail = p_tail.astype(BF16)
    ks = jnp.concatenate([k_main * m for m in low] + [k_tail], 0)
    yield
    dq = mm_nn(jnp.concatenate(dss + [ds_tail], 1), ks)
    dk, dv = mm_tn(jnp.concatenate(dss, 0), qs), mm_tn(pbs, das)
    dk_tail = mm_tn(ds_tail, q)
    dv_tail = mm_tn(pb_tail, da)
    yield
    dq = dq * (HEAD_DIM**-0.5)
    dk_tail = sum(dk_tail[8 * h : 8 * h + 8] * masks[h] for h in range(heads))
    dv_tail = sum(dv_tail[8 * h : 8 * h + 8] * masks[h] for h in range(heads))
    rest = jnp.zeros((gb.shape[0] - MAIN - 8, WIDE), F32)
    dk = jnp.concatenate([dk, dk_tail, rest], 0)
    dv = jnp.concatenate([dv, dv_tail, rest], 0)
    gm = jnp.concatenate([dq, dk, dv], 1).astype(BF16)
    yield
    gn = mm_nn(gm, w_ref[0 : 3 * WIDE, :])
    yield
    last(dq, dv, gm, gn)


def attn_back_kernel(*refs, heads, tail_valid, own, accs, finish):
    it = iter(refs)
    gb_ref, w_ref, mix_ref, lse_ref = (next(it) for _ in range(4))
    acc_refs = [next(it) for _ in range(accs)]
    if finish:
        info, begin_ref, gmid_ref, mask_ref, vec_ref = (next(it) for _ in range(5))
        mid_ref, hsum_ref, qsum_ref = (next(it) for _ in range(3))
    else:
        gn_ref = next(it)
    if own:
        gm_ref, sum_ref = next(it), next(it)
    if finish:
        gtok_ref, keep_ref, give_ref, pack = (next(it) for _ in range(4))
    first = pl.program_id(0) == 0
    per, rows, width = gb_ref.shape
    many, positions = [], []

    def last(i, dq, dv, gm, gn):
        if own:
            gm_ref[i] = gm
            many.append(jnp.concatenate([row_sum(dq), row_sum(dv), jnp.zeros((6, WIDE), F32)], 0))
        for ref in acc_refs:
            gn = gn + ref[i]
        if not finish:
            gn_ref[i] = gn
            return
        xhat, rstd = norm_parts(begin_ref[i])
        grad_begin = gmid_ref[i] + norm_back(xhat, rstd, gn, row(vec_ref, PRE_ATTN_GAIN))
        crop = pl.program_id(0) * per + i
        flagged = flag_wide(mask_ref, crop, rows, MAIN + tail_valid - mask_ref.shape[1], width)
        cleared = jnp.where(flagged, 0.0, grad_begin)
        gtok_ref[i] = cleared
        many.append(
            jnp.concatenate([row_sum(gn * xhat), row_sum(gn), row_sum(grad_begin - cleared)], 0)
        )
        positions.append(grad_begin)

    interleave(
        [
            attention_backward(
                gb_ref[i], w_ref, mix_ref[i], lse_ref[i], heads, tail_valid, functools.partial(last, i)
            )
            for i in range(per)
        ]
    )
    sums, grad_pos = (sum(x[1:], x[0]) if x else None for x in (many, positions))
    if own:
        sum_ref[...] = jnp.where(first, sums, sum_ref[...] + sums)
    if not finish:
        return
    after_mid = rows + 8

    @pl.when(first)
    def _():
        pack[0:rows, :] = grad_pos
        pack[after_mid : after_mid + 3, :] = sums

    @pl.when(jnp.logical_not(first))
    def _():
        pack[0:rows, :] += grad_pos
        pack[after_mid : after_mid + 3, :] += sums

    @pl.when(pl.program_id(0) == pl.num_programs(0) - 1)
    def _():
        pack[rows:after_mid, :] = mid_ref[...]
        pack[after_mid + 3 : after_mid + 4, :] = hsum_ref[0:1, :]
        quarter = width // 4
        small = heads * HEAD_DIM // 4
        deep = keep_ref.shape[1]
        for i in range(4):
            for t in range(2):
                pack[after_mid + 4 + t : after_mid + 5 + t, i * quarter : i * quarter + small] = qsum_ref[
                    t : t + 1, i * small : (i + 1) * small
                ]
        for i in range(4):

            def put(ref):
                part = pack[:, i * quarter : (i + 1) * quarter]
                ref[i // 2] = jnp.concatenate([part[j * deep : (j + 1) * deep] for j in range(4)], 1)

            pl.when(info[1] == i % 2)(functools.partial(put, keep_ref))
            pl.when(info[1] != i % 2)(functools.partial(put, give_ref))


def attn_back(gb, w, mixed, lse, accs, heads, tail_valid, own=False, finish=None):
    crops, rows, width = gb.shape
    per = BACK_PER
    crop = functools.partial(block, per=per)
    args = [gb, w, mixed, lse, *accs]
    specs = [crop(gb.shape), once(w.shape), crop(mixed.shape), crop(lse.shape)]
    specs += [crop(a.shape) for a in accs]
    outs, scratch = [], []
    if finish is not None:
        info, begin, gmid, *tables = finish
        args += [info, begin, gmid, *tables]
        specs += [pl.BlockSpec(memory_space=pltpu.SMEM), crop(begin.shape), crop(gmid.shape)]
        specs += [once(x.shape) for x in tables]
        scratch.append(pltpu.VMEM((rows + 16, width), F32))
    else:
        outs.append(((crops, rows, width), F32, crop))
    if own:
        outs += [((crops, rows, 3 * WIDE), BF16, crop), ((8, WIDE), F32, whole)]
    if finish is not None:
        outs += [
            ((crops, rows, width), F32, crop),
            ((2, (rows + 16) // 4, width), F32, whole),
            ((2, (rows + 16) // 4, width), F32, whole),
        ]
    return pl.pallas_call(
        functools.partial(
            attn_back_kernel,
            heads=heads,
            tail_valid=tail_valid,
            own=own,
            accs=len(accs),
            finish=finish is not None,
        ),
        grid=(crops // per,),
        in_specs=specs,
        out_specs=[kind(shape) for shape, _, kind in outs],
        out_shape=[jax.ShapeDtypeStruct(shape, dtype) for shape, dtype, _ in outs],
        scratch_shapes=scratch,
        compiler_params=params(LAST_MEM if finish is not None else BACK_MEM),
        cost_estimate=cost(31 if finish is not None else 22),
        name="attention_back",
    )(*args)


def gelu_and_slope(h):
    phi = 0.5 * (1.0 + lax.erf(h * (2.0**-0.5)))
    bell = jnp.exp(-0.5 * h * h) * 0.3989422804014327
    return h * phi, phi + h * bell


def mlp_chain(n2, go, w1_ref, w2_ref, bias, last):
    h = mm_nn(n2, w1_ref[...]) + bias[0:1, :]
    ga = mm_nt(go, w2_ref[...])
    yield
    a, slope = gelu_and_slope(h)
    a = a.astype(BF16)
    gh = ga * slope
    gh_low = gh.astype(BF16)
    yield
    out, gn = mm_nn(a, w2_ref[...]), mm_nt(gh_low, w1_ref[...])
    yield
    last(out, gn, a, gh, gh_low)


def place_mlp(info, pieces, w1_ref, w2_ref, bias_ref):
    place_pieces(info, pieces, w1_ref, 0, lambda j: j * PART)
    place_pieces(info, pieces, w2_ref, PART + 8, lambda j: j * PART)
    bias_ref[...] = pieces[0][PART : PART + 8, :]


def placed_mlp(width, hidden):
    return [((width, hidden), BF16), ((hidden, width), BF16), ((8, hidden), F32)]


def mlp_kernel(*refs, ready, counts, accs, own, finish):
    it = iter(refs)
    info, n2_ref, up_ref, vec_ref = (next(it) for _ in range(4))
    shards = [tuple(next(it) for _ in range(3)) for _ in range(ready)]
    pieces = [take_pieces(it, n) for n in counts]
    acc_refs = [(next(it), next(it)) for _ in range(accs)]
    if finish:
        begin_ref, br_ref = next(it), next(it)
        res_ref, gmid_ref, gb_ref, sum_ref = (next(it) for _ in range(4))
    else:
        out_ref, gn_ref = next(it), next(it)
    if own:
        a_ref, gh_ref, go_ref, hsum_ref = (next(it) for _ in range(4))
    first = pl.program_id(0) == 0
    placed = [tuple(next(it) for _ in range(3)) for _ in counts]

    @pl.when(first)
    def _():
        for parts, to in zip(pieces, placed):
            place_mlp(info, parts, *to)

    if not own:
        shards += placed
    per = n2_ref.shape[0]
    many = []

    def last(i, up, grad_output, go, out, gn, a, gh, gh_low):
        if own:
            a_ref[i] = a
            go_ref[i] = go
            gh_ref[i] = gh_low
            many.append(jnp.concatenate([row_sum(gh), jnp.zeros((7, gh.shape[1]), F32)], 0))
        if not finish:
            out_ref[i] = out
            gn_ref[i] = gn
            return
        out = out + row(vec_ref, FC2_BIAS)
        branch = br_ref[i] + row(vec_ref, PROJ_BIAS)
        attn_scale = row(vec_ref, ATTN_SCALE)
        middle = begin_ref[i] + attn_scale * branch
        result = middle + row(vec_ref, MLP_SCALE) * out
        res_ref[i] = result.astype(BF16)
        xhat, rstd = norm_parts(middle)
        gmid = up + norm_back(xhat, rstd, gn, row(vec_ref, PRE_MLP_GAIN))
        gmid_ref[i] = gmid
        gbr = gmid * attn_scale
        gb_ref[i] = gbr.astype(BF16)
        sums = (up * out, grad_output, gn * xhat, gn, gmid * branch, gbr)
        many.append(
            jnp.concatenate([row_sum(x) for x in sums] + [jnp.zeros((2, gn.shape[1]), F32)], 0)
        )

    for i in range(per):
        up = up_ref[i].astype(F32)
        grad_output = up * row(vec_ref, MLP_SCALE)
        go = grad_output.astype(BF16)
        parts = [None] * len(shards)

        def keep(j, *part, parts=parts):
            parts[j] = part

        interleave(
            [
                mlp_chain(n2_ref[i], go, *shard, functools.partial(keep, j))
                for j, shard in enumerate(shards)
            ]
        )
        out, gn = parts[0][:2]
        for o_ref, g_ref in acc_refs:
            out, gn = out + o_ref[i], gn + g_ref[i]
        if len(parts) > 1:
            rest = [parts[1][k] + parts[2][k] for k in range(2)]
            out, gn = out + rest[0], gn + rest[1]
        last(i, up, grad_output, go, out, gn, *parts[-1][2:])
    if many:
        ref = sum_ref if finish else hsum_ref
        sums = sum(many[1:], many[0])
        ref[...] = jnp.where(first, sums, ref[...] + sums)


def mlp(n2, up, vecs, ready, pieces, info, accs, hidden, own=False, finish=None):
    crops, rows, width = n2.shape
    per = MLP_PER
    crop = functools.partial(block, per=per)
    args, specs = [], []

    def add(x, spec):
        args.append(x)
        specs.append(spec)

    add(info, pl.BlockSpec(memory_space=pltpu.SMEM))
    add(n2, crop(n2.shape))
    add(up, crop(up.shape))
    add(vecs, once(vecs.shape))
    for w in sum(ready, ()):
        add(w, once(w.shape))
    for x in sum(pieces, []):
        add(x, once(x.shape))
    for pair in accs:
        for a in pair:
            add(a, crop(a.shape))
    full = (crops, rows, width)
    scratch = []
    if finish is not None:
        add(finish[0], crop(finish[0].shape))
        add(finish[1], crop(finish[1].shape))
        outs = [
            (full, BF16, crop),
            (full, F32, crop),
            (full, BF16, crop),
            ((8, width), F32, whole),
        ]
    else:
        outs = [(full, F32, crop), (full, F32, crop)]
    placed = placed_mlp(width, hidden) * len(pieces)
    if own:
        outs += [((crops, rows, hidden), BF16, crop)] * 2 + [(full, BF16, crop), ((8, hidden), F32, whole)]
        outs += [(shape, dtype, once) for shape, dtype in placed]
    else:
        scratch = [pltpu.VMEM(shape, dtype) for shape, dtype in placed]
    return pl.pallas_call(
        functools.partial(
            mlp_kernel,
            ready=len(ready),
            counts=tuple(len(x) for x in pieces),
            accs=len(accs),
            own=own,
            finish=finish is not None,
        ),
        grid=(crops // per,),
        in_specs=specs,
        out_specs=[kind(shape) for shape, _, kind in outs],
        out_shape=[jax.ShapeDtypeStruct(shape, dtype) for shape, dtype, _ in outs],
        scratch_shapes=scratch,
        compiler_params=params(MLP_MEM if own else VMEM_MOST),
        cost_estimate=cost(16 if own else 45),
        name="mlp",
    )(*args)


def weight_grad_kernel(x1_ref, y1_ref, x2_ref, y2_ref, out_ref, *, parts):
    first, second = mm_tn(x1_ref[...], y1_ref[...]), mm_tn(x2_ref[...], y2_ref[...])
    out_ref[...] = jnp.concatenate([(first, second)[i][:, lo:hi] for i, lo, hi in parts], 1)


def weight_grads(x1, y1, x2, y2, parts):
    rows, width = x1.shape
    col = pl.BlockSpec((rows, WIDE), lambda i: (0, i))
    wide = sum(hi - lo for _, lo, hi in parts)
    return pl.pallas_call(
        functools.partial(weight_grad_kernel, parts=parts),
        grid=(width // WIDE,),
        in_specs=[col, once(y1.shape), col, once(y2.shape)],
        out_specs=pl.BlockSpec((WIDE, wide), lambda i: (i, 0)),
        out_shape=jax.ShapeDtypeStruct((width, wide), F32),
        compiler_params=params(GRAD_MEM),
        cost_estimate=cost(10),
        name="weight_grads",
    )(x1, y1, x2, y2)


def plane_perm(inner, outer, move):
    pairs = []
    for i in range(inner):
        for o in range(outer):
            j, r = move(i, o)
            pairs.append((i * outer + o, j * outer + r))
    return pairs


def after(x, *others):
    return lax.optimization_barrier((x, *others))[0] if others else x


def fence(new, *done):
    return lax.optimization_barrier((*new, *done))[: len(new)]


class PlaneSum:
    def __init__(self, sizes, inner, mine, give):
        _, self.inner_n, self.outer_n = sizes
        self.side = inner // 2
        self.inner = inner
        self.mine, self.give = mine, give

    def cores(self):
        self.one = lax.ppermute(self.give, "inner", [(i, i ^ 1) for i in range(self.inner_n)])
        return self.one

    def pick(self, side):
        at = side if self.mine.shape[0] == 2 else 2 * side + self.inner % 2
        return sum(lax.dynamic_index_in_dim(x, at, 0, keepdims=False) for x in (self.mine, self.one))

    def sides(self, lo=0, hi=None):
        give = self.pick(1 - self.side)[:, lo:hi]
        return lax.ppermute(give, "inner", [(i, i ^ 2) for i in range(self.inner_n)])

    def total(self, two, lo=0, hi=None):
        return self.pick(self.side)[:, lo:hi] + two


def sum_groups(x, outer_n):
    k = 1
    while k < outer_n:
        x = x + lax.ppermute(x, "outer", [(o, o ^ k) for o in range(outer_n)])
        k *= 2
    return x


def leave_kernel(x_ref, qkv_ref, proj_ref):
    side = proj_ref.shape[0]
    for t in range(3):
        qkv_ref[t] = x_ref[:, t * side : (t + 1) * side]
    proj_ref[...] = x_ref[:, 3 * side : 4 * side].T


def leave(x, side):
    rows = x.shape[0]
    return pl.pallas_call(
        leave_kernel,
        out_shape=[
            jax.ShapeDtypeStruct((3, rows, side), F32),
            jax.ShapeDtypeStruct((side, rows), F32),
        ],
        compiler_params=params(16),
        cost_estimate=cost(2),
        name="leave",
    )(x)


def per_device(
    sizes,
    tokens,
    patch_mask,
    cotangent,
    mask_token,
    pos_embed,
    pre_attn_gain,
    pre_attn_bias,
    qkv_weight,
    qv_bias,
    proj_weight,
    proj_bias,
    attn_scale,
    pre_mlp_gain,
    pre_mlp_bias,
    fc1_weight,
    fc1_bias,
    fc2_weight,
    fc2_bias,
    mlp_scale,
):
    tensor_n, inner_n, outer_n = sizes
    crops, seq, width = tokens.shape
    head_width = qkv_weight.shape[2]
    heads = head_width // HEAD_DIM
    hidden = fc1_weight.shape[1]
    rows = -(-seq // 16) * 16
    tail_valid = seq - MAIN
    t = lax.axis_index("tensor")
    inner = lax.axis_index("inner")
    outer = lax.axis_index("outer")
    place = inner * 2 + outer % 2
    info = jnp.stack([place, inner % 2]).astype(jnp.int32)

    qkv_rows = qkv_weight.transpose(1, 2, 0).reshape(3 * head_width, width)

    def eighth(x):
        return lax.dynamic_slice_in_dim(x, place * PART, PART, 0).astype(F32)

    ones = jnp.ones((heads,), F32)
    zeros = jnp.zeros((WIDE,), F32)
    attn_bias = jnp.concatenate(
        [qv_bias[0], zeros[head_width:], zeros, qv_bias[1], ones, zeros[head_width + heads :]]
    )[None, :]
    mlp_bias = fc1_bias[None, :]
    below = jnp.zeros((7, width), F32)
    attn_piece = jnp.concatenate(
        [eighth(jnp.concatenate([qkv_rows, proj_weight], 0)), attn_bias, below], 0
    )
    own_mlp = (fc1_weight, fc2_weight, mlp_bias)
    chunks = ((0, 72), (72, 200))
    perms = (
        plane_perm(inner_n, outer_n, lambda i, o: (i, o ^ 1) if i % 2 else (i ^ 2, o)),
        plane_perm(inner_n, outer_n, lambda i, o: (i ^ 2, o) if i % 2 else (i, o ^ 1)),
        plane_perm(inner_n, outer_n, lambda i, o: (i ^ 1, o)),
    )
    def over_z(x, k):
        return lax.ppermute(x, "tensor", [(i, i ^ k) for i in range(tensor_n)])

    along, far, peer = (functools.partial(lax.ppermute, axis_name=PLANE, perm=p) for p in perms)

    vecs = jnp.stack(
        [
            mask_token,
            pre_attn_gain,
            pre_attn_bias,
            proj_bias,
            attn_scale,
            pre_mlp_gain,
            pre_mlp_bias,
            fc2_bias,
            mlp_scale,
        ]
    )
    run = functools.partial(attn, heads=heads, tail_valid=tail_valid)
    layer = functools.partial(mlp, hidden=hidden)

    quarter = width // inner_n

    def plane_sum(x):
        x = x.reshape(inner_n, quarter, -1)
        return PlaneSum(sizes, inner, x, x)

    def pair(first, second):
        return jnp.stack([first, second])

    a1, a2 = over_z(attn_piece, 1), over_z(attn_piece, 2)
    begin, n1, *pieces = enter(
        info, tokens.transpose(1, 0, 2), patch_mask, vecs, pos_embed, rows, own_mlp, chunks
    )

    n1, a1, a2, m2_piece = fence((n1, a1, a2, pieces[0]))
    b1, b2 = along(a1), along(a2)
    a3 = over_z(a2, 1)
    m2 = [over_z(m2_piece, 2)]
    half = crops // 2
    own_w = [attn_bias, qkv_rows, proj_weight]
    early = run(n1, own_w, None, [], span=(0, half))

    both1 = pair(a1, b1)
    cot, both1, a3, m1_piece = fence(
        (cotangent.transpose(1, 0, 2), both1, a3, pieces[0]), early[0], b2, *m2
    )
    c1, d1 = far(both1), peer(both1)
    m1 = [over_z(m1_piece, 1)]
    up = upstream(cot, rows)

    both2 = pair(a2, b2)
    n1, c1, both2, a3, m1_piece = fence((n1, c1, both2, a3, pieces[1]), up, d1, *m1)
    e1 = peer(c1)
    c2 = far(both2)
    b3 = along(a3)
    m1.append(over_z(m1_piece, 1))
    br0, mix0, lse0, w_0, att0 = run(n1, own_w, None, [], span=(half, crops), into=early)

    both3, four2 = pair(a3, b3), jnp.concatenate([both2, c2], 0)
    m1 = jnp.concatenate(m1, 0)
    n1, four2, both3, m1, m2_piece = fence(
        (n1, four2, both3, m1, pieces[1]), br0, e1
    )
    de2 = peer(four2)
    c3 = far(both3)
    f1 = along(m1)
    m2.append(over_z(m2_piece, 2))
    br1, mix1, lse1, w_1 = run(n1, [both1, c1, d1, e1], info, [br0])

    four3, two1 = jnp.concatenate([both3, c3], 0), pair(m1, f1)
    m2 = jnp.concatenate(m2, 0)
    n1, four3, two1, m2 = fence((n1, four3, two1, m2), br1, de2)
    de3 = peer(four3)
    g1, h1 = far(two1), peer(two1)
    m3 = over_z(m2, 1)
    br2, mix2, lse2, w_2 = run(n1, [four2, de2], info, [])

    n1, g1, m2, m3 = fence((n1, g1, m2, m3), br2, de3, h1)
    i1 = peer(g1)
    f2 = along(m2)
    g3, h3 = [far(m3)], [peer(m3)]
    br, mix3, lse3, w_3, n2 = run(n1, [four3, de3], info, [br2, br1], finish=(begin, vecs))

    two2 = pair(m2, f2)
    n2, two2, f2, g3_own = fence((n2, two2, f2, *g3), i1, *h3)
    g2, h2 = far(two2), peer(two2)
    f3 = over_z(f2, 1)
    i3 = [peer(g3_own)]
    out0, gn0, a0, gh0, go0, hsum, *mlp_1 = layer(
        n2, up, vecs, [own_mlp], [[two1, g1, h1, i1]], info, [], own=True
    )

    flat = lambda x: x.reshape(crops * rows, -1)
    n2, g2, f3 = fence((n2, g2, f3), out0, h2, *i3)
    i2 = peer(g2)
    g3.append(far(f3))
    h3.append(peer(f3))
    mlp_grads = weight_grads(
        flat(n2), flat(gh0), flat(go0), flat(a0), ((0, 0, hidden), (1, 0, hidden))
    )

    n2, last_part, mlp_grads = fence((n2, g3[1], mlp_grads), i2, h3[1])
    i3.append(peer(last_part))
    n2, mlp_grads = fence((n2, mlp_grads), i3[1])

    mlp_sum = plane_sum(mlp_grads)
    s1 = mlp_sum.cores()
    result, gmid, gb, mid_sums = layer(
        n2,
        up,
        vecs,
        [tuple(mlp_1)],
        [[two2, g2, h2, i2], [m3, f3, *g3, *h3, *i3]],
        info,
        [(out0, gn0)],
        finish=(begin, br),
    )

    back = functools.partial(attn_back, heads=heads, tail_valid=tail_valid)
    gb, mlp_sum.one = fence((gb, s1))
    s2 = mlp_sum.sides(0, hidden)
    gn0, gm0, qv_sums = back(gb, w_0, mix0, lse0, [], own=True)
    attn_grads = weight_grads(
        flat(n1),
        flat(gm0),
        flat(gb),
        flat(att0),
        tuple((0, i * WIDE, i * WIDE + head_width) for i in range(3)) + ((1, 0, head_width),),
    )

    gb, attn_grads, s2, mlp_sum.one = fence((gb, attn_grads, s2, mlp_sum.one))
    attn_sum = plane_sum(attn_grads)
    s1 = attn_sum.cores()
    grad_fc1 = sum_groups(mlp_sum.total(s2, 0, hidden), outer_n)
    s3 = mlp_sum.sides(hidden)
    (gn1,) = back(gb, w_1, mix1, lse1, [gn0])

    gb, attn_sum.one, s3 = fence((gb, s1, s3), gn1, grad_fc1)
    s2 = attn_sum.sides()
    grad_fc2 = sum_groups(mlp_sum.total(s3, hidden), outer_n)
    (gn2,) = back(gb, w_2, mix2, lse2, [])

    gb, s2 = fence((gb, s2), gn2, grad_fc2)
    shares_attn = sum_groups(attn_sum.total(s2), outer_n)
    gtok, keep, give = back(
        gb,
        w_3,
        mix3,
        lse3,
        [gn2, gn1],
        finish=(info, begin, gmid, patch_mask, vecs, mid_sums, hsum, qv_sums),
    )

    small = head_width // inner_n
    small_sum = PlaneSum(sizes, inner, keep, after(give, shares_attn))
    small_sum.cores()
    give, mine = small_sum.pick(1 - small_sum.side), small_sum.pick(small_sum.side)
    if outer_n == 2:
        corner = plane_perm(inner_n, outer_n, lambda i, o: (i ^ 2, o ^ 1))
        give, mine, result, gtok = fence((give, mine, result, gtok))
        near = lax.ppermute(give, "inner", [(i, i ^ 2) for i in range(inner_n)])
        over = lax.ppermute(mine, "outer", [(0, 1), (1, 0)])
        across = lax.ppermute(give, PLANE, corner)
        small_sums = (mine + near) + (over + across)
    else:
        small_sums = sum_groups(small_sum.total(small_sum.sides()), outer_n)
    result, gtok = by_token([result, gtok], seq)
    small_sums = small_sums.reshape(-1, inner_n, quarter).transpose(1, 0, 2).reshape(-1, quarter)
    grad_qkv, grad_proj = leave(shares_attn, head_width)
    mid = lambda i: small_sums[rows + i]
    vec = lambda i: small_sums[rows + 8 + i]
    return (
        result.transpose(1, 0, 2),
        gtok.transpose(1, 0, 2),
        vec(2),
        small_sums[:seq],
        vec(0),
        vec(1),
        grad_qkv.transpose(1, 0, 2),
        jnp.stack([vec(4)[:small], vec(5)[:small]]),
        grad_proj,
        mid(5),
        mid(4),
        mid(2),
        mid(3),
        grad_fc1,
        vec(3),
        grad_fc2.T,
        mid(1),
        mid(0),
    )


def solution(mesh):
    in_specs = (
        P(("inner", "outer"), None, None),
        P(("inner", "outer"), None),
        P(("inner", "outer"), None, None),
        P(),
        P(),
        P(),
        P(),
        P(None, None, "tensor"),
        P(None, "tensor"),
        P("tensor", None),
        P(),
        P(),
        P(),
        P(),
        P(None, "tensor"),
        P("tensor"),
        P("tensor", None),
        P(),
        P(),
    )
    out_specs = (
        P(("inner", "outer"), None, None),
        P(("inner", "outer"), None, None),
        P("inner"),
        P(None, "inner"),
        P("inner"),
        P("inner"),
        P("inner", None, "tensor"),
        P(None, ("tensor", "inner")),
        P("tensor", "inner"),
        P("inner"),
        P("inner"),
        P("inner"),
        P("inner"),
        P("inner", "tensor"),
        P(("tensor", "inner")),
        P("tensor", "inner"),
        P("inner"),
        P("inner"),
    )
    sizes = tuple(mesh.shape[name] for name in ("tensor", "inner", "outer"))
    return jax.shard_map(
        functools.partial(per_device, sizes),
        mesh=mesh,
        in_specs=in_specs,
        out_specs=out_specs,
        check_vma=False,
    )
```

```python
import functools

import jax
import jax.numpy as jnp
from jax import lax
from jax.experimental import pallas as pl
from jax.experimental.pallas import tpu as pltpu
from jax.sharding import PartitionSpec as P

HEAD_DIM = 64
EPS = 1e-06
F32 = jnp.float32
BF16 = jnp.bfloat16
NEG = -1e30
LANES = 128
WIDE = 256
MAIN = 256
MIB = 1024 * 1024
ENTER_MEM, ATTN_MEM, MLP_MEM, GRAD_MEM, BACK_MEM, LAST_MEM = 50, 50, 50, 50, 50, 50
VMEM_MOST = 60
PLANE = ("inner", "outer")
PART = 96


def mm_nt(a, b):
    return lax.dot_general(a, b, (((1,), (1,)), ((), ())), preferred_element_type=F32)


def mm_nn(a, b):
    return lax.dot_general(a, b, (((1,), (0,)), ((), ())), preferred_element_type=F32)


def mm_tn(a, b):
    return lax.dot_general(a, b, (((0,), (0,)), ((), ())), preferred_element_type=F32)


ATTN_PER, BACK_PER, LAST_PER, MLP_PER = 2, 1, 1, 1


def cost(us):
    return pl.CostEstimate(flops=int(us * 1.15e9), bytes_accessed=1 << 20, transcendentals=0)


(
    MASK_TOKEN,
    PRE_ATTN_GAIN,
    PRE_ATTN_BIAS,
    PROJ_BIAS,
    ATTN_SCALE,
    PRE_MLP_GAIN,
    PRE_MLP_BIAS,
    FC2_BIAS,
    MLP_SCALE,
) = range(9)


def row(ref, i):
    return ref[i : i + 1, :]


def params(limit):
    return pltpu.CompilerParams(vmem_limit_bytes=limit * MIB)


def block(shape, per=1):
    return pl.BlockSpec((per,) + tuple(shape[1:]), lambda c: (c,) + (0,) * (len(shape) - 1))


def whole(shape):
    return pl.BlockSpec(tuple(shape), lambda c: (0,) * len(shape))


def once(shape):
    return pl.BlockSpec(tuple(shape), lambda c: (0,) * len(shape), pipeline_mode=pl.Buffered(1))


def row_sum(x):
    return jnp.sum(x, 0, keepdims=True)


def norm_parts(v):
    center = v - jnp.mean(v, -1, keepdims=True)
    rstd = lax.rsqrt(jnp.mean(center * center, -1, keepdims=True) + EPS)
    return center * rstd, rstd


def norm_back(xhat, rstd, u, gain):
    gu = u * gain
    return (
        gu - jnp.mean(gu, -1, keepdims=True) - xhat * jnp.mean(gu * xhat, -1, keepdims=True)
    ) * rstd


def put_columns(ref, rows, x):
    for j in range(ref.shape[0]):
        ref[j, rows, :] = x[:, j * LANES : (j + 1) * LANES]


def get_columns(ref, rows):
    return jnp.concatenate([ref[j, rows, :] for j in range(ref.shape[0])], 1)


def flag_lanes(mask_ref, crop, rows, prefix):
    crop_mask = mask_ref[pl.ds(crop, 1), :]
    patches = crop_mask.shape[1]
    ones = jnp.broadcast_to((crop_mask == 1).astype(F32), (LANES, patches)).astype(BF16)
    token = lax.broadcasted_iota(jnp.int32, (rows, patches), 0)
    patch = lax.broadcasted_iota(jnp.int32, (rows, patches), 1)
    return mm_nt((token == patch + prefix).astype(F32).astype(BF16), ones)


def flag_wide(mask_ref, crop, rows, prefix, width):
    return jnp.concatenate([flag_lanes(mask_ref, crop, rows, prefix)] * (width // LANES), 1) > 0.5


def by_crop(src_ref, scratch):
    seq, crops, _ = src_ref.shape
    step = 29 if seq % 29 == 0 else 1

    @pl.when(pl.program_id(0) == 0)
    def _():
        def move(i, carry):
            dst = pl.ds(pl.multiple_of(i * (step * crops), crops), step * crops)
            put_columns(scratch, dst, src_ref[pl.ds(i * step, step)].astype(F32).reshape(step * crops, -1))
            return carry

        lax.fori_loop(0, seq // step, move, 0)
        scratch[:, seq * crops :, :] = jnp.zeros_like(scratch[:, seq * crops :, :])

    return get_columns(scratch, pl.ds(pl.program_id(0), scratch.shape[1] // crops, stride=crops))


def enter_kernel(info, tok_ref, mask_ref, vec_ref, pos_ref, w1_ref, w2_ref, bias_ref, *refs, chunks):
    begin_ref, n1_ref, *chunk_refs, scratch = refs

    @pl.when(pl.program_id(0) == 0)
    def _():
        mine = pl.ds(pl.multiple_of(info[0] * PART, 32), PART)
        hidden = w1_ref.shape[1]
        below = jnp.zeros((7, hidden), F32)
        piece = [w1_ref[mine, :].astype(F32), bias_ref[...], below, w2_ref[mine, :].astype(F32)]
        piece = jnp.concatenate(piece, 0)
        for (lo, hi), ref in zip(chunks, chunk_refs):
            ref[...] = piece[lo:hi]

    tok = by_crop(tok_ref, scratch)
    rows = tok.shape[0]
    near = pos_ref.shape[0] // 8 * 8
    rest = pos_ref.shape[0] - near
    pos = [pos_ref[0:near, :]]
    if rest:
        pos.append(jnp.concatenate([pos_ref[near:, :], jnp.zeros((8 - rest, tok.shape[1]), F32)], 0))
    pos.append(jnp.zeros((rows - near - 8 * (rest > 0), tok.shape[1]), F32))
    pos = jnp.concatenate(pos, 0)
    prefix = tok_ref.shape[0] - mask_ref.shape[1]
    flagged = flag_wide(mask_ref, pl.program_id(0), rows, prefix, tok.shape[1])
    begin = jnp.where(flagged, row(vec_ref, MASK_TOKEN), tok) + pos
    begin_ref[0] = begin
    xhat, _ = norm_parts(begin)
    n1_ref[0] = (xhat * row(vec_ref, PRE_ATTN_GAIN) + row(vec_ref, PRE_ATTN_BIAS)).astype(BF16)


def enter(info, tok, mask, vecs, pos, rows, own_mlp, chunks):
    seq, crops, width = tok.shape
    shape = (crops, rows, width)
    args = (tok, mask, vecs, pos, *own_mlp)
    small = [(hi - lo, width) for lo, hi in chunks]
    return pl.pallas_call(
        functools.partial(enter_kernel, chunks=chunks),
        grid=(crops,),
        in_specs=[pl.BlockSpec(memory_space=pltpu.SMEM)] + [once(x.shape) for x in args],
        out_specs=[block(shape)] * 2 + [once(x) for x in small],
        out_shape=[
            jax.ShapeDtypeStruct(shape, F32),
            jax.ShapeDtypeStruct(shape, BF16),
            *(jax.ShapeDtypeStruct(x, F32) for x in small),
        ],
        scratch_shapes=[pltpu.VMEM((width // LANES, rows * crops, LANES), F32)],
        compiler_params=params(ENTER_MEM),
        cost_estimate=cost(7),
        name="enter",
    )(info, *args)


def upstream_kernel(cot_ref, up_ref, scratch):
    up_ref[0] = by_crop(cot_ref, scratch).astype(BF16)


def upstream(cot, rows):
    seq, crops, width = cot.shape
    shape = (crops, rows, width)
    return pl.pallas_call(
        upstream_kernel,
        grid=(crops,),
        in_specs=[once(cot.shape)],
        out_specs=block(shape),
        out_shape=jax.ShapeDtypeStruct(shape, BF16),
        scratch_shapes=[pltpu.VMEM((width // LANES, rows * crops, LANES), F32)],
        compiler_params=params(ENTER_MEM),
        cost_estimate=cost(6),
        name="upstream",
    )(cot)


def by_token_kernel(*refs):
    arrays = (len(refs) - 1) // 2
    scratch = refs[-1]
    for x_ref, out_ref in zip(refs[:arrays], refs[arrays:-1]):
        crops, step, _ = x_ref.shape

        def one(c, carry, x_ref=x_ref, crops=crops, step=step):
            put_columns(scratch, pl.ds(c, step, stride=crops), x_ref[c].astype(F32))
            return carry

        lax.fori_loop(0, crops, one, 0)
        out = get_columns(scratch, slice(None))
        out_ref[...] = out.reshape(out_ref.shape).astype(out_ref.dtype)


def by_token(arrays, seq):
    crops, rows, width = arrays[0].shape
    step = 48
    return pl.pallas_call(
        by_token_kernel,
        grid=(-(-seq // step),),
        in_specs=[pl.BlockSpec((crops, step, width), lambda i: (0, i, 0))] * len(arrays),
        out_specs=[pl.BlockSpec((step, crops, width), lambda i: (i, 0, 0))] * len(arrays),
        out_shape=[jax.ShapeDtypeStruct((seq, crops, width), x.dtype) for x in arrays],
        scratch_shapes=[pltpu.VMEM((width // LANES, step * crops, LANES), F32)],
        compiler_params=params(14),
        cost_estimate=cost(8),
        name="by_token",
    )(*arrays)


def head_masks(heads):
    lane = lax.broadcasted_iota(jnp.int32, (1, WIDE), 1)
    return [((lane // HEAD_DIM) == h).astype(F32) for h in range(heads)], lane


def per_head_rows(x, masks):
    parts = [x * m for m in masks]
    parts.append(jnp.zeros((LANES - 8 * len(masks), x.shape[1]), F32))
    return jnp.concatenate(parts, 0).astype(BF16)


def pick(index, parts):
    out = parts[-1]
    for h in range(len(parts) - 2, -1, -1):
        out = jnp.where(index == h, parts[h], out)
    return out


def interleave(chains):
    live, waiting = [], list(chains)
    while live or waiting:
        live += waiting[:1]
        del waiting[:1]
        live = [c for c in live[::-1] if next(c, True) is None][::-1]


def by_head(x, heads):
    rows = x.shape[0] // heads
    return [x[h * rows : (h + 1) * rows] for h in range(heads)]


def attention_forward(n1, w_ref, bias, heads, tail_valid, last):
    masks, lane = head_masks(heads)
    low = [m.astype(BF16) for m in masks]
    head_width = heads * HEAD_DIM
    mixed = (mm_nt(n1, w_ref[0 : 3 * WIDE, :]) + bias).astype(BF16)
    yield
    q = mixed[:, 0:WIDE] * jnp.asarray(HEAD_DIM**-0.5, BF16)
    k, v = mixed[:, WIDE : 2 * WIDE], mixed[:, 2 * WIDE : 3 * WIDE]
    mixed = jnp.concatenate([q, k, v], 1)
    k_main, v_main = k[0:MAIN], v[0:MAIN]
    v_masks = [m + (lane == head_width + h).astype(F32) for h, m in enumerate(masks)]
    k_tail = per_head_rows(k[MAIN : MAIN + 8].astype(F32), masks)
    v_tail = per_head_rows(v[MAIN : MAIN + 8].astype(F32), v_masks)
    col = lax.broadcasted_iota(jnp.int32, (1, LANES), 1)
    valid = (col < 8 * heads) & ((col % 8) < tail_valid)
    qs = jnp.concatenate([q * m for m in low], 0)
    vs = jnp.concatenate([v_main * m.astype(BF16) for m in v_masks] + [v_tail], 0)
    yield
    s_tail = mm_nt(q, k_tail)
    scores = by_head(mm_nt(qs, k_main), heads)
    yield
    s_tail = jnp.where(valid, s_tail, NEG)
    tops, exps = [], []
    for h, s in enumerate(scores):
        top = jnp.where((col // 8) == h, s_tail, NEG)
        for i in range(MAIN // LANES):
            top = jnp.maximum(top, s[:, i * LANES : (i + 1) * LANES])
        top = jnp.max(top, -1, keepdims=True)
        tops.append(top)
        exps.append(jnp.exp(s - top).astype(BF16))
    exps.append(jnp.exp(s_tail - pick(col // 8, tops)).astype(BF16))
    yield
    total = mm_nn(jnp.concatenate(exps, 1), vs)
    yield
    sums = [total[:, head_width + h : head_width + h + 1] for h in range(heads)]
    scale = pick(lane // HEAD_DIM, [1.0 / s for s in sums])
    attended = (total * scale).astype(BF16)
    log_total = pick(col, [t + jnp.log(s) for t, s in zip(tops, sums)])
    yield
    branch = mm_nn(attended, w_ref[3 * WIDE : 4 * WIDE, :])
    yield
    last(mixed, log_total, attended, branch)


def take_pieces(it, count):
    found = []
    for ref in (next(it) for _ in range(count)):
        found += [ref] if len(ref.shape) == 2 else [ref.at[i] for i in range(ref.shape[0])]
    return found


def place_pieces(info_ref, pieces, out_ref, base, first):
    p, core = info_ref[0], info_ref[1]
    q = p ^ 2
    a_bit = jnp.where(core == 0, 4, 1)
    b_bit = 5 - a_bit
    idents = (p, p ^ a_bit, p ^ b_bit, p ^ 5, q, q ^ b_bit, q ^ a_bit, q ^ 5)
    for ref, ident in zip(pieces, idents, strict=True):
        dst = pl.multiple_of(first(ident), 32)

        def some(i, carry, ref=ref, dst=dst):
            at = pl.multiple_of(i * 32, 32)
            out_ref[pl.ds(dst + at, 32), :] = ref[pl.ds(base + at, 32), :].astype(BF16)
            return carry

        lax.fori_loop(0, PART // 32, some, 0)


def attn_kernel(*refs, heads, tail_valid, own, into, accs, finish, gathers):
    it = iter(refs)
    if own:
        n1_ref, bias_ref, qkv_ref, proj_ref = (next(it) for _ in range(4))
        bias = bias_ref[...]
    else:
        info, n1_ref = next(it), next(it)
        pieces = take_pieces(it, gathers)
        bias = pieces[0][PART : PART + 1, :]
    acc_refs = [next(it) for _ in range(accs)]
    if finish:
        begin_ref, vec_ref = next(it), next(it)
    for _ in range(into):
        next(it)
    br_ref, mix_ref, lse_ref, w_ref = (next(it) for _ in range(4))

    @pl.when(pl.program_id(0) == 0)
    def _():
        width = heads * HEAD_DIM
        for i in range(4):
            w_ref[i * WIDE + width : (i + 1) * WIDE, :] = jnp.zeros((WIDE - width, w_ref.shape[1]), BF16)
        if own:
            for i in range(3):
                w_ref[i * WIDE : i * WIDE + width, :] = qkv_ref[i * width : (i + 1) * width, :]
            w_ref[3 * WIDE : 3 * WIDE + width, :] = proj_ref[...]
        else:
            place_pieces(info, pieces, w_ref, 0, lambda i: (i >> 1) * WIDE + (i & 1) * PART)

    att_ref = next(it) if own else None
    n2_ref = next(it) if finish else None

    def last(i, mixed, log_total, attended, branch):
        mix_ref[i] = mixed
        lse_ref[i] = log_total
        if own:
            att_ref[i] = attended
        for ref in acc_refs:
            branch = branch + ref[i]
        br_ref[i] = branch
        if finish:
            middle = begin_ref[i] + row(vec_ref, ATTN_SCALE) * (branch + row(vec_ref, PROJ_BIAS))
            xhat, _ = norm_parts(middle)
            n2 = xhat * row(vec_ref, PRE_MLP_GAIN) + row(vec_ref, PRE_MLP_BIAS)
            n2_ref[i] = n2.astype(BF16)

    interleave(
        [
            attention_forward(n1_ref[i], w_ref, bias, heads, tail_valid, functools.partial(last, i))
            for i in range(n1_ref.shape[0])
        ]
    )


def attn(n1, weights, info, accs, heads, tail_valid, finish=None, span=None, into=()):
    crops, rows, width = n1.shape
    own = info is None
    lo, hi = span or (0, crops)
    args, specs = [], []

    per = ATTN_PER

    def crop(shape):
        at = lambda c: (c + lo // per,) + (0,) * (len(shape) - 1)
        return pl.BlockSpec((per,) + tuple(shape[1:]), at)

    def add(x, spec):
        args.append(x)
        specs.append(spec)

    if not own:
        add(info, pl.BlockSpec(memory_space=pltpu.SMEM))
    add(n1, crop(n1.shape))
    for w in weights:
        add(w, once(w.shape))
    for a in accs:
        add(a, crop(a.shape))
    if finish is not None:
        add(finish[0], crop(finish[0].shape))
        add(finish[1], once(finish[1].shape))
    outs = [
        ((crops, rows, width), F32, crop),
        ((crops, rows, 3 * WIDE), BF16, crop),
        ((crops, rows, LANES), F32, crop),
        ((4 * WIDE, width), BF16, whole),
    ]
    if own:
        outs.append(((crops, rows, WIDE), BF16, crop))
    if finish is not None:
        outs.append(((crops, rows, width), BF16, crop))
    aliases = {}
    for i, x in enumerate(into):
        if outs[i][2] is crop:
            aliases[len(args)] = i
            add(x, pl.BlockSpec(memory_space=pl.ANY))
    return pl.pallas_call(
        functools.partial(
            attn_kernel,
            heads=heads,
            tail_valid=tail_valid,
            own=own,
            gathers=len(weights),
            into=len(aliases),
            accs=len(accs),
            finish=finish is not None,
        ),
        grid=((hi - lo) // per,),
        in_specs=specs,
        out_specs=[kind(shape) for shape, _, kind in outs],
        out_shape=[jax.ShapeDtypeStruct(shape, dtype) for shape, dtype, _ in outs],
        input_output_aliases=aliases,
        compiler_params=params(ATTN_MEM),
        cost_estimate=cost((21 if finish is not None else 16) * (hi - lo) / crops),
        name="attention",
    )(*args)


def attention_backward(gb, w_ref, mix, lse_in, heads, tail_valid, last):
    masks, lane = head_masks(heads)
    low = [m.astype(BF16) for m in masks]
    da = mm_nt(gb, w_ref[3 * WIDE : 4 * WIDE, :])
    q, k, v = (mix[:, i * WIDE : (i + 1) * WIDE] for i in range(3))
    k_main, v_main = k[0:MAIN], v[0:MAIN]
    k_tail = per_head_rows(k[MAIN : MAIN + 8].astype(F32), masks)
    v_tail = per_head_rows(v[MAIN : MAIN + 8].astype(F32), masks)
    qs = jnp.concatenate([q * m for m in low], 0)
    s_tail = mm_nt(q, k_tail)
    scores = by_head(mm_nt(qs, k_main), heads)
    yield
    da = da.astype(BF16)
    das = jnp.concatenate([da * m for m in low], 0)
    col = lax.broadcasted_iota(jnp.int32, (1, LANES), 1)
    valid = (col < 8 * heads) & ((col % 8) < tail_valid)
    lse = [lse_in[:, h : h + 1] for h in range(heads)]
    p_tail = jnp.where(valid, jnp.exp(s_tail - pick(col // 8, lse)), 0.0)
    ps = [jnp.exp(s - t) for s, t in zip(scores, lse)]
    yield
    dp_tail = mm_nt(da, v_tail)
    dps = by_head(mm_nt(das, v_main), heads)
    yield
    x_tail = p_tail * dp_tail
    deltas, dss = [], []
    for h, (p, dp) in enumerate(zip(ps, dps)):
        x = p * dp
        delta = jnp.where((col // 8) == h, x_tail, 0.0)
        for i in range(MAIN // LANES):
            delta = delta + x[:, i * LANES : (i + 1) * LANES]
        delta = jnp.sum(delta, -1, keepdims=True)
        deltas.append(delta)
        dss.append((p * (dp - delta)).astype(BF16))
    ds_tail = (p_tail * (dp_tail - pick(col // 8, deltas))).astype(BF16)
    pbs = jnp.concatenate([p.astype(BF16) for p in ps], 0)
    pb_tail = p_tail.astype(BF16)
    ks = jnp.concatenate([k_main * m for m in low] + [k_tail], 0)
    yield
    dq = mm_nn(jnp.concatenate(dss + [ds_tail], 1), ks)
    dk, dv = mm_tn(jnp.concatenate(dss, 0), qs), mm_tn(pbs, das)
    dk_tail = mm_tn(ds_tail, q)
    dv_tail = mm_tn(pb_tail, da)
    yield
    dq = dq * (HEAD_DIM**-0.5)
    dk_tail = sum(dk_tail[8 * h : 8 * h + 8] * masks[h] for h in range(heads))
    dv_tail = sum(dv_tail[8 * h : 8 * h + 8] * masks[h] for h in range(heads))
    rest = jnp.zeros((gb.shape[0] - MAIN - 8, WIDE), F32)
    dk = jnp.concatenate([dk, dk_tail, rest], 0)
    dv = jnp.concatenate([dv, dv_tail, rest], 0)
    gm = jnp.concatenate([dq, dk, dv], 1).astype(BF16)
    yield
    gn = mm_nn(gm, w_ref[0 : 3 * WIDE, :])
    yield
    last(dq, dv, gm, gn)


def attn_back_kernel(*refs, heads, tail_valid, own, accs, finish):
    it = iter(refs)
    gb_ref, w_ref, mix_ref, lse_ref = (next(it) for _ in range(4))
    acc_refs = [next(it) for _ in range(accs)]
    if finish:
        info, begin_ref, gmid_ref, mask_ref, vec_ref = (next(it) for _ in range(5))
        mid_ref, hsum_ref, qsum_ref = (next(it) for _ in range(3))
    else:
        gn_ref = next(it)
    if own:
        gm_ref, sum_ref = next(it), next(it)
    if finish:
        gtok_ref, keep_ref, give_ref, pack = (next(it) for _ in range(4))
    first = pl.program_id(0) == 0
    per, rows, width = gb_ref.shape
    many, positions = [], []

    def last(i, dq, dv, gm, gn):
        if own:
            gm_ref[i] = gm
            many.append(jnp.concatenate([row_sum(dq), row_sum(dv), jnp.zeros((6, WIDE), F32)], 0))
        for ref in acc_refs:
            gn = gn + ref[i]
        if not finish:
            gn_ref[i] = gn
            return
        xhat, rstd = norm_parts(begin_ref[i])
        grad_begin = gmid_ref[i] + norm_back(xhat, rstd, gn, row(vec_ref, PRE_ATTN_GAIN))
        crop = pl.program_id(0) * per + i
        flagged = flag_wide(mask_ref, crop, rows, MAIN + tail_valid - mask_ref.shape[1], width)
        cleared = jnp.where(flagged, 0.0, grad_begin)
        gtok_ref[i] = cleared
        many.append(
            jnp.concatenate([row_sum(gn * xhat), row_sum(gn), row_sum(grad_begin - cleared)], 0)
        )
        positions.append(grad_begin)

    interleave(
        [
            attention_backward(
                gb_ref[i], w_ref, mix_ref[i], lse_ref[i], heads, tail_valid, functools.partial(last, i)
            )
            for i in range(per)
        ]
    )
    sums, grad_pos = (sum(x[1:], x[0]) if x else None for x in (many, positions))
    if own:
        sum_ref[...] = jnp.where(first, sums, sum_ref[...] + sums)
    if not finish:
        return
    after_mid = rows + 8

    @pl.when(first)
    def _():
        pack[0:rows, :] = grad_pos
        pack[after_mid : after_mid + 3, :] = sums

    @pl.when(jnp.logical_not(first))
    def _():
        pack[0:rows, :] += grad_pos
        pack[after_mid : after_mid + 3, :] += sums

    @pl.when(pl.program_id(0) == pl.num_programs(0) - 1)
    def _():
        pack[rows:after_mid, :] = mid_ref[...]
        pack[after_mid + 3 : after_mid + 4, :] = hsum_ref[0:1, :]
        quarter = width // 4
        small = heads * HEAD_DIM // 4
        deep = keep_ref.shape[1]
        for i in range(4):
            for t in range(2):
                pack[after_mid + 4 + t : after_mid + 5 + t, i * quarter : i * quarter + small] = qsum_ref[
                    t : t + 1, i * small : (i + 1) * small
                ]
        for i in range(4):

            def put(ref):
                part = pack[:, i * quarter : (i + 1) * quarter]
                ref[i // 2] = jnp.concatenate([part[j * deep : (j + 1) * deep] for j in range(4)], 1)

            pl.when(info[1] == i % 2)(functools.partial(put, keep_ref))
            pl.when(info[1] != i % 2)(functools.partial(put, give_ref))


def attn_back(gb, w, mixed, lse, accs, heads, tail_valid, own=False, finish=None):
    crops, rows, width = gb.shape
    per = BACK_PER if finish is None else LAST_PER
    crop = functools.partial(block, per=per)
    args = [gb, w, mixed, lse, *accs]
    specs = [crop(gb.shape), once(w.shape), crop(mixed.shape), crop(lse.shape)]
    specs += [crop(a.shape) for a in accs]
    outs, scratch = [], []
    if finish is not None:
        info, begin, gmid, *tables = finish
        args += [info, begin, gmid, *tables]
        specs += [pl.BlockSpec(memory_space=pltpu.SMEM), crop(begin.shape), crop(gmid.shape)]
        specs += [once(x.shape) for x in tables]
        scratch.append(pltpu.VMEM((rows + 16, width), F32))
    else:
        outs.append(((crops, rows, width), F32, crop))
    if own:
        outs += [((crops, rows, 3 * WIDE), BF16, crop), ((8, WIDE), F32, whole)]
    if finish is not None:
        outs += [
            ((crops, rows, width), F32, crop),
            ((2, (rows + 16) // 4, width), F32, whole),
            ((2, (rows + 16) // 4, width), F32, whole),
        ]
    return pl.pallas_call(
        functools.partial(
            attn_back_kernel,
            heads=heads,
            tail_valid=tail_valid,
            own=own,
            accs=len(accs),
            finish=finish is not None,
        ),
        grid=(crops // per,),
        in_specs=specs,
        out_specs=[kind(shape) for shape, _, kind in outs],
        out_shape=[jax.ShapeDtypeStruct(shape, dtype) for shape, dtype, _ in outs],
        scratch_shapes=scratch,
        compiler_params=params(LAST_MEM if finish is not None else BACK_MEM),
        cost_estimate=cost(31 if finish is not None else 22),
        name="attention_back",
    )(*args)


def gelu_and_slope(h):
    phi = 0.5 * (1.0 + lax.erf(h * (2.0**-0.5)))
    bell = jnp.exp(-0.5 * h * h) * 0.3989422804014327
    return h * phi, phi + h * bell


def mlp_chain(n2, go, w1_ref, w2_ref, bias, last):
    h = mm_nn(n2, w1_ref[...]) + bias[0:1, :]
    ga = mm_nt(go, w2_ref[...])
    yield
    a, slope = gelu_and_slope(h)
    a = a.astype(BF16)
    gh = ga * slope
    gh_low = gh.astype(BF16)
    yield
    out, gn = mm_nn(a, w2_ref[...]), mm_nt(gh_low, w1_ref[...])
    yield
    last(out, gn, a, gh, gh_low)


def place_mlp(info, pieces, w1_ref, w2_ref, bias_ref):
    place_pieces(info, pieces, w1_ref, 0, lambda j: j * PART)
    place_pieces(info, pieces, w2_ref, PART + 8, lambda j: j * PART)
    bias_ref[...] = pieces[0][PART : PART + 8, :]


def placed_mlp(width, hidden):
    return [((width, hidden), BF16), ((hidden, width), BF16), ((8, hidden), F32)]


def mlp_kernel(*refs, ready, counts, accs, own, finish):
    it = iter(refs)
    info, n2_ref, up_ref, vec_ref = (next(it) for _ in range(4))
    shards = [tuple(next(it) for _ in range(3)) for _ in range(ready)]
    pieces = [take_pieces(it, n) for n in counts]
    acc_refs = [(next(it), next(it)) for _ in range(accs)]
    if finish:
        begin_ref, br_ref = next(it), next(it)
        res_ref, gmid_ref, gb_ref, sum_ref = (next(it) for _ in range(4))
    else:
        out_ref, gn_ref = next(it), next(it)
    if own:
        a_ref, gh_ref, go_ref, hsum_ref = (next(it) for _ in range(4))
    first = pl.program_id(0) == 0
    placed = [tuple(next(it) for _ in range(3)) for _ in counts]

    @pl.when(first)
    def _():
        for parts, to in zip(pieces, placed):
            place_mlp(info, parts, *to)

    if not own:
        shards += placed
    per = n2_ref.shape[0]
    many = []

    def last(i, up, grad_output, go, out, gn, a, gh, gh_low):
        if own:
            a_ref[i] = a
            go_ref[i] = go
            gh_ref[i] = gh_low
            many.append(jnp.concatenate([row_sum(gh), jnp.zeros((7, gh.shape[1]), F32)], 0))
        if not finish:
            out_ref[i] = out
            gn_ref[i] = gn
            return
        out = out + row(vec_ref, FC2_BIAS)
        branch = br_ref[i] + row(vec_ref, PROJ_BIAS)
        attn_scale = row(vec_ref, ATTN_SCALE)
        middle = begin_ref[i] + attn_scale * branch
        result = middle + row(vec_ref, MLP_SCALE) * out
        res_ref[i] = result.astype(BF16)
        xhat, rstd = norm_parts(middle)
        gmid = up + norm_back(xhat, rstd, gn, row(vec_ref, PRE_MLP_GAIN))
        gmid_ref[i] = gmid
        gbr = gmid * attn_scale
        gb_ref[i] = gbr.astype(BF16)
        sums = (up * out, grad_output, gn * xhat, gn, gmid * branch, gbr)
        many.append(
            jnp.concatenate([row_sum(x) for x in sums] + [jnp.zeros((2, gn.shape[1]), F32)], 0)
        )

    for i in range(per):
        up = up_ref[i].astype(F32)
        grad_output = up * row(vec_ref, MLP_SCALE)
        go = grad_output.astype(BF16)
        parts = [None] * len(shards)

        def keep(j, *part, parts=parts):
            parts[j] = part

        interleave(
            [
                mlp_chain(n2_ref[i], go, *shard, functools.partial(keep, j))
                for j, shard in enumerate(shards)
            ]
        )
        out, gn = parts[0][:2]
        for o_ref, g_ref in acc_refs:
            out, gn = out + o_ref[i], gn + g_ref[i]
        if len(parts) > 1:
            rest = [parts[1][k] + parts[2][k] for k in range(2)]
            out, gn = out + rest[0], gn + rest[1]
        last(i, up, grad_output, go, out, gn, *parts[-1][2:])
    if many:
        ref = sum_ref if finish else hsum_ref
        sums = sum(many[1:], many[0])
        ref[...] = jnp.where(first, sums, ref[...] + sums)


def mlp(n2, up, vecs, ready, pieces, info, accs, hidden, own=False, finish=None):
    crops, rows, width = n2.shape
    per = MLP_PER
    crop = functools.partial(block, per=per)
    args, specs = [], []

    def add(x, spec):
        args.append(x)
        specs.append(spec)

    add(info, pl.BlockSpec(memory_space=pltpu.SMEM))
    add(n2, crop(n2.shape))
    add(up, crop(up.shape))
    add(vecs, once(vecs.shape))
    for w in sum(ready, ()):
        add(w, once(w.shape))
    for x in sum(pieces, []):
        add(x, once(x.shape))
    for pair in accs:
        for a in pair:
            add(a, crop(a.shape))
    full = (crops, rows, width)
    scratch = []
    if finish is not None:
        add(finish[0], crop(finish[0].shape))
        add(finish[1], crop(finish[1].shape))
        outs = [
            (full, BF16, crop),
            (full, F32, crop),
            (full, BF16, crop),
            ((8, width), F32, whole),
        ]
    else:
        outs = [(full, F32, crop), (full, F32, crop)]
    placed = placed_mlp(width, hidden) * len(pieces)
    if own:
        outs += [((crops, rows, hidden), BF16, crop)] * 2 + [(full, BF16, crop), ((8, hidden), F32, whole)]
        outs += [(shape, dtype, once) for shape, dtype in placed]
    else:
        scratch = [pltpu.VMEM(shape, dtype) for shape, dtype in placed]
    return pl.pallas_call(
        functools.partial(
            mlp_kernel,
            ready=len(ready),
            counts=tuple(len(x) for x in pieces),
            accs=len(accs),
            own=own,
            finish=finish is not None,
        ),
        grid=(crops // per,),
        in_specs=specs,
        out_specs=[kind(shape) for shape, _, kind in outs],
        out_shape=[jax.ShapeDtypeStruct(shape, dtype) for shape, dtype, _ in outs],
        scratch_shapes=scratch,
        compiler_params=params(MLP_MEM if own else VMEM_MOST),
        cost_estimate=cost(16 if own else 45),
        name="mlp",
    )(*args)


def weight_grad_kernel(x1_ref, y1_ref, x2_ref, y2_ref, out_ref, *, parts):
    first, second = mm_tn(x1_ref[...], y1_ref[...]), mm_tn(x2_ref[...], y2_ref[...])
    out_ref[...] = jnp.concatenate([(first, second)[i][:, lo:hi] for i, lo, hi in parts], 1)


def weight_grads(x1, y1, x2, y2, parts):
    rows, width = x1.shape
    col = pl.BlockSpec((rows, WIDE), lambda i: (0, i))
    wide = sum(hi - lo for _, lo, hi in parts)
    return pl.pallas_call(
        functools.partial(weight_grad_kernel, parts=parts),
        grid=(width // WIDE,),
        in_specs=[col, once(y1.shape), col, once(y2.shape)],
        out_specs=pl.BlockSpec((WIDE, wide), lambda i: (i, 0)),
        out_shape=jax.ShapeDtypeStruct((width, wide), F32),
        compiler_params=params(GRAD_MEM),
        cost_estimate=cost(10),
        name="weight_grads",
    )(x1, y1, x2, y2)


def plane_perm(inner, outer, move):
    pairs = []
    for i in range(inner):
        for o in range(outer):
            j, r = move(i, o)
            pairs.append((i * outer + o, j * outer + r))
    return pairs


def after(x, *others):
    return lax.optimization_barrier((x, *others))[0] if others else x


def fence(new, *done):
    return lax.optimization_barrier((*new, *done))[: len(new)]


class PlaneSum:
    def __init__(self, sizes, inner, mine, give):
        _, self.inner_n, self.outer_n = sizes
        self.side = inner // 2
        self.inner = inner
        self.mine, self.give = mine, give

    def cores(self):
        self.one = lax.ppermute(self.give, "inner", [(i, i ^ 1) for i in range(self.inner_n)])
        return self.one

    def pick(self, side):
        at = side if self.mine.shape[0] == 2 else 2 * side + self.inner % 2
        return sum(lax.dynamic_index_in_dim(x, at, 0, keepdims=False) for x in (self.mine, self.one))

    def sides(self, lo=0, hi=None):
        give = self.pick(1 - self.side)[:, lo:hi]
        return lax.ppermute(give, "inner", [(i, i ^ 2) for i in range(self.inner_n)])

    def total(self, two, lo=0, hi=None):
        return self.pick(self.side)[:, lo:hi] + two


def sum_groups(x, outer_n):
    k = 1
    while k < outer_n:
        x = x + lax.ppermute(x, "outer", [(o, o ^ k) for o in range(outer_n)])
        k *= 2
    return x


def leave_kernel(x_ref, qkv_ref, proj_ref):
    side = proj_ref.shape[0]
    for t in range(3):
        qkv_ref[t] = x_ref[:, t * side : (t + 1) * side]
    proj_ref[...] = x_ref[:, 3 * side : 4 * side].T


def leave(x, side):
    rows = x.shape[0]
    return pl.pallas_call(
        leave_kernel,
        out_shape=[
            jax.ShapeDtypeStruct((3, rows, side), F32),
            jax.ShapeDtypeStruct((side, rows), F32),
        ],
        compiler_params=params(16),
        cost_estimate=cost(2),
        name="leave",
    )(x)


def per_device(
    sizes,
    tokens,
    patch_mask,
    cotangent,
    mask_token,
    pos_embed,
    pre_attn_gain,
    pre_attn_bias,
    qkv_weight,
    qv_bias,
    proj_weight,
    proj_bias,
    attn_scale,
    pre_mlp_gain,
    pre_mlp_bias,
    fc1_weight,
    fc1_bias,
    fc2_weight,
    fc2_bias,
    mlp_scale,
):
    tensor_n, inner_n, outer_n = sizes
    crops, seq, width = tokens.shape
    head_width = qkv_weight.shape[2]
    heads = head_width // HEAD_DIM
    hidden = fc1_weight.shape[1]
    rows = -(-seq // 16) * 16
    tail_valid = seq - MAIN
    t = lax.axis_index("tensor")
    inner = lax.axis_index("inner")
    outer = lax.axis_index("outer")
    place = inner * 2 + outer % 2
    info = jnp.stack([place, inner % 2]).astype(jnp.int32)

    qkv_rows = qkv_weight.transpose(1, 2, 0).reshape(3 * head_width, width)

    def eighth(x):
        return lax.dynamic_slice_in_dim(x, place * PART, PART, 0).astype(F32)

    ones = jnp.ones((heads,), F32)
    zeros = jnp.zeros((WIDE,), F32)
    attn_bias = jnp.concatenate(
        [qv_bias[0], zeros[head_width:], zeros, qv_bias[1], ones, zeros[head_width + heads :]]
    )[None, :]
    mlp_bias = fc1_bias[None, :]
    below = jnp.zeros((7, width), F32)
    attn_piece = jnp.concatenate(
        [eighth(jnp.concatenate([qkv_rows, proj_weight], 0)), attn_bias, below], 0
    )
    own_mlp = (fc1_weight, fc2_weight, mlp_bias)
    chunks = ((0, 72), (72, 200))
    perms = (
        plane_perm(inner_n, outer_n, lambda i, o: (i, o ^ 1) if i % 2 else (i ^ 2, o)),
        plane_perm(inner_n, outer_n, lambda i, o: (i ^ 2, o) if i % 2 else (i, o ^ 1)),
        plane_perm(inner_n, outer_n, lambda i, o: (i ^ 1, o)),
    )
    def over_z(x, k):
        return lax.ppermute(x, "tensor", [(i, i ^ k) for i in range(tensor_n)])

    along, far, peer = (functools.partial(lax.ppermute, axis_name=PLANE, perm=p) for p in perms)

    vecs = jnp.stack(
        [
            mask_token,
            pre_attn_gain,
            pre_attn_bias,
            proj_bias,
            attn_scale,
            pre_mlp_gain,
            pre_mlp_bias,
            fc2_bias,
            mlp_scale,
        ]
    )
    run = functools.partial(attn, heads=heads, tail_valid=tail_valid)
    layer = functools.partial(mlp, hidden=hidden)

    quarter = width // inner_n

    def plane_sum(x):
        x = x.reshape(inner_n, quarter, -1)
        return PlaneSum(sizes, inner, x, x)

    def pair(first, second):
        return jnp.stack([first, second])

    a1, a2 = over_z(attn_piece, 1), over_z(attn_piece, 2)
    begin, n1, *pieces = enter(
        info, tokens.transpose(1, 0, 2), patch_mask, vecs, pos_embed, rows, own_mlp, chunks
    )

    n1, a1, a2, m2_piece = fence((n1, a1, a2, pieces[0]))
    b1, b2 = along(a1), along(a2)
    a3 = over_z(a2, 1)
    m2 = [over_z(m2_piece, 2)]
    half = crops // 2
    own_w = [attn_bias, qkv_rows, proj_weight]
    early = run(n1, own_w, None, [], span=(0, half))

    both1 = pair(a1, b1)
    cot, both1, a3, m1_piece = fence(
        (cotangent.transpose(1, 0, 2), both1, a3, pieces[0]), early[0], b2, *m2
    )
    c1, d1 = far(both1), peer(both1)
    m1 = [over_z(m1_piece, 1)]
    up = upstream(cot, rows)

    both2 = pair(a2, b2)
    n1, c1, both2, a3, m1_piece = fence((n1, c1, both2, a3, pieces[1]), up, d1, *m1)
    e1 = peer(c1)
    c2 = far(both2)
    b3 = along(a3)
    m1.append(over_z(m1_piece, 1))
    br0, mix0, lse0, w_0, att0 = run(n1, own_w, None, [], span=(half, crops), into=early)

    both3, four2 = pair(a3, b3), jnp.concatenate([both2, c2], 0)
    m1 = jnp.concatenate(m1, 0)
    n1, four2, both3, m1, m2_piece = fence(
        (n1, four2, both3, m1, pieces[1]), br0, e1
    )
    de2 = peer(four2)
    c3 = far(both3)
    f1 = along(m1)
    m2.append(over_z(m2_piece, 2))
    br1, mix1, lse1, w_1 = run(n1, [both1, c1, d1, e1], info, [br0])

    four3, two1 = jnp.concatenate([both3, c3], 0), pair(m1, f1)
    m2 = jnp.concatenate(m2, 0)
    n1, four3, two1, m2 = fence((n1, four3, two1, m2), br1, de2)
    de3 = peer(four3)
    g1, h1 = far(two1), peer(two1)
    m3 = over_z(m2, 1)
    br2, mix2, lse2, w_2 = run(n1, [four2, de2], info, [])

    n1, g1, m2, m3 = fence((n1, g1, m2, m3), br2, de3, h1)
    i1 = peer(g1)
    f2 = along(m2)
    g3, h3 = [far(m3)], [peer(m3)]
    br, mix3, lse3, w_3, n2 = run(n1, [four3, de3], info, [br2, br1], finish=(begin, vecs))

    two2 = pair(m2, f2)
    n2, two2, f2, g3_own = fence((n2, two2, f2, *g3), i1, *h3)
    g2, h2 = far(two2), peer(two2)
    f3 = over_z(f2, 1)
    i3 = [peer(g3_own)]
    out0, gn0, a0, gh0, go0, hsum, *mlp_1 = layer(
        n2, up, vecs, [own_mlp], [[two1, g1, h1, i1]], info, [], own=True
    )

    flat = lambda x: x.reshape(crops * rows, -1)
    n2, g2, f3 = fence((n2, g2, f3), out0, h2, *i3)
    i2 = peer(g2)
    g3.append(far(f3))
    h3.append(peer(f3))
    mlp_grads = weight_grads(
        flat(n2), flat(gh0), flat(go0), flat(a0), ((0, 0, hidden), (1, 0, hidden))
    )

    n2, last_part, mlp_grads = fence((n2, g3[1], mlp_grads), i2, h3[1])
    i3.append(peer(last_part))
    n2, mlp_grads = fence((n2, mlp_grads), i3[1])

    mlp_sum = plane_sum(mlp_grads)
    s1 = mlp_sum.cores()
    result, gmid, gb, mid_sums = layer(
        n2,
        up,
        vecs,
        [tuple(mlp_1)],
        [[two2, g2, h2, i2], [m3, f3, *g3, *h3, *i3]],
        info,
        [(out0, gn0)],
        finish=(begin, br),
    )

    back = functools.partial(attn_back, heads=heads, tail_valid=tail_valid)
    gb, mlp_sum.one = fence((gb, s1))
    s2 = mlp_sum.sides(0, hidden)
    gn0, gm0, qv_sums = back(gb, w_0, mix0, lse0, [], own=True)
    attn_grads = weight_grads(
        flat(n1),
        flat(gm0),
        flat(gb),
        flat(att0),
        tuple((0, i * WIDE, i * WIDE + head_width) for i in range(3)) + ((1, 0, head_width),),
    )

    gb, attn_grads, s2, mlp_sum.one = fence((gb, attn_grads, s2, mlp_sum.one))
    attn_sum = plane_sum(attn_grads)
    s1 = attn_sum.cores()
    grad_fc1 = sum_groups(mlp_sum.total(s2, 0, hidden), outer_n)
    s3 = mlp_sum.sides(hidden)
    (gn1,) = back(gb, w_1, mix1, lse1, [gn0])

    gb, attn_sum.one, s3 = fence((gb, s1, s3), gn1, grad_fc1)
    s2 = attn_sum.sides()
    grad_fc2 = sum_groups(mlp_sum.total(s3, hidden), outer_n)
    (gn2,) = back(gb, w_2, mix2, lse2, [])

    gb, s2 = fence((gb, s2), gn2, grad_fc2)
    shares_attn = sum_groups(attn_sum.total(s2), outer_n)
    gtok, keep, give = back(
        gb,
        w_3,
        mix3,
        lse3,
        [gn2, gn1],
        finish=(info, begin, gmid, patch_mask, vecs, mid_sums, hsum, qv_sums),
    )

    small = head_width // inner_n
    small_sum = PlaneSum(sizes, inner, keep, after(give, shares_attn))
    small_sum.cores()
    give, mine = small_sum.pick(1 - small_sum.side), small_sum.pick(small_sum.side)
    if outer_n == 2:
        corner = plane_perm(inner_n, outer_n, lambda i, o: (i ^ 2, o ^ 1))
        give, mine, result, gtok = fence((give, mine, result, gtok))
        near = lax.ppermute(give, "inner", [(i, i ^ 2) for i in range(inner_n)])
        over = lax.ppermute(mine, "outer", [(0, 1), (1, 0)])
        across = lax.ppermute(give, PLANE, corner)
        small_sums = (mine + near) + (over + across)
    else:
        small_sums = sum_groups(small_sum.total(small_sum.sides()), outer_n)
    result, gtok = by_token([result, gtok], seq)
    small_sums = small_sums.reshape(-1, inner_n, quarter).transpose(1, 0, 2).reshape(-1, quarter)
    grad_qkv, grad_proj = leave(shares_attn, head_width)
    mid = lambda i: small_sums[rows + i]
    vec = lambda i: small_sums[rows + 8 + i]
    return (
        result.transpose(1, 0, 2),
        gtok.transpose(1, 0, 2),
        vec(2),
        small_sums[:seq],
        vec(0),
        vec(1),
        grad_qkv.transpose(1, 0, 2),
        jnp.stack([vec(4)[:small], vec(5)[:small]]),
        grad_proj,
        mid(5),
        mid(4),
        mid(2),
        mid(3),
        grad_fc1,
        vec(3),
        grad_fc2.T,
        mid(1),
        mid(0),
    )


def solution(mesh):
    in_specs = (
        P(("inner", "outer"), None, None),
        P(("inner", "outer"), None),
        P(("inner", "outer"), None, None),
        P(),
        P(),
        P(),
        P(),
        P(None, None, "tensor"),
        P(None, "tensor"),
        P("tensor", None),
        P(),
        P(),
        P(),
        P(),
        P(None, "tensor"),
        P("tensor"),
        P("tensor", None),
        P(),
        P(),
    )
    out_specs = (
        P(("inner", "outer"), None, None),
        P(("inner", "outer"), None, None),
        P("inner"),
        P(None, "inner"),
        P("inner"),
        P("inner"),
        P("inner", None, "tensor"),
        P(None, ("tensor", "inner")),
        P("tensor", "inner"),
        P("inner"),
        P("inner"),
        P("inner"),
        P("inner"),
        P("inner", "tensor"),
        P(("tensor", "inner")),
        P("tensor", "inner"),
        P("inner"),
        P("inner"),
    )
    sizes = tuple(mesh.shape[name] for name in ("tensor", "inner", "outer"))
    return jax.shard_map(
        functools.partial(per_device, sizes),
        mesh=mesh,
        in_specs=in_specs,
        out_specs=out_specs,
        check_vma=False,
    )
```
